32 devices in a mesh: dp: 16 (over z, y, x), tensor: 2 (over core).
Axes of the slice: x: 2, y: 2, z: 4, core: 2. Of those that a mesh axis runs over, the one named last changes fastest.
Arguments:
- features: bfloat16 [16384, 4096], P(('dp', 'tensor')), may hold values from -20 to 20
- key_grads: bfloat16 [16384, 256], P('dp', 'tensor'), may hold values from -20 to 20
- error_in: bfloat16 [16, 4096, 256], P('dp', None, 'tensor'), may hold values from -24 to 24
- selected: int32 [16, 2, 32], P('dp', 'tensor'), may hold values from 0 to 4095, as said below
- bin_edges: int32 [17], replicated, may hold values from 0 to 4096, as said below
- threshold: int32 [1], replicated, may hold values from 1 to 15
- moment: float32 [4096, 256], P('dp', 'tensor'), may hold values from -2 to 2
- second: float32 [4096, 256], P('dp', 'tensor'), may hold values from 0.05 to 2
- master: float32 [4096, 256], P('dp', 'tensor'), may hold values from -0.0625 to 0.0625
Outputs:
- keys: bfloat16 [16384, 256], P('dp', 'tensor')
- error_out: bfloat16 [16, 4096, 256], P('dp', None, 'tensor')
- moment_new: float32 [4096, 256], P('dp', 'tensor')
- second_new: float32 [4096, 256], P('dp', 'tensor')
- master_new: float32 [4096, 256], P('dp', 'tensor')
The draws below stay inside these ranges and needn't reach their ends.
Inputs may be any that keep to these rules, and one draw needn't show every extreme that they name: Each device's 32 rows are distinct; the rows o * 256 to (o + 1) * 256 - 1 form owner o's region, and one device's row of selected names at most 6 rows of one region; there is one region, the same for every row of selected, that receives exactly 6 blocks from each row; every other region receives at most 6 from a row. bin_edges[0] = 0, bin_edges[16] = 4096, strictly increasing.
All inputs are finite; a program needn't handle non-finite values.
Results may differ from the reference program's by a relative error of at most 0.001.
The reference program's roundings to bfloat16 on the way (of `weight`) count: a program that leaves them out, or rounds other values in their place, can miss the bound.
Values may be sent and summed in bfloat16 or wider, within the bound.
No kernel may reach another device: no remote copies, remote signals or barrier semaphores. Data moves between devices by JAX's collectives and lax.ppermute only.
A program may use at most 64 MiB of HBM per device.

```python
import math
import jax
import jax.numpy as jnp
from jax import lax

ROWS = 4096
HD = 128
TOK_DEV = 1024
CAP = 6
BINS = 16
COLS = 256
TOKENS = 16384
KEEP = 32
REGION = 256
N_DP = 16
N_TENSOR = 2


def draw_features(key, part):
    freq = jax.random.randint(jax.random.fold_in(key, 21), (), 1, 4).astype(jnp.float32)
    phase = jax.random.uniform(jax.random.fold_in(key, 22), (), jnp.float32, 0.0, 6.283)
    place = jnp.arange(ROWS, dtype=jnp.float32) / ROWS
    depth = 0.45
    base = jnp.clip(jax.random.normal(jax.random.fold_in(key, 23), (TOKENS, ROWS), jnp.float32), -6.0, 6.0)
    profile = jnp.exp(2.302585 * depth * jnp.sin(6.283185 * freq * place + phase))
    return (base * profile[None, :]).astype(jnp.bfloat16)


def draw_key_grads(key, part):
    rise = 1.0 + 2.0 * jnp.arange(TOKENS, dtype=jnp.float32) / (TOKENS - 1)
    level = 4.0 / TOK_DEV ** 0.5
    values = jax.random.normal(jax.random.fold_in(key, 11), (TOKENS, COLS), jnp.float32)
    return jnp.clip(values * rise[:, None] * level, -19.5, 19.5).astype(jnp.bfloat16)


def pick_blocks(device_key, hot_owner):
    bias_key, noise_key, perm_key, order_key = jax.random.split(device_key, 4)
    bias = jax.random.randint(bias_key, (N_DP, 1), 0, 4).astype(jnp.int32) * 4096
    noise = jax.random.randint(noise_key, (N_DP, CAP), 0, 4096).astype(jnp.int32)
    owner_column = jnp.arange(N_DP, dtype=jnp.int32)[:, None]
    score = jnp.where(owner_column == hot_owner, -1, bias + noise)
    flat = score.reshape(-1) * (N_DP * CAP) + jnp.arange(N_DP * CAP, dtype=jnp.int32)
    top_values, picked = lax.top_k(flat, KEEP - CAP)
    picked = picked.astype(jnp.int32)
    owners = jnp.concatenate([picked // CAP, jnp.full((CAP,), hot_owner, jnp.int32)])
    slots = jnp.concatenate([picked % CAP, jnp.arange(CAP, dtype=jnp.int32)])
    perms = jax.vmap(lambda k: jax.random.permutation(k, REGION).astype(jnp.int32))(jax.random.split(perm_key, N_DP))
    blocks = owners * REGION + perms[owners, slots]
    return jax.random.permutation(order_key, blocks).astype(jnp.int32)


def draw_selected(key, part):
    hot_owner = jax.random.randint(jax.random.fold_in(key, 1), (), 0, N_DP).astype(jnp.int32)
    device_keys = jax.random.split(jax.random.fold_in(key, 2), N_DP * N_TENSOR)
    picks = jax.vmap(pick_blocks, in_axes=(0, None))(device_keys, hot_owner)
    return picks.reshape(N_DP, N_TENSOR, KEEP).astype(jnp.int32)


def draw_bin_edges(key, part):
    order = jax.random.permutation(jax.random.fold_in(key, 5), ROWS - 1).astype(jnp.int32)
    inner = jnp.sort(order[:BINS - 1] + 1)
    return jnp.concatenate([jnp.zeros((1,), jnp.int32), inner, jnp.full((1,), ROWS, jnp.int32)])


def block_levels(key, shape, cuts, least, high):
    level = 1.0
    for axis_at, shards_of in cuts:
        draws = jax.random.uniform(jax.random.fold_in(jax.random.fold_in(key, 6), axis_at), (shards_of,), jnp.float32, least / len(cuts), high / len(cuts))
        level = level * jnp.repeat(jnp.exp(draws), shape[axis_at] // shards_of).reshape((-1,) + (1,) * (len(shape) - 1 - axis_at))
    return level


def gaussian(stream_key, shape, spread, most, cuts=(), held_as=jnp.bfloat16):
    array = jax.random.normal(stream_key, shape, jnp.float32) * spread
    if len(cuts) > 0:
        array = block_levels(stream_key, shape, cuts, -0.22, 0.18) * array
    return jnp.clip(array, min=-most, max=most).astype(held_as)


def setup_inputs(seed: int = 0) -> dict:
    seeds = jax.random.split(jax.random.key(seed), 10)
    return {
        "features": draw_features(jax.random.fold_in(seeds[9], 71), 0),
        "key_grads": draw_key_grads(jax.random.fold_in(seeds[9], 71), 0),
        "error_in": gaussian(seeds[2], (N_DP, ROWS, COLS), 4.0, 24.0, ((0, 16), (2, 2))),
        "selected": draw_selected(jax.random.fold_in(seeds[9], 71), 0),
        "bin_edges": draw_bin_edges(jax.random.fold_in(seeds[9], 71), 0),
        "threshold": jax.random.randint(seeds[5], (1,), 1, BINS).astype(jnp.int32),
        "moment": gaussian(seeds[6], (ROWS, COLS), 0.3, 2.0, ((0, 16), (1, 2)), jnp.float32),
        "second": jnp.clip(jnp.exp(math.log(2.0) - 3.6888794 * jax.random.uniform(seeds[7], (ROWS, COLS), jnp.float32) ** block_levels(seeds[7], (ROWS, COLS), ((0, 16), (1, 2)), -0.2, 0.2)), 0.05, 2.0),
        "master": gaussian(seeds[8], (ROWS, COLS), (2 * ROWS) ** -0.5, 0.0625, ((0, 16), (1, 2)), jnp.float32),
    }


beta_first = 0.9
beta_second = 0.95
learn_rate = 0.001
decay_rate = 0.1
epsilon = 1e-06
adam_epsilon = 1e-08
step_count = 10.0

def reference(features, key_grads, error_in, selected, bin_edges, threshold, moment, second, master):
    highest = lax.Precision.HIGHEST
    feats = features.reshape(N_DP, TOK_DEV, ROWS)
    grads_in = key_grads.reshape(N_DP, TOK_DEV, COLS)

    def local_sum(triple):
        return jnp.dot(triple[0].T, triple[1], preferred_element_type=jnp.float32) + triple[2].astype(jnp.float32)
    summed = lax.map(local_sum, (feats, grads_in, error_in))
    blocks = summed.reshape(N_DP, ROWS, N_TENSOR, HD)
    squares = lax.optimization_barrier(jnp.sum(blocks * blocks, axis=3))
    row_ids = jnp.arange(ROWS, dtype=jnp.int32)
    member = ((row_ids[:, None] >= bin_edges[None, :BINS]) & (row_ids[:, None] < bin_edges[None, 1:])).astype(jnp.float32)
    energy = jnp.dot(member.T, lax.optimization_barrier(jnp.sum(squares, axis=0)), precision=highest)
    widths = (bin_edges[1:] - bin_edges[:BINS]).astype(jnp.float32)
    levels = jnp.arange(BINS, dtype=jnp.int32)
    normal = 1.0 / jnp.sqrt(energy / (N_DP * HD * widths[:, None]) + epsilon)
    scale = jnp.where((levels >= threshold[0])[:, None], normal, jnp.ones_like(normal))
    row_scale = jnp.dot(member, scale, precision=highest)
    device_index = jnp.arange(N_DP, dtype=jnp.int32)[:, None, None]
    head_index = jnp.arange(N_TENSOR, dtype=jnp.int32)[None, :, None]
    chosen = jnp.zeros((N_DP, N_TENSOR, ROWS), jnp.float32).at[device_index, head_index, selected].set(1.0)
    chosen = jnp.transpose(chosen, (0, 2, 1))
    kept = blocks * chosen[..., None]
    error_out = (blocks - kept).reshape(N_DP, ROWS, COLS).astype(jnp.bfloat16)
    grad = lax.optimization_barrier(jnp.sum(kept * row_scale[None, :, :, None], axis=0)).reshape(ROWS, COLS)
    moment_new = beta_first * moment + (1.0 - beta_first) * grad
    second_new = beta_second * second + (1.0 - beta_second) * grad * grad
    first_hat = moment_new / (1.0 - beta_first ** step_count)
    second_hat = second_new / (1.0 - beta_second ** step_count)
    master_new = master - learn_rate * (first_hat / (jnp.sqrt(second_hat) + adam_epsilon) + decay_rate * master)
    weight = master_new.astype(jnp.bfloat16)

    def project(rows_block):
        return jnp.dot(rows_block, weight, preferred_element_type=jnp.float32)
    keys = lax.map(project, feats).reshape(TOKENS, COLS).astype(jnp.bfloat16)
    return (keys, error_out, moment_new, second_new, master_new)
```

```python
import functools

import jax
import jax.numpy as jnp
from jax import lax
from jax.experimental import pallas as pl
from jax.experimental.pallas import tpu as pltpu
from jax.sharding import PartitionSpec as P

CAP = 6
SLOTS = 8
LANES = 128

beta_first = 0.9
beta_second = 0.95
learn_rate = 0.001
decay_rate = 0.1
epsilon = 1e-06
adam_epsilon = 1e-08
step_count = 10.0

VMEM = pl.BlockSpec(memory_space=pltpu.VMEM)
SMEM = pl.BlockSpec(memory_space=pltpu.SMEM)
PARAMS = pltpu.CompilerParams(vmem_limit_bytes=48 << 20)


def shift(x, axis, step):
    n = lax.axis_size(axis)
    return lax.ppermute(x, axis, [(i, (i + step) % n) for i in range(n)])


def swap(x, axis, mask):
    return lax.ppermute(x, axis, [(i, i ^ mask) for i in range(lax.axis_size(axis))])


def cost(flops, nbytes):
    return pl.CostEstimate(flops=flops, bytes_accessed=nbytes, transcendentals=0)


def partial_kernel(core, f_ref, g_ref, *rest):
    p = lax.dot_general(
        f_ref[...], g_ref[...], (((0,), (0,)), ((), ())), preferred_element_type=jnp.float32
    )
    if len(rest) == 2:
        p = p + rest[0][...].astype(jnp.float32)
    rest[-1][...] = p


def partial_sum(core, features, grads, first, count, error=None):
    tokens, rows = features.shape
    width = grads.shape[1]
    tile = min(1024, count)
    at = first // tile
    specs = [
        pl.BlockSpec((tokens, tile), lambda i, c: (0, i + at)),
        pl.BlockSpec((tokens, width), lambda i, c: (c[0], 0)),
    ]
    args = [features, grads]
    if error is not None:
        specs.append(pl.BlockSpec((tile, width), lambda i, c: (i + at, 0)))
        args.append(error)
    return pl.pallas_call(
        partial_kernel,
        grid_spec=pltpu.PrefetchScalarGridSpec(
            num_scalar_prefetch=1,
            grid=(count // tile,),
            in_specs=specs,
            out_specs=pl.BlockSpec((tile, width), lambda i, c: (i, 0)),
        ),
        out_shape=jax.ShapeDtypeStruct((count, width), jnp.float32),
        compiler_params=PARAMS,
        cost_estimate=cost(2 * tokens * count * width, 2 * tokens * count + 4 * count * width),
    )(core, *args)


def collect_kernel(n_parts, owners, bins, sel, lo_ref, hi_ref, *refs):
    parts, (sum_ref, out_ref, count_ref) = refs[:n_parts], refs[n_parts:]
    rows, width = sum_ref.shape
    region = rows // owners
    lo, hi = lo_ref[...], hi_ref[...]
    tile = 256

    def block(i, acc):
        first = pl.multiple_of(i * tile, tile)
        s = parts[0][pl.ds(first, tile), :]
        for ref in parts[1:]:
            s = s + ref[pl.ds(first, tile), :]
        sum_ref[pl.ds(first, tile), :] = s
        q = jnp.sum(s * s, axis=1, keepdims=True)
        ids = first + lax.broadcasted_iota(jnp.int32, (tile, LANES), 0)
        hit = (ids >= lo) & (ids < hi)
        return acc + jnp.sum(jnp.where(hit, q, 0.0).reshape(tile // 8, 8, LANES), axis=0)

    acc = lax.fori_loop(0, rows // tile, block, jnp.zeros((8, LANES), jnp.float32))
    energy = jnp.sum(acc, axis=0, keepdims=True)
    lane = lax.broadcasted_iota(jnp.int32, (1, LANES), 1)
    out_ref[...] = jnp.zeros_like(out_ref)
    note = jnp.where((lane >= bins) & (lane < bins + CAP), -1.0, energy)
    for o in range(owners):
        out_ref[o * SLOTS + CAP : o * SLOTS + CAP + 1, :] = note
        count_ref[o] = 0

    def take(i, carry):
        r = sel[i]
        o = lax.div(r, region)
        k = count_ref[o]
        count_ref[o] = k + 1
        out_ref[pl.ds(o * SLOTS + k, 1), :] = sum_ref[pl.ds(r, 1), :]
        sum_ref[pl.ds(r, 1), :] = jnp.zeros((1, width), jnp.float32)
        at = pl.ds(o * SLOTS + CAP, 1)
        out_ref[at, :] = jnp.where(
            lane == bins + k, (r - o * region).astype(jnp.float32), out_ref[at, :]
        )
        return carry

    lax.fori_loop(0, sel.shape[0], take, 0)


def collect(selected, lo, hi, parts, owners, bins):
    rows, width = parts[0].shape
    return pl.pallas_call(
        functools.partial(collect_kernel, len(parts), owners, bins),
        in_specs=[SMEM, VMEM, VMEM] + [VMEM] * len(parts),
        out_specs=[VMEM, VMEM],
        out_shape=[
            jax.ShapeDtypeStruct((rows, width), jnp.float32),
            jax.ShapeDtypeStruct((owners * SLOTS, width), jnp.float32),
        ],
        scratch_shapes=[pltpu.SMEM((owners,), jnp.int32)],
        compiler_params=PARAMS,
        cost_estimate=cost(8 * rows * width, 4 * rows * width * 3),
    )(selected, lo, hi, *parts)


def adam_kernel(bins, info, lo_ref, hi_ref, arr_ref, m_ref, v_ref, w_ref, mo, vo, wo, bo):
    owners, slots, width = arr_ref.shape
    region = m_ref.shape[0]
    lo, hi = lo_ref[...], hi_ref[...]
    lane = lax.broadcasted_iota(jnp.int32, (1, LANES), 1)
    arr = arr_ref[...]
    notes = arr[:, CAP : CAP + 1, :]
    energy = jnp.sum(notes, axis=0)
    widths = jnp.maximum(hi - lo, 1).astype(jnp.float32)
    normal = 1.0 / jnp.sqrt(energy / (owners * width * widths) + epsilon)
    scale = jnp.where((lane >= info[1]) & (lane < bins), normal, 1.0)
    ids = info[0] * region + lax.broadcasted_iota(jnp.int32, (region, LANES), 0)
    row_scale = jnp.sum(
        jnp.where((ids >= lo) & (ids < hi), scale, 0.0), axis=1, keepdims=True
    )
    slot = lax.broadcasted_iota(jnp.int32, (owners, slots, LANES), 1)
    lane3 = lax.broadcasted_iota(jnp.int32, (owners, slots, LANES), 2)
    offset = jnp.sum(
        jnp.where((lane3 == bins + slot) & (slot < CAP), notes, 0.0), axis=2, keepdims=True
    )
    slot1 = lax.broadcasted_iota(jnp.int32, (owners, slots, 1), 1)
    offset = jnp.where(slot1 < CAP, offset, -1.0).reshape(owners * slots, 1)
    row = lax.broadcasted_iota(jnp.int32, (owners * slots, region), 1).astype(jnp.float32)
    place = jnp.where(row == offset, 1.0, 0.0)
    grad = lax.dot_general(
        place,
        arr.reshape(owners * slots, width),
        (((0,), (0,)), ((), ())),
        precision=lax.Precision.HIGHEST,
        preferred_element_type=jnp.float32,
    )
    grad = grad * row_scale
    master = w_ref[...]
    moment_new = beta_first * m_ref[...] + (1.0 - beta_first) * grad
    second_new = beta_second * v_ref[...] + (1.0 - beta_second) * grad * grad
    first_hat = moment_new / (1.0 - beta_first**step_count)
    second_hat = second_new / (1.0 - beta_second**step_count)
    master_new = master - learn_rate * (
        first_hat / (jnp.sqrt(second_hat) + adam_epsilon) + decay_rate * master
    )
    mo[...] = moment_new
    vo[...] = second_new
    wo[...] = master_new
    bo[...] = master_new.astype(jnp.bfloat16)


def adam(info, lo, hi, arrived, moment, second, master, bins):
    f32 = jax.ShapeDtypeStruct(master.shape, jnp.float32)
    return pl.pallas_call(
        functools.partial(adam_kernel, bins),
        in_specs=[SMEM] + [VMEM] * 6,
        out_specs=[VMEM] * 4,
        out_shape=[f32, f32, f32, jax.ShapeDtypeStruct(master.shape, jnp.bfloat16)],
        compiler_params=PARAMS,
        cost_estimate=cost(2 * 6 * arrived.size * master.shape[0], 30 * master.size),
    )(info, lo, hi, arrived, moment, second, master)


def project_kernel(first, last, n_f, at, *refs):
    feats, (w_ref, *old, out_ref, total) = refs[:n_f], refs[n_f:]
    step = pl.program_id(0)
    tokens = feats[0].shape[0]

    @pl.when(step == 0)
    def _():
        total[...] = jnp.zeros_like(total) if first else old[0][...]

    for i, f_ref in enumerate(feats):
        total[i * tokens : (i + 1) * tokens, :] += jnp.dot(
            f_ref[...], w_ref[0], preferred_element_type=jnp.float32
        )

    @pl.when(step == pl.num_programs(0) - 1)
    def _():
        if not last:
            out_ref[...] = total[...]
        else:
            for i in range(n_f):
                place = lax.rem(at[at.shape[0] - 1] + i, n_f) * tokens
                out_ref[pl.ds(pl.multiple_of(place, tokens), tokens), :] = total[
                    i * tokens : (i + 1) * tokens, :
                ].astype(out_ref.dtype)


def project(at, feats, pieces, total, last):
    count, region, width = pieces.shape
    tokens = feats[0].shape[0]
    whole = len(feats) * tokens
    first = total is None
    full = pl.BlockSpec((whole, width), lambda i, a: (0, 0))
    return pl.pallas_call(
        functools.partial(project_kernel, first, last, len(feats)),
        grid_spec=pltpu.PrefetchScalarGridSpec(
            num_scalar_prefetch=1,
            grid=(count,),
            in_specs=[pl.BlockSpec((tokens, region), lambda i, a: (0, a[i]))] * len(feats)
            + [pl.BlockSpec((1, region, width), lambda i, a: (i, 0, 0))]
            + ([] if first else [full]),
            out_specs=full,
            scratch_shapes=[pltpu.VMEM((whole, width), jnp.float32)],
        ),
        out_shape=jax.ShapeDtypeStruct((whole, width), jnp.bfloat16 if last else jnp.float32),
        compiler_params=PARAMS,
        cost_estimate=cost(
            2 * whole * count * region * width, 2 * whole * count * region + 8 * whole * width
        ),
    )(at, *feats, pieces, *([] if first else [total]))


def spans(mask_bits):
    masks = [0]
    for b in mask_bits:
        masks = masks + [m | b for m in masks]
    return masks


def shards(features, key_grads, error_in, selected, bin_edges, threshold, moment, second, master):
    cores, owners = lax.axis_size("tensor"), lax.axis_size("dp")
    core, me = lax.axis_index("tensor"), lax.axis_index("dp")
    tokens, rows = features.shape
    width = key_grads.shape[1]
    region = rows // owners
    bins = bin_edges.shape[0] - 1
    pad = (0, LANES - bins)
    lo = jnp.pad(bin_edges[:-1], pad)[None]
    hi = jnp.pad(bin_edges[1:], pad)[None]
    core1 = core.reshape(1).astype(jnp.int32)

    pieces = 2 if cores == 2 else 1
    count = rows // pieces
    got = []
    for s in range(1, cores):
        theirs = shift(key_grads, "tensor", s)
        got.append(
            jnp.concatenate(
                [
                    shift(partial_sum(core1, features, theirs, j * count, count), "tensor", -s)
                    for j in range(pieces)
                ],
                axis=0,
            )
        )
    own = partial_sum(core1, features, key_grads, 0, rows, error_in[0])
    rest, outgoing = collect(selected[0, 0], lo, hi, [own] + got, owners, bins)
    error_out = rest.astype(jnp.bfloat16)[None]
    feats = [features] + [shift(features, "tensor", -s) for s in range(1, cores)]

    arrived = lax.all_to_all(
        outgoing.reshape(owners, SLOTS, width), "dp", split_axis=0, concat_axis=0, tiled=True
    )
    info = jnp.stack([me.astype(jnp.int32), threshold[0]])
    moment_new, second_new, master_new, weight = adam(
        info, lo, hi, arrived, moment, second, master, bins
    )

    bits = [1 << i for i in range(owners.bit_length() - 1)]
    if 1 << len(bits) == owners and len(bits) > 2 and region % LANES == 0:
        plane, line = spans(bits[:2]), spans(bits[2:])
        mine = jnp.stack([weight if m == 0 else swap(weight, "dp", m) for m in line])
        total = None
        for j, b in enumerate(plane):
            here = mine if b == 0 else swap(mine, "dp", b)
            at = jnp.stack([me ^ (b ^ m) for m in line] + [core]).astype(jnp.int32)
            total = project(at, feats, here, total, j == len(plane) - 1)
        keys = total
    else:
        whole = jnp.concatenate(feats, axis=0)
        whole = jnp.roll(whole, core * tokens, axis=0)
        keys = jnp.dot(
            whole,
            lax.all_gather(weight, "dp", axis=0, tiled=True),
            preferred_element_type=jnp.float32,
        ).astype(jnp.bfloat16)
    return (keys, error_out, moment_new, second_new, master_new)


def solution(mesh):
    in_specs = (
        P(("dp", "tensor"), None),
        P("dp", "tensor"),
        P("dp", None, "tensor"),
        P("dp", "tensor", None),
        P(),
        P(),
        P("dp", "tensor"),
        P("dp", "tensor"),
        P("dp", "tensor"),
    )
    out_specs = (
        P("dp", "tensor"),
        P("dp", None, "tensor"),
        P("dp", "tensor"),
        P("dp", "tensor"),
        P("dp", "tensor"),
    )
    return jax.shard_map(shards, mesh=mesh, in_specs=in_specs, out_specs=out_specs, check_vma=False)
```

```python
import functools

import jax
import jax.numpy as jnp
from jax import lax
from jax.experimental import pallas as pl
from jax.experimental.pallas import tpu as pltpu
from jax.sharding import PartitionSpec as P

CAP = 6
SLOTS = 8
LANES = 128

beta_first = 0.9
beta_second = 0.95
learn_rate = 0.001
decay_rate = 0.1
epsilon = 1e-06
adam_epsilon = 1e-08
step_count = 10.0

VMEM = pl.BlockSpec(memory_space=pltpu.VMEM)
SMEM = pl.BlockSpec(memory_space=pltpu.SMEM)
ANY = pl.BlockSpec(memory_space=pl.ANY)


def shift(x, axis, step):
    n = lax.axis_size(axis)
    return lax.ppermute(x, axis, [(i, (i + step) % n) for i in range(n)])


def swap(x, axis, mask):
    return lax.ppermute(x, axis, [(i, i ^ mask) for i in range(lax.axis_size(axis))])


def params(*arrays):
    total = sum(a.size * jnp.dtype(a.dtype).itemsize for a in arrays)
    return pltpu.CompilerParams(vmem_limit_bytes=total + (6 << 20))


def cost(flops, nbytes):
    return pl.CostEstimate(flops=flops, bytes_accessed=nbytes, transcendentals=0)


def own_kernel(tile, core, f_any, e_any, g_ref, f_ref, o_ref, e_buf, f_sem, e_sem):
    tokens, rows = f_ref.shape
    count = rows // tile
    g = g_ref[pl.ds(pl.multiple_of(core[0] * tokens, tokens), tokens), :]
    copies = []
    for j in range(count):
        cols = pl.ds(j * tile, tile)
        copies.append(pltpu.make_async_copy(f_any.at[:, cols], f_ref.at[:, cols], f_sem.at[j]))
        copies[-1].start()
    error_copy = pltpu.make_async_copy(e_any, e_buf, e_sem)
    error_copy.start()
    for j in range(count):
        copies[j].wait()
        o_ref[j * tile : (j + 1) * tile, :] = lax.dot_general(
            f_ref[:, j * tile : (j + 1) * tile],
            g,
            (((0,), (0,)), ((), ())),
            preferred_element_type=jnp.float32,
        )
    error_copy.wait()
    for j in range(count):
        at = slice(j * tile, (j + 1) * tile)
        o_ref[at, :] += e_buf[at, :].astype(jnp.float32)


def own_sum(core, features, error, grads):
    tokens, rows = features.shape
    width = grads.shape[1]
    tile = min(512, rows)
    own = jax.ShapeDtypeStruct((rows, width), jnp.float32)
    return pl.pallas_call(
        functools.partial(own_kernel, tile),
        in_specs=[SMEM, ANY, ANY, VMEM],
        out_specs=[VMEM, VMEM],
        out_shape=[
            pltpu.VMEM(features.shape, features.dtype),
            own,
        ],
        scratch_shapes=[
            pltpu.VMEM(error.shape, error.dtype),
            pltpu.SemaphoreType.DMA((rows // tile,)),
            pltpu.SemaphoreType.DMA,
        ],
        compiler_params=params(features, error, own, grads),
        cost_estimate=cost(2 * tokens * rows * width, 2 * tokens * rows + 6 * rows * width),
    )(
        core,
        pltpu.with_memory_space_constraint(features, pltpu.HBM),
        pltpu.with_memory_space_constraint(error, pltpu.HBM),
        grads,
    )


def their_kernel(first, core, f_ref, g_ref, o_ref):
    tokens = f_ref.shape[0]
    count = o_ref.shape[0]
    o_ref[...] = lax.dot_general(
        f_ref[:, first : first + count],
        g_ref[pl.ds(pl.multiple_of(core[0] * tokens, tokens), tokens), :],
        (((0,), (0,)), ((), ())),
        preferred_element_type=jnp.float32,
    )


def their_sum(core, features, grads, first, count):
    tokens = features.shape[0]
    width = grads.shape[1]
    part = jax.ShapeDtypeStruct((count, width), jnp.float32)
    return pl.pallas_call(
        functools.partial(their_kernel, first),
        in_specs=[SMEM, VMEM, VMEM],
        out_specs=VMEM,
        out_shape=part,
        compiler_params=params(features, grads, part),
        cost_estimate=cost(2 * tokens * count * width, 2 * tokens * count + 4 * count * width),
    )(core, features, grads)


def collect_kernel(n_chunks, owners, bins, sel, lo_ref, hi_ref, own_ref, *refs):
    parts, (sum_ref, out_ref, count_ref) = refs[:-3], refs[-3:]
    rows, width = sum_ref.shape
    region = rows // owners
    lo, hi = lo_ref[...], hi_ref[...]
    count = rows // n_chunks
    tile = min(1024, count)
    acc = jnp.zeros((8, LANES), jnp.float32)
    for first in range(0, rows, tile):
        s = own_ref[first : first + tile, :]
        for ref in parts[first // count :: n_chunks]:
            s = s + ref[first % count : first % count + tile, :]
        sum_ref[first : first + tile, :] = s
        q = jnp.sum(s * s, axis=1, keepdims=True)
        ids = first + lax.broadcasted_iota(jnp.int32, (tile, LANES), 0)
        hit = (ids >= lo) & (ids < hi)
        acc = acc + jnp.sum(jnp.where(hit, q, 0.0).reshape(tile // 8, 8, LANES), axis=0)
    energy = jnp.sum(acc, axis=0, keepdims=True)
    lane = lax.broadcasted_iota(jnp.int32, (1, LANES), 1)
    out_ref[...] = jnp.zeros_like(out_ref)
    note = jnp.where((lane >= bins) & (lane < bins + CAP), -1.0, energy)
    for o in range(owners):
        out_ref[o * SLOTS + CAP : o * SLOTS + CAP + 1, :] = note
        count_ref[o] = 0

    def take(i, carry):
        r = sel[i]
        o = lax.div(r, region)
        k = count_ref[o]
        count_ref[o] = k + 1
        out_ref[pl.ds(o * SLOTS + k, 1), :] = sum_ref[pl.ds(r, 1), :]
        sum_ref[pl.ds(r, 1), :] = jnp.zeros((1, width), jnp.float32)
        at = pl.ds(o * SLOTS + CAP, 1)
        out_ref[at, :] = jnp.where(
            lane == bins + k, (r - o * region).astype(jnp.float32), out_ref[at, :]
        )
        return carry

    lax.fori_loop(0, sel.shape[0], take, 0, unroll=8)


def collect(selected, lo, hi, own, parts, n_chunks, owners, bins):
    rows, width = own.shape
    return pl.pallas_call(
        functools.partial(collect_kernel, n_chunks, owners, bins),
        in_specs=[SMEM, VMEM, VMEM, VMEM] + [VMEM] * len(parts),
        out_specs=[VMEM, VMEM],
        out_shape=[
            jax.ShapeDtypeStruct((rows, width), jnp.float32),
            jax.ShapeDtypeStruct((owners * SLOTS, width), jnp.float32),
        ],
        scratch_shapes=[pltpu.SMEM((owners,), jnp.int32)],
        compiler_params=params(own, own, own, *parts),
        cost_estimate=cost(8 * rows * width, 4 * rows * width * 3),
    )(selected, lo, hi, own, *parts)


def adam_kernel(bins, info, lo_ref, hi_ref, arr_ref, m_ref, v_ref, w_ref, mo, vo, wo, bo):
    owners, slots, width = arr_ref.shape
    region = m_ref.shape[0]
    lo, hi = lo_ref[...], hi_ref[...]
    lane = lax.broadcasted_iota(jnp.int32, (1, LANES), 1)
    arr = arr_ref[...]
    notes = arr[:, CAP : CAP + 1, :]
    energy = jnp.sum(notes, axis=0)
    widths = jnp.maximum(hi - lo, 1).astype(jnp.float32)
    normal = 1.0 / jnp.sqrt(energy / (owners * width * widths) + epsilon)
    scale = jnp.where((lane >= info[1]) & (lane < bins), normal, 1.0)
    ids = info[0] * region + lax.broadcasted_iota(jnp.int32, (region, LANES), 0)
    row_scale = jnp.sum(
        jnp.where((ids >= lo) & (ids < hi), scale, 0.0), axis=1, keepdims=True
    )
    slot = lax.broadcasted_iota(jnp.int32, (owners, slots, LANES), 1)
    lane3 = lax.broadcasted_iota(jnp.int32, (owners, slots, LANES), 2)
    offset = jnp.sum(
        jnp.where((lane3 == bins + slot) & (slot < CAP), notes, 0.0), axis=2, keepdims=True
    )
    slot1 = lax.broadcasted_iota(jnp.int32, (owners, slots, 1), 1)
    offset = jnp.where(slot1 < CAP, offset, -1.0).reshape(owners * slots, 1)
    row = lax.broadcasted_iota(jnp.int32, (owners * slots, region), 1).astype(jnp.float32)
    place = jnp.where(row == offset, 1.0, 0.0)
    grad = lax.dot_general(
        place,
        arr.reshape(owners * slots, width),
        (((0,), (0,)), ((), ())),
        precision=lax.Precision.HIGHEST,
        preferred_element_type=jnp.float32,
    )
    grad = grad * row_scale
    master = w_ref[...]
    moment_new = beta_first * m_ref[...] + (1.0 - beta_first) * grad
    second_new = beta_second * v_ref[...] + (1.0 - beta_second) * grad * grad
    first_hat = moment_new / (1.0 - beta_first**step_count)
    second_hat = second_new / (1.0 - beta_second**step_count)
    master_new = master - learn_rate * (
        first_hat / (jnp.sqrt(second_hat) + adam_epsilon) + decay_rate * master
    )
    mo[...] = moment_new
    vo[...] = second_new
    wo[...] = master_new
    bo[...] = master_new.astype(jnp.bfloat16)


def adam(info, lo, hi, arrived, moment, second, master, bins):
    f32 = jax.ShapeDtypeStruct(master.shape, jnp.float32)
    return pl.pallas_call(
        functools.partial(adam_kernel, bins),
        in_specs=[SMEM] + [VMEM] * 6,
        out_specs=[VMEM] * 4,
        out_shape=[f32, f32, f32, jax.ShapeDtypeStruct(master.shape, jnp.bfloat16)],
        compiler_params=params(arrived, arrived, *[f32] * 7),
        cost_estimate=cost(2 * 6 * arrived.size * master.shape[0], 30 * master.size),
    )(info, lo, hi, arrived, moment, second, master)


def project_kernel(last, n_f, at, w_ref, *refs):
    feats, old, out_ref = refs[:n_f], refs[n_f:-1], refs[-1]
    count, region, width = w_ref.shape
    tokens = feats[0].shape[0]
    for i, f_ref in enumerate(feats):
        mine = pl.ds(i * tokens, tokens)
        total = old[0][mine, :] if old else None
        for j in range(count):
            cols = pl.ds(pl.multiple_of(at[j] * region, region), region)
            part = jnp.dot(f_ref[:, cols], w_ref[j], preferred_element_type=jnp.float32)
            total = part if total is None else total + part
        if last:
            place = lax.rem(at[count] + i, n_f) * tokens
            mine = pl.ds(pl.multiple_of(place, tokens), tokens)
        out_ref[mine, :] = total.astype(out_ref.dtype)


def project(at, feats, pieces, total, last):
    count, region, width = pieces.shape
    whole = len(feats) * feats[0].shape[0]
    old = [] if total is None else [total]
    out = jax.ShapeDtypeStruct((whole, width), jnp.bfloat16 if last else jnp.float32)
    return pl.pallas_call(
        functools.partial(project_kernel, last, len(feats)),
        in_specs=[SMEM, VMEM] + [VMEM] * (len(feats) + len(old)),
        out_specs=VMEM,
        out_shape=out,
        compiler_params=params(pieces, out, *feats, *old),
        cost_estimate=cost(
            2 * whole * count * region * width, 2 * whole * count * region + 8 * whole * width
        ),
    )(at, pieces, *feats, *old)


def spans(mask_bits):
    masks = [0]
    for b in mask_bits:
        masks = masks + [m | b for m in masks]
    return masks


def shards(features, key_grads, error_in, selected, bin_edges, threshold, moment, second, master):
    cores, owners = lax.axis_size("tensor"), lax.axis_size("dp")
    core, me = lax.axis_index("tensor"), lax.axis_index("dp")
    tokens, rows = features.shape
    width = key_grads.shape[1]
    region = rows // owners
    bins = bin_edges.shape[0] - 1
    pad = (0, LANES - bins)
    lo = jnp.pad(bin_edges[:-1], pad)[None]
    hi = jnp.pad(bin_edges[1:], pad)[None]
    core1 = core.reshape(1).astype(jnp.int32)

    held, own = own_sum(core1, features, error_in[0], key_grads)
    n_chunks = 4 if cores == 2 else 1
    count = rows // n_chunks
    got, made = [], []
    for s in range(1, cores):
        theirs = shift(key_grads, "tensor", s)
        for j in range(n_chunks):
            part = their_sum(core1, held, theirs, j * count, count)
            made.append(part)
            got.append(shift(part, "tensor", -s))
    rest, outgoing = collect(selected[0, 0], lo, hi, own, got, n_chunks, owners, bins)
    error_out = rest.astype(jnp.bfloat16)[None]
    later, _ = lax.optimization_barrier((features, made))
    feats = [held] + [shift(later, "tensor", -s) for s in range(1, cores)]

    arrived = lax.all_to_all(
        outgoing.reshape(owners, SLOTS, width), "dp", split_axis=0, concat_axis=0, tiled=True
    )
    info = jnp.stack([me.astype(jnp.int32), threshold[0]])
    moment_new, second_new, master_new, weight = adam(
        info, lo, hi, arrived, moment, second, master, bins
    )

    bits = [1 << i for i in range(owners.bit_length() - 1)]
    if 1 << len(bits) == owners and len(bits) > 2 and region % LANES == 0:
        plane, line = spans(bits[:2]), spans(bits[2:])
        mine = jnp.stack([weight if m == 0 else swap(weight, "dp", m) for m in line])
        total = None
        for j, b in enumerate(plane):
            here = mine if b == 0 else swap(mine, "dp", b)
            at = jnp.stack([me ^ (b ^ m) for m in line] + [core]).astype(jnp.int32)
            total = project(at, feats, here, total, j == len(plane) - 1)
        keys = total
    else:
        whole = jnp.concatenate(feats, axis=0)
        whole = jnp.roll(whole, core * tokens, axis=0)
        keys = jnp.dot(
            whole,
            lax.all_gather(weight, "dp", axis=0, tiled=True),
            preferred_element_type=jnp.float32,
        ).astype(jnp.bfloat16)
    return (keys, error_out, moment_new, second_new, master_new)


def solution(mesh):
    in_specs = (
        P(("dp", "tensor"), None),
        P("dp", "tensor"),
        P("dp", None, "tensor"),
        P("dp", "tensor", None),
        P(),
        P(),
        P("dp", "tensor"),
        P("dp", "tensor"),
        P("dp", "tensor"),
    )
    out_specs = (
        P("dp", "tensor"),
        P("dp", None, "tensor"),
        P("dp", "tensor"),
        P("dp", "tensor"),
        P("dp", "tensor"),
    )
    return jax.shard_map(shards, mesh=mesh, in_specs=in_specs, out_specs=out_specs, check_vma=False)
```

```python
import functools

import jax
import jax.numpy as jnp
from jax import lax
from jax.experimental import pallas as pl
from jax.experimental.pallas import tpu as pltpu
from jax.sharding import PartitionSpec as P

CAP = 6
SLOTS = 8
LANES = 128

beta_first = 0.9
beta_second = 0.95
learn_rate = 0.001
decay_rate = 0.1
epsilon = 1e-06
adam_epsilon = 1e-08
step_count = 10.0

VMEM = pl.BlockSpec(memory_space=pltpu.VMEM)
SMEM = pl.BlockSpec(memory_space=pltpu.SMEM)
ANY = pl.BlockSpec(memory_space=pl.ANY)


def shift(x, axis, step):
    n = lax.axis_size(axis)
    return lax.ppermute(x, axis, [(i, (i + step) % n) for i in range(n)])


def swap(x, axis, mask):
    return lax.ppermute(x, axis, [(i, i ^ mask) for i in range(lax.axis_size(axis))])


def params(*arrays):
    total = sum(a.size * jnp.dtype(a.dtype).itemsize for a in arrays)
    return pltpu.CompilerParams(vmem_limit_bytes=total + (6 << 20))


def cost(flops, nbytes):
    return pl.CostEstimate(flops=flops, bytes_accessed=nbytes, transcendentals=0)


def load_kernel(pieces, *refs):
    n = len(refs) // 2
    sources, targets, sem = refs[:n], refs[n : 2 * n], refs[2 * n]
    copies = []
    for i in range(n):
        rows = sources[i].shape[0] // pieces
        for j in range(pieces):
            part = pl.ds(j * rows, rows)
            copies.append(
                pltpu.make_async_copy(sources[i].at[part], targets[i].at[part], sem.at[i, j])
            )
            copies[-1].start()
    for copy in copies:
        copy.wait()


def load(arrays):
    pieces = 8
    return pl.pallas_call(
        functools.partial(load_kernel, pieces),
        in_specs=[ANY] * len(arrays),
        out_specs=[VMEM] * len(arrays),
        out_shape=[pltpu.VMEM(a.shape, a.dtype) for a in arrays],
        scratch_shapes=[pltpu.SemaphoreType.DMA((len(arrays), pieces))],
        compiler_params=params(*arrays),
        cost_estimate=cost(0, 4 * sum(a.size for a in arrays)),
    )(*[pltpu.with_memory_space_constraint(a, pltpu.HBM) for a in arrays])


def part_kernel(first, core, f_ref, g_ref, *rest):
    tokens = f_ref.shape[0]
    count = rest[-1].shape[0]
    tile = min(1024, count)
    g = g_ref[pl.ds(pl.multiple_of(core[0] * tokens, tokens), tokens), :]
    for at in range(0, count, tile):
        p = lax.dot_general(
            f_ref[:, first + at : first + at + tile],
            g,
            (((0,), (0,)), ((), ())),
            preferred_element_type=jnp.float32,
        )
        if len(rest) > 1:
            p = p + rest[0][at : at + tile, :].astype(jnp.float32)
        rest[-1][at : at + tile, :] = p


def part_sum(core, features, grads, first, count, *error):
    tokens = features.shape[0]
    width = grads.shape[1]
    part = jax.ShapeDtypeStruct((count, width), jnp.float32)
    return pl.pallas_call(
        functools.partial(part_kernel, first),
        in_specs=[SMEM, VMEM, VMEM] + [VMEM] * len(error),
        out_specs=VMEM,
        out_shape=part,
        compiler_params=params(features, grads, part, *error),
        cost_estimate=cost(2 * tokens * count * width, 2 * tokens * count + 4 * count * width),
    )(core, features, grads, *error)


def collect_kernel(n_chunks, owners, bins, sel, lo_ref, hi_ref, own_ref, *refs):
    parts, (sum_ref, out_ref, count_ref) = refs[:-3], refs[-3:]
    rows, width = sum_ref.shape
    region = rows // owners
    lo, hi = lo_ref[...], hi_ref[...]
    count = rows // n_chunks
    tile = min(1024, count)
    acc = jnp.zeros((8, LANES), jnp.float32)
    for first in range(0, rows, tile):
        s = own_ref[first : first + tile, :]
        for ref in parts[first // count :: n_chunks]:
            s = s + ref[first % count : first % count + tile, :]
        sum_ref[first : first + tile, :] = s
        q = jnp.sum(s * s, axis=1, keepdims=True)
        ids = first + lax.broadcasted_iota(jnp.int32, (tile, LANES), 0)
        hit = (ids >= lo) & (ids < hi)
        acc = acc + jnp.sum(jnp.where(hit, q, 0.0).reshape(tile // 8, 8, LANES), axis=0)
    energy = jnp.sum(acc, axis=0, keepdims=True)
    lane = lax.broadcasted_iota(jnp.int32, (1, LANES), 1)
    out_ref[...] = jnp.zeros_like(out_ref)
    note = jnp.where((lane >= bins) & (lane < bins + CAP), -1.0, energy)
    for o in range(owners):
        out_ref[o * SLOTS + CAP : o * SLOTS + CAP + 1, :] = note
        count_ref[o] = 0

    def take(i, carry):
        r = sel[i]
        o = lax.div(r, region)
        k = count_ref[o]
        count_ref[o] = k + 1
        out_ref[pl.ds(o * SLOTS + k, 1), :] = sum_ref[pl.ds(r, 1), :]
        sum_ref[pl.ds(r, 1), :] = jnp.zeros((1, width), jnp.float32)
        at = pl.ds(o * SLOTS + CAP, 1)
        out_ref[at, :] = jnp.where(
            lane == bins + k, (r - o * region).astype(jnp.float32), out_ref[at, :]
        )
        return carry

    lax.fori_loop(0, sel.shape[0], take, 0, unroll=8)


def collect(selected, lo, hi, own, parts, n_chunks, owners, bins):
    rows, width = own.shape
    return pl.pallas_call(
        functools.partial(collect_kernel, n_chunks, owners, bins),
        in_specs=[SMEM, VMEM, VMEM, VMEM] + [VMEM] * len(parts),
        out_specs=[VMEM, VMEM],
        out_shape=[
            jax.ShapeDtypeStruct((rows, width), jnp.float32),
            jax.ShapeDtypeStruct((owners * SLOTS, width), jnp.float32),
        ],
        scratch_shapes=[pltpu.SMEM((owners,), jnp.int32)],
        compiler_params=params(own, own, own, *parts),
        cost_estimate=cost(8 * rows * width, 4 * rows * width * 3),
    )(selected, lo, hi, own, *parts)


def adam_kernel(bins, info, lo_ref, hi_ref, arr_ref, m_ref, v_ref, w_ref, mo, vo, wo, bo):
    owners, slots, width = arr_ref.shape
    region = m_ref.shape[0]
    lo, hi = lo_ref[...], hi_ref[...]
    lane = lax.broadcasted_iota(jnp.int32, (1, LANES), 1)
    arr = arr_ref[...]
    notes = arr[:, CAP : CAP + 1, :]
    energy = jnp.sum(notes, axis=0)
    widths = jnp.maximum(hi - lo, 1).astype(jnp.float32)
    normal = 1.0 / jnp.sqrt(energy / (owners * width * widths) + epsilon)
    scale = jnp.where((lane >= info[1]) & (lane < bins), normal, 1.0)
    ids = info[0] * region + lax.broadcasted_iota(jnp.int32, (region, LANES), 0)
    row_scale = jnp.sum(
        jnp.where((ids >= lo) & (ids < hi), scale, 0.0), axis=1, keepdims=True
    )
    slot = lax.broadcasted_iota(jnp.int32, (owners, slots, LANES), 1)
    lane3 = lax.broadcasted_iota(jnp.int32, (owners, slots, LANES), 2)
    offset = jnp.sum(
        jnp.where((lane3 == bins + slot) & (slot < CAP), notes, 0.0), axis=2, keepdims=True
    )
    slot1 = lax.broadcasted_iota(jnp.int32, (owners, slots, 1), 1)
    offset = jnp.where(slot1 < CAP, offset, -1.0).reshape(owners * slots, 1)
    row = lax.broadcasted_iota(jnp.int32, (owners * slots, region), 1).astype(jnp.float32)
    place = jnp.where(row == offset, 1.0, 0.0)
    grad = lax.dot_general(
        place,
        arr.reshape(owners * slots, width),
        (((0,), (0,)), ((), ())),
        precision=lax.Precision.HIGHEST,
        preferred_element_type=jnp.float32,
    )
    grad = grad * row_scale
    master = w_ref[...]
    moment_new = beta_first * m_ref[...] + (1.0 - beta_first) * grad
    second_new = beta_second * v_ref[...] + (1.0 - beta_second) * grad * grad
    first_hat = moment_new / (1.0 - beta_first**step_count)
    second_hat = second_new / (1.0 - beta_second**step_count)
    master_new = master - learn_rate * (
        first_hat / (jnp.sqrt(second_hat) + adam_epsilon) + decay_rate * master
    )
    mo[...] = moment_new
    vo[...] = second_new
    wo[...] = master_new
    bo[...] = master_new.astype(jnp.bfloat16)


def adam(info, lo, hi, arrived, moment, second, master, bins):
    f32 = jax.ShapeDtypeStruct(master.shape, jnp.float32)
    return pl.pallas_call(
        functools.partial(adam_kernel, bins),
        in_specs=[SMEM] + [VMEM] * 6,
        out_specs=[VMEM] * 4,
        out_shape=[f32, f32, f32, jax.ShapeDtypeStruct(master.shape, jnp.bfloat16)],
        compiler_params=params(arrived, arrived, *[f32] * 7),
        cost_estimate=cost(2 * 6 * arrived.size * master.shape[0], 30 * master.size),
    )(info, lo, hi, arrived, moment, second, master)


def project_kernel(last, n_f, at, w_ref, *refs):
    feats, old, out_ref = refs[:n_f], refs[n_f:-1], refs[-1]
    count, region, width = w_ref.shape
    tokens = feats[0].shape[0]
    for i, f_ref in enumerate(feats):
        mine = pl.ds(i * tokens, tokens)
        total = old[0][mine, :] if old else None
        for j in range(count):
            cols = pl.ds(pl.multiple_of(at[j] * region, region), region)
            part = jnp.dot(f_ref[:, cols], w_ref[j], preferred_element_type=jnp.float32)
            total = part if total is None else total + part
        if last:
            place = lax.rem(at[count] + i, n_f) * tokens
            mine = pl.ds(pl.multiple_of(place, tokens), tokens)
        out_ref[mine, :] = total.astype(out_ref.dtype)


def project(at, feats, pieces, total, last):
    count, region, width = pieces.shape
    whole = len(feats) * feats[0].shape[0]
    old = [] if total is None else [total]
    out = jax.ShapeDtypeStruct((whole, width), jnp.bfloat16 if last else jnp.float32)
    return pl.pallas_call(
        functools.partial(project_kernel, last, len(feats)),
        in_specs=[SMEM, VMEM] + [VMEM] * (len(feats) + len(old)),
        out_specs=VMEM,
        out_shape=out,
        compiler_params=params(pieces, out, *feats, *old),
        cost_estimate=cost(
            2 * whole * count * region * width, 2 * whole * count * region + 8 * whole * width
        ),
    )(at, pieces, *feats, *old)


def spans(mask_bits):
    masks = [0]
    for b in mask_bits:
        masks = masks + [m | b for m in masks]
    return masks


def shards(features, key_grads, error_in, selected, bin_edges, threshold, moment, second, master):
    cores, owners = lax.axis_size("tensor"), lax.axis_size("dp")
    core, me = lax.axis_index("tensor"), lax.axis_index("dp")
    tokens, rows = features.shape
    width = key_grads.shape[1]
    region = rows // owners
    bins = bin_edges.shape[0] - 1
    pad = (0, LANES - bins)
    lo = jnp.pad(bin_edges[:-1], pad)[None]
    hi = jnp.pad(bin_edges[1:], pad)[None]
    core1 = core.reshape(1).astype(jnp.int32)

    [held] = load([features])
    n_chunks = 4 if cores == 2 else 1
    count = rows // n_chunks
    made, got = [], []
    for s in range(1, cores):
        theirs = shift(key_grads, "tensor", s)
        for j in range(n_chunks):
            made.append(part_sum(core1, held, theirs, j * count, count))
            got.append(shift(made[-1], "tensor", -s))
    mine, _ = lax.optimization_barrier((key_grads, made[-1]))
    own = part_sum(core1, held, mine, 0, rows, error_in[0])
    later, _ = lax.optimization_barrier((features, [own] + got))
    rest, outgoing = collect(selected[0, 0], lo, hi, own, got, n_chunks, owners, bins)
    error_out = rest.astype(jnp.bfloat16)[None]
    feats = [features] + [shift(later, "tensor", -s) for s in range(1, cores)]

    arrived = lax.all_to_all(
        outgoing.reshape(owners, SLOTS, width), "dp", split_axis=0, concat_axis=0, tiled=True
    )
    info = jnp.stack([me.astype(jnp.int32), threshold[0]])
    moment_new, second_new, master_new, weight = adam(
        info, lo, hi, arrived, moment, second, master, bins
    )

    bits = [1 << i for i in range(owners.bit_length() - 1)]
    if 1 << len(bits) == owners and len(bits) > 2 and region % LANES == 0:
        plane, line = spans(bits[:2]), spans(bits[2:])
        mine = jnp.stack([weight if m == 0 else swap(weight, "dp", m) for m in line])
        feats = load(feats)
        total = None
        for j, b in enumerate(plane):
            here = mine if b == 0 else swap(mine, "dp", b)
            at = jnp.stack([me ^ (b ^ m) for m in line] + [core]).astype(jnp.int32)
            total = project(at, feats, here, total, j == len(plane) - 1)
        keys = total
    else:
        whole = jnp.concatenate(feats, axis=0)
        whole = jnp.roll(whole, core * tokens, axis=0)
        keys = jnp.dot(
            whole,
            lax.all_gather(weight, "dp", axis=0, tiled=True),
            preferred_element_type=jnp.float32,
        ).astype(jnp.bfloat16)
    return (keys, error_out, moment_new, second_new, master_new)


def solution(mesh):
    in_specs = (
        P(("dp", "tensor"), None),
        P("dp", "tensor"),
        P("dp", None, "tensor"),
        P("dp", "tensor", None),
        P(),
        P(),
        P("dp", "tensor"),
        P("dp", "tensor"),
        P("dp", "tensor"),
    )
    out_specs = (
        P("dp", "tensor"),
        P("dp", None, "tensor"),
        P("dp", "tensor"),
        P("dp", "tensor"),
        P("dp", "tensor"),
    )
    return jax.shard_map(shards, mesh=mesh, in_specs=in_specs, out_specs=out_specs, check_vma=False)
```

```python
import functools

import jax
import jax.numpy as jnp
from jax import lax
from jax.experimental import pallas as pl
from jax.experimental.pallas import tpu as pltpu
from jax.sharding import PartitionSpec as P

CAP = 6
SLOTS = 8
LANES = 128

beta_first = 0.9
beta_second = 0.95
learn_rate = 0.001
decay_rate = 0.1
epsilon = 1e-06
adam_epsilon = 1e-08
step_count = 10.0

VMEM = pl.BlockSpec(memory_space=pltpu.VMEM)
SMEM = pl.BlockSpec(memory_space=pltpu.SMEM)
ANY = pl.BlockSpec(memory_space=pl.ANY)


def shift(x, axis, step):
    n = lax.axis_size(axis)
    return lax.ppermute(x, axis, [(i, (i + step) % n) for i in range(n)])


def swap(x, axis, mask):
    return lax.ppermute(x, axis, [(i, i ^ mask) for i in range(lax.axis_size(axis))])


def params(*arrays):
    total = sum(a.size * jnp.dtype(a.dtype).itemsize for a in arrays)
    return pltpu.CompilerParams(vmem_limit_bytes=total + (6 << 20))


def cost(flops, nbytes):
    return pl.CostEstimate(flops=flops, bytes_accessed=nbytes, transcendentals=0)


def load_kernel(pieces, n, *refs):
    sources, refs = refs[:n], refs[n:]
    state, refs = (refs[:3], refs[3:]) if len(refs) > n + 1 else ((), refs)
    copies = []
    if state:
        held, s_sem, refs = refs[-2], refs[-1], refs[:-2]
        copies = [
            pltpu.make_async_copy(ref, held.at[i], s_sem.at[i]) for i, ref in enumerate(state)
        ]
        for copy in copies:
            copy.start()
        base, refs = refs[0], refs[1:]
    targets, sem = refs[:n], refs[n]
    moves = []
    for i in range(n):
        rows = sources[i].shape[0] // pieces
        for j in range(pieces):
            part = pl.ds(j * rows, rows)
            moves.append(
                pltpu.make_async_copy(sources[i].at[part], targets[i].at[part], sem.at[i, j])
            )
            moves[-1].start()
    for copy in copies:
        copy.wait()
    if state:
        grad = jnp.zeros(base.shape, jnp.float32)
        base[...] = adam_step(held[0], held[1], held[2], grad)[2].astype(base.dtype)
    for move in moves:
        move.wait()


def load(arrays, *state):
    pieces = 8
    base, scratch = [], []
    if state:
        base = [jax.ShapeDtypeStruct(state[0].shape, jnp.bfloat16)]
        scratch = [
            pltpu.VMEM((len(state), *state[0].shape), jnp.float32),
            pltpu.SemaphoreType.DMA((len(state),)),
        ]
    fixed = [pltpu.with_memory_space_constraint(a, pltpu.HBM) for a in (*arrays, *state)]
    return pl.pallas_call(
        functools.partial(load_kernel, pieces, len(arrays)),
        in_specs=[ANY] * len(fixed),
        out_specs=[VMEM] * (len(base) + len(arrays)),
        out_shape=base + [pltpu.VMEM(a.shape, a.dtype) for a in arrays],
        scratch_shapes=[pltpu.SemaphoreType.DMA((len(arrays), pieces))] + scratch,
        compiler_params=params(*arrays, *state, *base),
        cost_estimate=cost(0, 4 * sum(a.size for a in arrays)),
    )(*fixed)


def part_kernel(first, core, f_ref, g_ref, *rest):
    tokens = f_ref.shape[0]
    count = rest[-1].shape[0]
    tile = min(1024, count)
    g = g_ref[pl.ds(pl.multiple_of(core[0] * tokens, tokens), tokens), :]
    for at in range(0, count, tile):
        p = lax.dot_general(
            f_ref[:, first + at : first + at + tile],
            g,
            (((0,), (0,)), ((), ())),
            preferred_element_type=jnp.float32,
        )
        if len(rest) > 1:
            p = p + rest[0][at : at + tile, :].astype(jnp.float32)
        rest[-1][at : at + tile, :] = p


def part_sum(core, features, grads, first, count, *error):
    tokens = features.shape[0]
    width = grads.shape[1]
    part = jax.ShapeDtypeStruct((count, width), jnp.float32)
    return pl.pallas_call(
        functools.partial(part_kernel, first),
        in_specs=[SMEM, VMEM, VMEM] + [VMEM] * len(error),
        out_specs=VMEM,
        out_shape=part,
        compiler_params=params(features, grads, part, *error),
        cost_estimate=cost(2 * tokens * count * width, 2 * tokens * count + 4 * count * width),
    )(core, features, grads, *error)


def collect_kernel(n_chunks, owners, bins, sel, lo_ref, hi_ref, own_ref, *refs):
    parts, (sum_ref, out_ref, count_ref) = refs[:-3], refs[-3:]
    rows, width = sum_ref.shape
    region = rows // owners
    lo, hi = lo_ref[...], hi_ref[...]
    count = rows // n_chunks
    tile = min(1024, count)
    acc = jnp.zeros((8, LANES), jnp.float32)
    for first in range(0, rows, tile):
        s = own_ref[first : first + tile, :]
        for ref in parts[first // count :: n_chunks]:
            s = s + ref[first % count : first % count + tile, :]
        sum_ref[first : first + tile, :] = s
        q = jnp.sum(s * s, axis=1, keepdims=True)
        ids = first + lax.broadcasted_iota(jnp.int32, (tile, LANES), 0)
        hit = (ids >= lo) & (ids < hi)
        acc = acc + jnp.sum(jnp.where(hit, q, 0.0).reshape(tile // 8, 8, LANES), axis=0)
    energy = jnp.sum(acc, axis=0, keepdims=True)
    lane = lax.broadcasted_iota(jnp.int32, (1, LANES), 1)
    out_ref[...] = jnp.zeros_like(out_ref)
    note = jnp.where((lane >= bins) & (lane < bins + CAP), -1.0, energy)
    for o in range(owners):
        out_ref[o * SLOTS + CAP : o * SLOTS + CAP + 1, :] = note
        count_ref[o] = 0

    def take(i, carry):
        r = sel[i]
        o = lax.div(r, region)
        k = count_ref[o]
        count_ref[o] = k + 1
        out_ref[pl.ds(o * SLOTS + k, 1), :] = sum_ref[pl.ds(r, 1), :]
        sum_ref[pl.ds(r, 1), :] = jnp.zeros((1, width), jnp.float32)
        at = pl.ds(o * SLOTS + CAP, 1)
        out_ref[at, :] = jnp.where(
            lane == bins + k, (r - o * region).astype(jnp.float32), out_ref[at, :]
        )
        return carry

    lax.fori_loop(0, sel.shape[0], take, 0, unroll=8)


def collect(selected, lo, hi, own, parts, n_chunks, owners, bins):
    rows, width = own.shape
    return pl.pallas_call(
        functools.partial(collect_kernel, n_chunks, owners, bins),
        in_specs=[SMEM, VMEM, VMEM, VMEM] + [VMEM] * len(parts),
        out_specs=[VMEM, VMEM],
        out_shape=[
            jax.ShapeDtypeStruct((rows, width), jnp.float32),
            jax.ShapeDtypeStruct((owners * SLOTS, width), jnp.float32),
        ],
        scratch_shapes=[pltpu.SMEM((owners,), jnp.int32)],
        compiler_params=params(own, own, own, *parts),
        cost_estimate=cost(8 * rows * width, 4 * rows * width * 3),
    )(selected, lo, hi, own, *parts)


def adam_step(moment, second, master, grad):
    moment_new = beta_first * moment + (1.0 - beta_first) * grad
    second_new = beta_second * second + (1.0 - beta_second) * grad * grad
    first_hat = moment_new / (1.0 - beta_first**step_count)
    second_hat = second_new / (1.0 - beta_second**step_count)
    master_new = master - learn_rate * (
        first_hat / (jnp.sqrt(second_hat) + adam_epsilon) + decay_rate * master
    )
    return moment_new, second_new, master_new


def adam_kernel(bins, info, lo_ref, hi_ref, arr_ref, m_ref, v_ref, w_ref, mo, vo, wo, bo):
    owners, slots, width = arr_ref.shape
    region = m_ref.shape[0]
    lo, hi = lo_ref[...], hi_ref[...]
    lane = lax.broadcasted_iota(jnp.int32, (1, LANES), 1)
    arr = arr_ref[...]
    notes = arr[:, CAP : CAP + 1, :]
    energy = jnp.sum(notes, axis=0)
    widths = jnp.maximum(hi - lo, 1).astype(jnp.float32)
    normal = 1.0 / jnp.sqrt(energy / (owners * width * widths) + epsilon)
    scale = jnp.where((lane >= info[1]) & (lane < bins), normal, 1.0)
    ids = info[0] * region + lax.broadcasted_iota(jnp.int32, (region, LANES), 0)
    row_scale = jnp.sum(
        jnp.where((ids >= lo) & (ids < hi), scale, 0.0), axis=1, keepdims=True
    )
    slot = lax.broadcasted_iota(jnp.int32, (owners, slots, LANES), 1)
    lane3 = lax.broadcasted_iota(jnp.int32, (owners, slots, LANES), 2)
    offset = jnp.sum(
        jnp.where((lane3 == bins + slot) & (slot < CAP), notes, 0.0), axis=2, keepdims=True
    )
    slot1 = lax.broadcasted_iota(jnp.int32, (owners, slots, 1), 1)
    offset = jnp.where(slot1 < CAP, offset, -1.0).reshape(owners * slots, 1)
    row = lax.broadcasted_iota(jnp.int32, (owners * slots, region), 1).astype(jnp.float32)
    place = jnp.where(row == offset, 1.0, 0.0)
    grad = lax.dot_general(
        place,
        arr.reshape(owners * slots, width),
        (((0,), (0,)), ((), ())),
        precision=lax.Precision.HIGHEST,
        preferred_element_type=jnp.float32,
    )
    moment_new, second_new, master_new = adam_step(
        m_ref[...], v_ref[...], w_ref[...], grad * row_scale
    )
    mo[...] = moment_new
    vo[...] = second_new
    wo[...] = master_new
    weight = master_new.astype(jnp.bfloat16)
    if bo.shape[0] == region:
        bo[...] = weight
        return
    sent = bo.shape[0]
    at = lax.broadcasted_iota(jnp.int32, (owners * slots, sent), 0)
    dense = (at // slots) * CAP + at % slots
    to = lax.broadcasted_iota(jnp.int32, (owners * slots, sent), 1)
    there = (dense == to) & (at % slots < CAP)
    number = jnp.sum(jnp.where(there, offset + 1.0, 0.0), axis=0, keepdims=True) - 1.0
    again = (offset == number) & (dense < to) & (at % slots < CAP)
    number = jnp.where(jnp.sum(jnp.where(again, 1.0, 0.0), axis=0, keepdims=True) > 0, -1.0, number)
    pick = jnp.where(
        lax.broadcasted_iota(jnp.int32, (region, sent), 0).astype(jnp.float32) == number, 1.0, 0.0
    )
    rows = lax.dot_general(
        pick.astype(jnp.bfloat16),
        weight,
        (((0,), (0,)), ((), ())),
        preferred_element_type=jnp.float32,
    )
    wide = jnp.concatenate([number, jnp.full((1, width - sent), -1.0, jnp.float32)], axis=1)
    last = lax.broadcasted_iota(jnp.int32, (sent, width), 0) == owners * CAP
    bo[...] = jnp.where(last, wide, rows).astype(jnp.bfloat16)


def adam(info, lo, hi, arrived, moment, second, master, bins, sent):
    f32 = jax.ShapeDtypeStruct(master.shape, jnp.float32)
    return pl.pallas_call(
        functools.partial(adam_kernel, bins),
        in_specs=[SMEM] + [VMEM] * 6,
        out_specs=[VMEM] * 4,
        out_shape=[f32, f32, f32, jax.ShapeDtypeStruct((sent, master.shape[1]), jnp.bfloat16)],
        compiler_params=params(arrived, arrived, *[f32] * 7),
        cost_estimate=cost(2 * 6 * arrived.size * master.shape[0], 30 * master.size),
    )(info, lo, hi, arrived, moment, second, master)


def project_kernel(last, n_slots, n_f, at, base_ref, new_ref, *refs):
    feats, old, out_ref = refs[:n_f], refs[n_f:-1], refs[-1]
    count, region, width = base_ref.shape
    sent = new_ref.shape[1]
    tokens = feats[0].shape[0]
    ids = lax.broadcasted_iota(jnp.int32, (region, sent), 0).astype(jnp.float32)
    weights = []
    for j in range(count):
        rows = new_ref[j]
        number = rows[n_slots : n_slots + 1, :sent].astype(jnp.float32)
        pick = jnp.where(ids == number, 1.0, 0.0)
        put = jnp.dot(pick.astype(jnp.bfloat16), rows, preferred_element_type=jnp.float32)
        hit = jnp.max(pick, axis=1, keepdims=True) > 0
        weights.append(
            jnp.where(hit, put, base_ref[j].astype(jnp.float32)).astype(jnp.bfloat16)
        )
    for i, f_ref in enumerate(feats):
        mine = pl.ds(i * tokens, tokens)
        total = old[0][mine, :] if old else None
        for j in range(count):
            cols = pl.ds(pl.multiple_of(at[j] * region, region), region)
            part = jnp.dot(f_ref[:, cols], weights[j], preferred_element_type=jnp.float32)
            total = part if total is None else total + part
        if last:
            place = lax.rem(at[count] + i, n_f) * tokens
            mine = pl.ds(pl.multiple_of(place, tokens), tokens)
        out_ref[mine, :] = total.astype(out_ref.dtype)


def project(at, feats, base, changed, total, last, n_slots):
    count, region, width = base.shape
    whole = len(feats) * feats[0].shape[0]
    old = [] if total is None else [total]
    out = jax.ShapeDtypeStruct((whole, width), jnp.bfloat16 if last else jnp.float32)
    return pl.pallas_call(
        functools.partial(project_kernel, last, n_slots, len(feats)),
        in_specs=[SMEM, VMEM, VMEM] + [VMEM] * (len(feats) + len(old)),
        out_specs=VMEM,
        out_shape=out,
        compiler_params=params(base, changed, out, *feats, *old),
        cost_estimate=cost(
            2 * whole * count * region * width, 2 * whole * count * region + 8 * whole * width
        ),
    )(at, base, changed, *feats, *old)


def spans(mask_bits):
    masks = [0]
    for b in mask_bits:
        masks = masks + [m | b for m in masks]
    return masks


def shards(features, key_grads, error_in, selected, bin_edges, threshold, moment, second, master):
    cores, owners = lax.axis_size("tensor"), lax.axis_size("dp")
    core, me = lax.axis_index("tensor"), lax.axis_index("dp")
    tokens, rows = features.shape
    width = key_grads.shape[1]
    region = rows // owners
    bins = bin_edges.shape[0] - 1
    pad = (0, LANES - bins)
    lo = jnp.pad(bin_edges[:-1], pad)[None]
    hi = jnp.pad(bin_edges[1:], pad)[None]
    core1 = core.reshape(1).astype(jnp.int32)

    bits = [1 << i for i in range(owners.bit_length() - 1)]
    n_slots = owners * CAP
    sent = (n_slots + 16) // 16 * 16
    fast = 1 << len(bits) == owners and len(bits) > 2 and region % LANES == 0
    fast = fast and sent <= LANES and region <= 256

    base, held = load([features], moment, second, master)
    n_chunks = 4 if cores == 2 else 1
    count = rows // n_chunks
    made, got = [], []
    for s in range(1, cores):
        theirs = shift(key_grads, "tensor", s)
        for j in range(n_chunks):
            made.append(part_sum(core1, held, theirs, j * count, count))
            got.append(shift(made[-1], "tensor", -s))
    mine, _ = lax.optimization_barrier((key_grads, made[-1]))
    own = part_sum(core1, held, mine, 0, rows, error_in[0])
    later, _ = lax.optimization_barrier((features, [own] + got))
    rest, outgoing = collect(selected[0, 0], lo, hi, own, got, n_chunks, owners, bins)
    error_out = rest.astype(jnp.bfloat16)[None]
    feats = [features] + [shift(later, "tensor", -s) for s in range(1, cores)]

    arrived = lax.all_to_all(
        outgoing.reshape(owners, SLOTS, width), "dp", split_axis=0, concat_axis=0, tiled=True
    )
    info = jnp.stack([me.astype(jnp.int32), threshold[0]])
    moment_new, second_new, master_new, changed = adam(
        info, lo, hi, arrived, moment, second, master, bins, sent if fast else region
    )

    if fast:
        plane, line = spans(bits[:2]), spans(bits[2:])

        def along(x):
            return jnp.stack([x if m == 0 else swap(x, "dp", m) for m in line])

        def across(x):
            return [x if b == 0 else swap(x, "dp", b) for b in plane]

        early, _ = lax.optimization_barrier((base, own))
        bases = across(along(early))
        changes = across(along(changed))
        feats = load(feats)
        total = None
        for j, b in enumerate(plane):
            at = jnp.stack([me ^ (b ^ m) for m in line] + [core]).astype(jnp.int32)
            final = j == len(plane) - 1
            total = project(at, feats, bases[j], changes[j], total, final, n_slots)
        keys = total
    else:
        whole = jnp.concatenate(feats, axis=0)
        whole = jnp.roll(whole, core * tokens, axis=0)
        keys = jnp.dot(
            whole,
            lax.all_gather(changed, "dp", axis=0, tiled=True),
            preferred_element_type=jnp.float32,
        ).astype(jnp.bfloat16)
    return (keys, error_out, moment_new, second_new, master_new)


def solution(mesh):
    in_specs = (
        P(("dp", "tensor"), None),
        P("dp", "tensor"),
        P("dp", None, "tensor"),
        P("dp", "tensor", None),
        P(),
        P(),
        P("dp", "tensor"),
        P("dp", "tensor"),
        P("dp", "tensor"),
    )
    out_specs = (
        P("dp", "tensor"),
        P("dp", None, "tensor"),
        P("dp", "tensor"),
        P("dp", "tensor"),
        P("dp", "tensor"),
    )
    return jax.shard_map(shards, mesh=mesh, in_specs=in_specs, out_specs=out_specs, check_vma=False)
```

```python
import functools

import jax
import jax.numpy as jnp
from jax import lax
from jax.experimental import pallas as pl
from jax.experimental.pallas import tpu as pltpu
from jax.sharding import PartitionSpec as P

CAP = 6
SLOTS = 8
LANES = 128

beta_first = 0.9
beta_second = 0.95
learn_rate = 0.001
decay_rate = 0.1
epsilon = 1e-06
adam_epsilon = 1e-08
step_count = 10.0

VMEM = pl.BlockSpec(memory_space=pltpu.VMEM)
SMEM = pl.BlockSpec(memory_space=pltpu.SMEM)
ANY = pl.BlockSpec(memory_space=pl.ANY)


def shift(x, axis, step):
    n = lax.axis_size(axis)
    return lax.ppermute(x, axis, [(i, (i + step) % n) for i in range(n)])


def swap(x, axis, mask):
    return lax.ppermute(x, axis, [(i, i ^ mask) for i in range(lax.axis_size(axis))])


def params(*arrays):
    total = sum(a.size * jnp.dtype(a.dtype).itemsize for a in arrays)
    return pltpu.CompilerParams(vmem_limit_bytes=total + (6 << 20))


def cost(flops, nbytes):
    return pl.CostEstimate(flops=flops, bytes_accessed=nbytes, transcendentals=0)


def load_kernel(pieces, *refs):
    n = len(refs) // 2
    sources, targets, sem = refs[:n], refs[n : 2 * n], refs[2 * n]
    copies = []
    for i in range(n):
        rows = sources[i].shape[0] // pieces
        for j in range(pieces):
            part = pl.ds(j * rows, rows)
            copies.append(
                pltpu.make_async_copy(sources[i].at[part], targets[i].at[part], sem.at[i, j])
            )
            copies[-1].start()
    for copy in copies:
        copy.wait()


def load(arrays):
    pieces = 8
    return pl.pallas_call(
        functools.partial(load_kernel, pieces),
        in_specs=[ANY] * len(arrays),
        out_specs=[VMEM] * len(arrays),
        out_shape=[pltpu.VMEM(a.shape, a.dtype) for a in arrays],
        scratch_shapes=[pltpu.SemaphoreType.DMA((len(arrays), pieces))],
        compiler_params=params(*arrays),
        cost_estimate=cost(0, 4 * sum(a.size for a in arrays)),
    )(*[pltpu.with_memory_space_constraint(a, pltpu.HBM) for a in arrays])


def part_kernel(first, core, f_ref, g_ref, *rest):
    tokens = f_ref.shape[0]
    count = rest[-1].shape[0]
    tile = min(1024, count)
    g = g_ref[pl.ds(pl.multiple_of(core[0] * tokens, tokens), tokens), :]
    for at in range(0, count, tile):
        p = lax.dot_general(
            f_ref[:, first + at : first + at + tile],
            g,
            (((0,), (0,)), ((), ())),
            preferred_element_type=jnp.float32,
        )
        if len(rest) > 1:
            p = p + rest[0][at : at + tile, :].astype(jnp.float32)
        rest[-1][at : at + tile, :] = p


def part_sum(core, features, grads, first, count, *error):
    tokens = features.shape[0]
    width = grads.shape[1]
    part = jax.ShapeDtypeStruct((count, width), jnp.float32)
    return pl.pallas_call(
        functools.partial(part_kernel, first),
        in_specs=[SMEM, VMEM, VMEM] + [VMEM] * len(error),
        out_specs=VMEM,
        out_shape=part,
        compiler_params=params(features, grads, part, *error),
        cost_estimate=cost(2 * tokens * count * width, 2 * tokens * count + 4 * count * width),
    )(core, features, grads, *error)


def collect_kernel(n_chunks, owners, bins, sel, lo_ref, hi_ref, own_ref, *refs):
    parts, (sum_ref, out_ref, count_ref) = refs[:-3], refs[-3:]
    rows, width = sum_ref.shape
    region = rows // owners
    lo, hi = lo_ref[...], hi_ref[...]
    count = rows // n_chunks
    tile = min(1024, count)
    acc = jnp.zeros((8, LANES), jnp.float32)
    for first in range(0, rows, tile):
        s = own_ref[first : first + tile, :]
        for ref in parts[first // count :: n_chunks]:
            s = s + ref[first % count : first % count + tile, :]
        sum_ref[first : first + tile, :] = s
        q = jnp.sum(s * s, axis=1, keepdims=True)
        ids = first + lax.broadcasted_iota(jnp.int32, (tile, LANES), 0)
        hit = (ids >= lo) & (ids < hi)
        acc = acc + jnp.sum(jnp.where(hit, q, 0.0).reshape(tile // 8, 8, LANES), axis=0)
    energy = jnp.sum(acc, axis=0, keepdims=True)
    lane = lax.broadcasted_iota(jnp.int32, (1, LANES), 1)
    out_ref[...] = jnp.zeros_like(out_ref)
    note = jnp.where((lane >= bins) & (lane < bins + CAP), -1.0, energy)
    for o in range(owners):
        out_ref[o * SLOTS + CAP : o * SLOTS + CAP + 1, :] = note
        count_ref[o] = 0

    def take(i, carry):
        r = sel[i]
        o = lax.div(r, region)
        k = count_ref[o]
        count_ref[o] = k + 1
        out_ref[pl.ds(o * SLOTS + k, 1), :] = sum_ref[pl.ds(r, 1), :]
        sum_ref[pl.ds(r, 1), :] = jnp.zeros((1, width), jnp.float32)
        at = pl.ds(o * SLOTS + CAP, 1)
        out_ref[at, :] = jnp.where(
            lane == bins + k, (r - o * region).astype(jnp.float32), out_ref[at, :]
        )
        return carry

    lax.fori_loop(0, sel.shape[0], take, 0, unroll=8)


def collect(selected, lo, hi, own, parts, n_chunks, owners, bins):
    rows, width = own.shape
    return pl.pallas_call(
        functools.partial(collect_kernel, n_chunks, owners, bins),
        in_specs=[SMEM, VMEM, VMEM, VMEM] + [VMEM] * len(parts),
        out_specs=[VMEM, VMEM],
        out_shape=[
            jax.ShapeDtypeStruct((rows, width), jnp.float32),
            jax.ShapeDtypeStruct((owners * SLOTS, width), jnp.float32),
        ],
        scratch_shapes=[pltpu.SMEM((owners,), jnp.int32)],
        compiler_params=params(own, own, own, *parts),
        cost_estimate=cost(8 * rows * width, 4 * rows * width * 3),
    )(selected, lo, hi, own, *parts)


def grad_kernel(bins, info, lo_ref, hi_ref, arr_ref, m_ref, v_ref, w_ref, g_ref, b_ref):
    owners, slots, width = arr_ref.shape
    region = g_ref.shape[0]
    lo, hi = lo_ref[...], hi_ref[...]
    lane = lax.broadcasted_iota(jnp.int32, (1, LANES), 1)
    arr = arr_ref[...]
    notes = arr[:, CAP : CAP + 1, :]
    energy = jnp.sum(notes, axis=0)
    widths = jnp.maximum(hi - lo, 1).astype(jnp.float32)
    normal = 1.0 / jnp.sqrt(energy / (owners * width * widths) + epsilon)
    scale = jnp.where((lane >= info[1]) & (lane < bins), normal, 1.0)
    ids = info[0] * region + lax.broadcasted_iota(jnp.int32, (region, LANES), 0)
    row_scale = jnp.sum(
        jnp.where((ids >= lo) & (ids < hi), scale, 0.0), axis=1, keepdims=True
    )
    slot = lax.broadcasted_iota(jnp.int32, (owners, slots, LANES), 1)
    lane3 = lax.broadcasted_iota(jnp.int32, (owners, slots, LANES), 2)
    offset = jnp.sum(
        jnp.where((lane3 == bins + slot) & (slot < CAP), notes, 0.0), axis=2, keepdims=True
    )
    slot1 = lax.broadcasted_iota(jnp.int32, (owners, slots, 1), 1)
    offset = jnp.where(slot1 < CAP, offset, -1.0).reshape(owners * slots, 1)
    row = lax.broadcasted_iota(jnp.int32, (owners * slots, region), 1).astype(jnp.float32)
    place = jnp.where(row == offset, 1.0, 0.0)
    grad = lax.dot_general(
        place,
        arr.reshape(owners * slots, width),
        (((0,), (0,)), ((), ())),
        precision=lax.Precision.HIGHEST,
        preferred_element_type=jnp.float32,
    )
    grad = grad * row_scale
    g_ref[...] = grad
    b_ref[...] = adam_step(m_ref[...], v_ref[...], w_ref[...], grad)[2].astype(b_ref.dtype)


def adam_step(moment, second, master, grad):
    moment_new = beta_first * moment + (1.0 - beta_first) * grad
    second_new = beta_second * second + (1.0 - beta_second) * grad * grad
    first_hat = moment_new / (1.0 - beta_first**step_count)
    second_hat = second_new / (1.0 - beta_second**step_count)
    master_new = master - learn_rate * (
        first_hat / (jnp.sqrt(second_hat) + adam_epsilon) + decay_rate * master
    )
    return moment_new, second_new, master_new


def weigh(info, lo, hi, arrived, moment, second, master, bins):
    f32 = jax.ShapeDtypeStruct(master.shape, jnp.float32)
    return pl.pallas_call(
        functools.partial(grad_kernel, bins),
        in_specs=[SMEM] + [VMEM] * 6,
        out_specs=[VMEM] * 2,
        out_shape=[f32, jax.ShapeDtypeStruct(master.shape, jnp.bfloat16)],
        compiler_params=params(arrived, arrived, *[f32] * 5),
        cost_estimate=cost(2 * 6 * arrived.size * master.shape[0], 30 * master.size),
    )(info, lo, hi, arrived, moment, second, master)


def project_kernel(step, last, n_f, at, *refs):
    feats, refs = refs[:n_f], refs[n_f:]
    if step == 0:
        sources, feats, sem = feats, refs[-n_f - 1 : -1], refs[-1]
        out_ref, refs = refs[-n_f - 2], refs[: -n_f - 2]
    else:
        out_ref, refs = refs[-1], refs[:-1]
    tokens, rows = feats[0].shape
    region = refs[0].shape[-2]
    owners = rows // region
    weights, old = [], None
    for ref in refs:
        if ref.dtype == jnp.float32:
            old = ref
        elif len(ref.shape) == 2:
            weights.append(ref[...])
        else:
            weights += [ref[j] for j in range(ref.shape[0])]
    count = len(weights)
    here = [
        pl.ds(pl.multiple_of(at[q] * region, region), region)
        for q in range(0 if step == 0 else step * count, owners if step == 0 else (step + 1) * count)
    ]
    if step == 0:
        moves = [
            [
                pltpu.make_async_copy(sources[i].at[:, c], feats[i].at[:, c], sem.at[i, q])
                for q, c in enumerate(here)
            ]
            for i in range(n_f)
        ]
        for q in range(owners):
            for i in range(n_f):
                moves[i][q].start()
    weight = jnp.concatenate(weights, axis=0)
    for i, f_ref in enumerate(feats):
        mine = pl.ds(i * tokens, tokens)
        if step == 0:
            for q in range(count):
                moves[i][q].wait()
        part = jnp.concatenate([f_ref[:, c] for c in here[:count]], axis=1)
        total = jnp.dot(part, weight, preferred_element_type=jnp.float32)
        if old is not None:
            total = total + old[mine, :]
        if last:
            place = lax.rem(at[owners] + i, n_f) * tokens
            mine = pl.ds(pl.multiple_of(place, tokens), tokens)
        out_ref[mine, :] = total.astype(out_ref.dtype)
    if step == 0:
        for i in range(n_f):
            for q in range(count, owners):
                moves[i][q].wait()


def project(step, at, feats, pieces, total, last):
    region, width = pieces[0].shape[-2:]
    tokens, rows = feats[0].shape
    whole = len(feats) * tokens
    old = [] if total is None else [total]
    out = jax.ShapeDtypeStruct((whole, width), jnp.bfloat16 if last else jnp.float32)
    held, scratch = [], []
    if step == 0:
        feats = [pltpu.with_memory_space_constraint(f, pltpu.HBM) for f in feats]
        held = [pltpu.VMEM(f.shape, f.dtype) for f in feats]
        scratch = [pltpu.SemaphoreType.DMA((len(feats), rows // region))]
    weights = sum(p.size for p in pieces)
    return pl.pallas_call(
        functools.partial(project_kernel, step, last, len(feats)),
        in_specs=[SMEM]
        + [ANY if step == 0 else VMEM] * len(feats)
        + [VMEM] * (len(pieces) + len(old)),
        out_specs=[VMEM] * (1 + len(held)),
        out_shape=[out] + held,
        scratch_shapes=scratch,
        compiler_params=params(*pieces, out, *feats, *old),
        cost_estimate=cost(
            2 * whole * weights, 2 * whole * (rows if held else weights // width) + 8 * whole * width
        ),
    )(at, *feats, *pieces, *old)


def spans(mask_bits):
    masks = [0]
    for b in mask_bits:
        masks = masks + [m | b for m in masks]
    return masks


def shards(features, key_grads, error_in, selected, bin_edges, threshold, moment, second, master):
    cores, owners = lax.axis_size("tensor"), lax.axis_size("dp")
    core, me = lax.axis_index("tensor"), lax.axis_index("dp")
    tokens, rows = features.shape
    width = key_grads.shape[1]
    region = rows // owners
    bins = bin_edges.shape[0] - 1
    pad = (0, LANES - bins)
    lo = jnp.pad(bin_edges[:-1], pad)[None]
    hi = jnp.pad(bin_edges[1:], pad)[None]
    core1 = core.reshape(1).astype(jnp.int32)

    [held] = load([features])
    n_chunks = 4 if cores == 2 else 1
    count = rows // n_chunks
    made, got = [], []
    for s in range(1, cores):
        theirs = shift(key_grads, "tensor", s)
        for j in range(n_chunks):
            made.append(part_sum(core1, held, theirs, j * count, count))
            got.append(shift(made[-1], "tensor", -s))
    mine, _ = lax.optimization_barrier((key_grads, made[-1]))
    own = part_sum(core1, held, mine, 0, rows, error_in[0])
    later, _ = lax.optimization_barrier((features, [own] + got))
    rest, outgoing = collect(selected[0, 0], lo, hi, own, got, n_chunks, owners, bins)
    error_out = rest.astype(jnp.bfloat16)[None]
    feats = [features] + [shift(later, "tensor", -s) for s in range(1, cores)]

    arrived = lax.all_to_all(
        outgoing.reshape(owners, SLOTS, width), "dp", split_axis=0, concat_axis=0, tiled=True
    )
    info = jnp.stack([me.astype(jnp.int32), threshold[0]])
    grad, weight = weigh(info, lo, hi, arrived, moment, second, master, bins)

    bits = [1 << i for i in range(owners.bit_length() - 1)]
    if 1 << len(bits) == owners and len(bits) > 2 and region % LANES == 0:
        plane, line = spans(bits[:2]), spans(bits[2:])
        rest = jnp.stack([swap(weight, "dp", m) for m in line[1:]])
        groups = [[weight, rest]]
        groups += [[swap(weight, "dp", b), swap(rest, "dp", b)] for b in plane[1:]]
        at = jnp.stack([me ^ (b ^ m) for b in plane for m in line] + [core]).astype(jnp.int32)
        keys, *feats = project(0, at, feats, groups[0], None, False)
        for j in range(1, len(plane)):
            [keys] = project(j, at, feats, groups[j], keys, j == len(plane) - 1)
    else:
        whole = jnp.concatenate(feats, axis=0)
        whole = jnp.roll(whole, core * tokens, axis=0)
        keys = jnp.dot(
            whole,
            lax.all_gather(weight, "dp", axis=0, tiled=True),
            preferred_element_type=jnp.float32,
        ).astype(jnp.bfloat16)
    moment_new, second_new, master_new = adam_step(moment, second, master, grad)
    return (keys, error_out, moment_new, second_new, master_new)


def solution(mesh):
    in_specs = (
        P(("dp", "tensor"), None),
        P("dp", "tensor"),
        P("dp", None, "tensor"),
        P("dp", "tensor", None),
        P(),
        P(),
        P("dp", "tensor"),
        P("dp", "tensor"),
        P("dp", "tensor"),
    )
    out_specs = (
        P("dp", "tensor"),
        P("dp", None, "tensor"),
        P("dp", "tensor"),
        P("dp", "tensor"),
        P("dp", "tensor"),
    )
    return jax.shard_map(shards, mesh=mesh, in_specs=in_specs, out_specs=out_specs, check_vma=False)
```

```python
import functools

import jax
import jax.numpy as jnp
from jax import lax
from jax.experimental import pallas as pl
from jax.experimental.pallas import tpu as pltpu
from jax.sharding import PartitionSpec as P

CAP = 6
SLOTS = 8
LANES = 128

beta_first = 0.9
beta_second = 0.95
learn_rate = 0.001
decay_rate = 0.1
epsilon = 1e-06
adam_epsilon = 1e-08
step_count = 10.0

VMEM = pl.BlockSpec(memory_space=pltpu.VMEM)
SMEM = pl.BlockSpec(memory_space=pltpu.SMEM)
ANY = pl.BlockSpec(memory_space=pl.ANY)


def shift(x, axis, step):
    n = lax.axis_size(axis)
    return lax.ppermute(x, axis, [(i, (i + step) % n) for i in range(n)])


def swap(x, axis, mask):
    return lax.ppermute(x, axis, [(i, i ^ mask) for i in range(lax.axis_size(axis))])


def params(*arrays):
    total = sum(a.size * jnp.dtype(a.dtype).itemsize for a in arrays)
    return pltpu.CompilerParams(vmem_limit_bytes=total + (6 << 20))


def bounds(edges):
    lane = lax.broadcasted_iota(jnp.int32, (1, LANES), 1)
    lo = hi = jnp.zeros((1, LANES), jnp.int32)
    for b in range(edges.shape[0] - 1):
        lo = jnp.where(lane == b, edges[b], lo)
        hi = jnp.where(lane == b, edges[b + 1], hi)
    return lo, hi


def cost(flops, nbytes):
    return pl.CostEstimate(flops=flops, bytes_accessed=nbytes, transcendentals=0)


def load_kernel(pieces, *refs):
    n = len(refs) // 2
    sources, targets, sem = refs[:n], refs[n : 2 * n], refs[2 * n]
    copies = []
    for i in range(n):
        rows = sources[i].shape[0] // pieces
        for j in range(pieces):
            part = pl.ds(j * rows, rows)
            copies.append(
                pltpu.make_async_copy(sources[i].at[part], targets[i].at[part], sem.at[i, j])
            )
            copies[-1].start()
    for copy in copies:
        copy.wait()


def load(arrays):
    pieces = 8
    return pl.pallas_call(
        functools.partial(load_kernel, pieces),
        in_specs=[ANY] * len(arrays),
        out_specs=[VMEM] * len(arrays),
        out_shape=[pltpu.VMEM(a.shape, a.dtype) for a in arrays],
        scratch_shapes=[pltpu.SemaphoreType.DMA((len(arrays), pieces))],
        compiler_params=params(*arrays),
        cost_estimate=cost(0, 4 * sum(a.size for a in arrays)),
    )(*[pltpu.with_memory_space_constraint(a, pltpu.HBM) for a in arrays])


def part_kernel(first, core, f_ref, g_ref, *rest):
    tokens = f_ref.shape[0]
    count = rest[-1].shape[0]
    tile = min(1024, count)
    g = g_ref[pl.ds(pl.multiple_of(core[0] * tokens, tokens), tokens), :]
    for at in range(0, count, tile):
        p = lax.dot_general(
            f_ref[:, first + at : first + at + tile],
            g,
            (((0,), (0,)), ((), ())),
            preferred_element_type=jnp.float32,
        )
        if len(rest) > 1:
            p = p + rest[0][at : at + tile, :].astype(jnp.float32)
        rest[-1][at : at + tile, :] = p


def part_sum(core, features, grads, first, count, *error):
    tokens = features.shape[0]
    width = grads.shape[1]
    part = jax.ShapeDtypeStruct((count, width), jnp.float32)
    return pl.pallas_call(
        functools.partial(part_kernel, first),
        in_specs=[SMEM, VMEM, VMEM] + [VMEM] * len(error),
        out_specs=VMEM,
        out_shape=part,
        compiler_params=params(features, grads, part, *error),
        cost_estimate=cost(2 * tokens * count * width, 2 * tokens * count + 4 * count * width),
    )(core, features, grads, *error)


def collect_kernel(n_chunks, owners, bins, sel, edges, own_ref, *refs):
    parts, (sum_ref, out_ref, count_ref) = refs[:-3], refs[-3:]
    rows, width = sum_ref.shape
    region = rows // owners
    lo, hi = bounds(edges)
    count = rows // n_chunks
    tile = min(1024, count)
    acc = jnp.zeros((8, LANES), jnp.float32)
    for first in range(0, rows, tile):
        s = own_ref[first : first + tile, :]
        for ref in parts[first // count :: n_chunks]:
            s = s + ref[first % count : first % count + tile, :]
        sum_ref[first : first + tile, :] = s
        q = jnp.sum(s * s, axis=1, keepdims=True)
        ids = first + lax.broadcasted_iota(jnp.int32, (tile, LANES), 0)
        hit = (ids >= lo) & (ids < hi)
        acc = acc + jnp.sum(jnp.where(hit, q, 0.0).reshape(tile // 8, 8, LANES), axis=0)
    energy = jnp.sum(acc, axis=0, keepdims=True)
    lane = lax.broadcasted_iota(jnp.int32, (1, LANES), 1)
    out_ref[...] = jnp.zeros_like(out_ref)
    note = jnp.where((lane >= bins) & (lane < bins + CAP), -1.0, energy)
    for o in range(owners):
        out_ref[o * SLOTS + CAP : o * SLOTS + CAP + 1, :] = note
        count_ref[o] = 0

    def take(i, carry):
        r = sel[i]
        o = lax.div(r, region)
        k = count_ref[o]
        count_ref[o] = k + 1
        out_ref[pl.ds(o * SLOTS + k, 1), :] = sum_ref[pl.ds(r, 1), :]
        sum_ref[pl.ds(r, 1), :] = jnp.zeros((1, width), jnp.float32)
        at = pl.ds(o * SLOTS + CAP, 1)
        out_ref[at, :] = jnp.where(
            lane == bins + k, (r - o * region).astype(jnp.float32), out_ref[at, :]
        )
        return carry

    lax.fori_loop(0, sel.shape[0], take, 0, unroll=8)


def collect(selected, edges, own, parts, n_chunks, owners, bins):
    rows, width = own.shape
    return pl.pallas_call(
        functools.partial(collect_kernel, n_chunks, owners, bins),
        in_specs=[SMEM, SMEM, VMEM] + [VMEM] * len(parts),
        out_specs=[VMEM, VMEM],
        out_shape=[
            jax.ShapeDtypeStruct((rows, width), jnp.float32),
            jax.ShapeDtypeStruct((owners * SLOTS, width), jnp.float32),
        ],
        scratch_shapes=[pltpu.SMEM((owners,), jnp.int32)],
        compiler_params=params(own, own, own, *parts),
        cost_estimate=cost(8 * rows * width, 4 * rows * width * 3),
    )(selected, edges, own, *parts)


def grad_kernel(bins, me, least, edges, arr_ref, m_ref, v_ref, w_ref, g_ref, b_ref):
    owners, slots, width = arr_ref.shape
    region = g_ref.shape[0]
    lo, hi = bounds(edges)
    lane = lax.broadcasted_iota(jnp.int32, (1, LANES), 1)
    arr = arr_ref[...]
    notes = arr[:, CAP : CAP + 1, :]
    energy = jnp.sum(notes, axis=0)
    widths = jnp.maximum(hi - lo, 1).astype(jnp.float32)
    normal = 1.0 / jnp.sqrt(energy / (owners * width * widths) + epsilon)
    scale = jnp.where((lane >= least[0]) & (lane < bins), normal, 1.0)
    ids = me[0] * region + lax.broadcasted_iota(jnp.int32, (region, LANES), 0)
    row_scale = jnp.sum(
        jnp.where((ids >= lo) & (ids < hi), scale, 0.0), axis=1, keepdims=True
    )
    slot = lax.broadcasted_iota(jnp.int32, (owners, slots, LANES), 1)
    lane3 = lax.broadcasted_iota(jnp.int32, (owners, slots, LANES), 2)
    offset = jnp.sum(
        jnp.where((lane3 == bins + slot) & (slot < CAP), notes, 0.0), axis=2, keepdims=True
    )
    slot1 = lax.broadcasted_iota(jnp.int32, (owners, slots, 1), 1)
    offset = jnp.where(slot1 < CAP, offset, -1.0).reshape(owners * slots, 1)
    row = lax.broadcasted_iota(jnp.int32, (owners * slots, region), 1).astype(jnp.float32)
    place = jnp.where(row == offset, 1.0, 0.0)
    grad = lax.dot_general(
        place,
        arr.reshape(owners * slots, width),
        (((0,), (0,)), ((), ())),
        precision=lax.Precision.HIGHEST,
        preferred_element_type=jnp.float32,
    )
    grad = grad * row_scale
    g_ref[...] = grad
    b_ref[...] = adam_step(m_ref[...], v_ref[...], w_ref[...], grad)[2].astype(b_ref.dtype)


def adam_step(moment, second, master, grad):
    moment_new = beta_first * moment + (1.0 - beta_first) * grad
    second_new = beta_second * second + (1.0 - beta_second) * grad * grad
    first_hat = moment_new / (1.0 - beta_first**step_count)
    second_hat = second_new / (1.0 - beta_second**step_count)
    master_new = master - learn_rate * (
        first_hat / (jnp.sqrt(second_hat) + adam_epsilon) + decay_rate * master
    )
    return moment_new, second_new, master_new


def weigh(me, least, edges, arrived, moment, second, master):
    f32 = jax.ShapeDtypeStruct(master.shape, jnp.float32)
    return pl.pallas_call(
        functools.partial(grad_kernel, edges.shape[0] - 1),
        in_specs=[SMEM] * 3 + [VMEM] * 4,
        out_specs=[VMEM] * 2,
        out_shape=[f32, jax.ShapeDtypeStruct(master.shape, jnp.bfloat16)],
        compiler_params=params(arrived, arrived, *[f32] * 5),
        cost_estimate=cost(2 * 6 * arrived.size * master.shape[0], 30 * master.size),
    )(me, least, edges, arrived, moment, second, master)


def state_kernel(g_ref, m_ref, v_ref, w_ref, *outs):
    new = adam_step(m_ref[...], v_ref[...], w_ref[...], g_ref[...])
    for out, value in zip(outs, new):
        out[...] = value


def state(grad, moment, second, master):
    return pl.pallas_call(
        state_kernel,
        in_specs=[VMEM] * 4,
        out_specs=[VMEM] * 3,
        out_shape=[jax.ShapeDtypeStruct(grad.shape, jnp.float32)] * 3,
        compiler_params=params(*[grad] * 7),
        cost_estimate=cost(20 * grad.size, 28 * grad.size),
    )(grad, moment, second, master)


def round_kernel(x_ref, o_ref):
    o_ref[...] = x_ref[...].astype(o_ref.dtype)


def rounded(x):
    out = jax.ShapeDtypeStruct(x.shape, jnp.bfloat16)
    return pl.pallas_call(
        round_kernel,
        in_specs=[VMEM],
        out_specs=VMEM,
        out_shape=out,
        compiler_params=params(x, out),
        cost_estimate=cost(x.size, 6 * x.size),
    )(x)


def join_kernel(*refs):
    for i, ref in enumerate(refs[:-1]):
        refs[-1][i] = ref[...]


def join(arrays):
    out = jax.ShapeDtypeStruct((len(arrays), *arrays[0].shape), arrays[0].dtype)
    return pl.pallas_call(
        join_kernel,
        in_specs=[VMEM] * len(arrays),
        out_specs=VMEM,
        out_shape=out,
        compiler_params=params(out, out),
        cost_estimate=cost(out.size, 4 * out.size),
    )(*arrays)


def project_kernel(masks, last, n_f, me, core, *refs):
    feats, pieces, out_ref = refs[:n_f], refs[n_f : n_f + 2], refs[-1]
    tokens = feats[0].shape[0]
    region = pieces[0].shape[0]
    weight = jnp.concatenate(
        [pieces[0][...]] + [pieces[1][j] for j in range(pieces[1].shape[0])], axis=0
    )
    for i, f_ref in enumerate(feats):
        mine = pl.ds(i * tokens, tokens)
        part = [
            f_ref[:, pl.ds(pl.multiple_of((me[0] ^ m) * region, region), region)] for m in masks
        ]
        total = jnp.dot(
            jnp.concatenate(part, axis=1), weight, preferred_element_type=jnp.float32
        )
        if len(refs) > n_f + 3:
            total = total + refs[n_f + 2][mine, :]
        if last:
            place = lax.rem(core[0] + i, n_f) * tokens
            mine = pl.ds(pl.multiple_of(place, tokens), tokens)
        out_ref[mine, :] = total.astype(out_ref.dtype)


def project(masks, me, core, feats, pieces, total, last):
    region, width = pieces[0].shape
    whole = len(feats) * feats[0].shape[0]
    old = [] if total is None else [total]
    out = jax.ShapeDtypeStruct((whole, width), jnp.bfloat16 if last else jnp.float32)
    depth = len(masks) * region
    return pl.pallas_call(
        functools.partial(project_kernel, masks, last, len(feats)),
        in_specs=[SMEM, SMEM] + [VMEM] * (len(feats) + 2 + len(old)),
        out_specs=VMEM,
        out_shape=out,
        compiler_params=params(*pieces, out, *feats, *old),
        cost_estimate=cost(2 * whole * depth * width, 2 * whole * depth + 8 * whole * width),
    )(me, core, *feats, *pieces, *old)


def spans(mask_bits):
    masks = [0]
    for b in mask_bits:
        masks = masks + [m | b for m in masks]
    return masks


def shards(features, key_grads, error_in, selected, bin_edges, threshold, moment, second, master):
    cores, owners = lax.axis_size("tensor"), lax.axis_size("dp")
    core, me = lax.axis_index("tensor"), lax.axis_index("dp")
    tokens, rows = features.shape
    width = key_grads.shape[1]
    region = rows // owners
    bins = bin_edges.shape[0] - 1
    core1 = core.reshape(1).astype(jnp.int32)
    me1 = me.reshape(1).astype(jnp.int32)

    [held] = load([features])
    n_chunks = 4 if cores == 2 else 1
    count = rows // n_chunks
    made, got = [], []
    for s in range(1, cores):
        theirs = shift(key_grads, "tensor", s)
        for j in range(n_chunks):
            made.append(part_sum(core1, held, theirs, j * count, count))
            got.append(shift(made[-1], "tensor", -s))
    mine, _ = lax.optimization_barrier((key_grads, made[-1]))
    own = part_sum(core1, held, mine, 0, rows, error_in[0])
    later, _ = lax.optimization_barrier((features, [own] + got))
    rest, outgoing = collect(selected[0, 0], bin_edges, own, got, n_chunks, owners, bins)
    error_out = rounded(rest)[None]
    feats = [held] + [shift(later, "tensor", -s) for s in range(1, cores)]

    arrived = lax.all_to_all(
        outgoing.reshape(owners, SLOTS, width), "dp", split_axis=0, concat_axis=0, tiled=True
    )
    grad, weight = weigh(me1, threshold, bin_edges, arrived, moment, second, master)
    bits = [1 << i for i in range(owners.bit_length() - 1)]
    if 1 << len(bits) == owners and len(bits) > 2 and region % LANES == 0:
        plane, line = spans(bits[:2]), spans(bits[2:])
        near = [swap(weight, "dp", b) for b in plane[1:]]
        far = [swap(weight, "dp", m) for m in line[1:]]
        near, far = lax.optimization_barrier((near, far))
        rest = join(far)
        groups = [[weight, rest]]
        groups += [[own, swap(rest, "dp", b)] for own, b in zip(near, plane[1:])]
        feats = [held, *load(feats[1:])]
        keys = None
        for j, b in enumerate(plane):
            masks = tuple(b ^ m for m in line)
            keys = project(masks, me1, core1, feats, groups[j], keys, j == len(plane) - 1)
    else:
        whole = jnp.concatenate(feats, axis=0)
        whole = jnp.roll(whole, core * tokens, axis=0)
        keys = jnp.dot(
            whole,
            lax.all_gather(weight, "dp", axis=0, tiled=True),
            preferred_element_type=jnp.float32,
        ).astype(jnp.bfloat16)
    moment_new, second_new, master_new = state(grad, moment, second, master)
    return (keys, error_out, moment_new, second_new, master_new)


def solution(mesh):
    in_specs = (
        P(("dp", "tensor"), None),
        P("dp", "tensor"),
        P("dp", None, "tensor"),
        P("dp", "tensor", None),
        P(),
        P(),
        P("dp", "tensor"),
        P("dp", "tensor"),
        P("dp", "tensor"),
    )
    out_specs = (
        P("dp", "tensor"),
        P("dp", None, "tensor"),
        P("dp", "tensor"),
        P("dp", "tensor"),
        P("dp", "tensor"),
    )
    return jax.shard_map(shards, mesh=mesh, in_specs=in_specs, out_specs=out_specs, check_vma=False)
```

```python
import functools

import jax
import jax.numpy as jnp
from jax import lax
from jax.experimental import pallas as pl
from jax.experimental.pallas import tpu as pltpu
from jax.sharding import PartitionSpec as P

CAP = 6
SLOTS = 8
LANES = 128

beta_first = 0.9
beta_second = 0.95
learn_rate = 0.001
decay_rate = 0.1
epsilon = 1e-06
adam_epsilon = 1e-08
step_count = 10.0

VMEM = pl.BlockSpec(memory_space=pltpu.VMEM)
SMEM = pl.BlockSpec(memory_space=pltpu.SMEM)
ANY = pl.BlockSpec(memory_space=pl.ANY)


def shift(x, axis, step):
    n = lax.axis_size(axis)
    return lax.ppermute(x, axis, [(i, (i + step) % n) for i in range(n)])


def swap(x, axis, mask):
    return lax.ppermute(x, axis, [(i, i ^ mask) for i in range(lax.axis_size(axis))])


def params(*arrays):
    total = sum(a.size * jnp.dtype(a.dtype).itemsize for a in arrays)
    return pltpu.CompilerParams(vmem_limit_bytes=total + (6 << 20))


def bounds(edges):
    lane = lax.broadcasted_iota(jnp.int32, (1, LANES), 1)
    lo = hi = jnp.zeros((1, LANES), jnp.int32)
    for b in range(edges.shape[0] - 1):
        lo = jnp.where(lane == b, edges[b], lo)
        hi = jnp.where(lane == b, edges[b + 1], hi)
    return lo, hi


def cost(flops, nbytes):
    return pl.CostEstimate(flops=flops, bytes_accessed=nbytes, transcendentals=0)


def load_kernel(pieces, *refs):
    n = len(refs) // 2
    sources, targets, sem = refs[:n], refs[n : 2 * n], refs[2 * n]
    copies = []
    for i in range(n):
        rows = sources[i].shape[0] // pieces
        for j in range(pieces):
            part = pl.ds(j * rows, rows)
            copies.append(
                pltpu.make_async_copy(sources[i].at[part], targets[i].at[part], sem.at[i, j])
            )
            copies[-1].start()
    for copy in copies:
        copy.wait()


def load(arrays):
    pieces = 8
    return pl.pallas_call(
        functools.partial(load_kernel, pieces),
        in_specs=[ANY] * len(arrays),
        out_specs=[VMEM] * len(arrays),
        out_shape=[pltpu.VMEM(a.shape, a.dtype) for a in arrays],
        scratch_shapes=[pltpu.SemaphoreType.DMA((len(arrays), pieces))],
        compiler_params=params(*arrays),
        cost_estimate=cost(0, 4 * sum(a.size for a in arrays)),
    )(*[pltpu.with_memory_space_constraint(a, pltpu.HBM) for a in arrays])


def part_kernel(first, core, f_ref, g_ref, *rest):
    tokens = f_ref.shape[0]
    count = rest[-1].shape[0]
    tile = min(1024, count)
    g = g_ref[pl.ds(pl.multiple_of(core[0] * tokens, tokens), tokens), :]
    for at in range(0, count, tile):
        p = lax.dot_general(
            f_ref[:, first + at : first + at + tile],
            g,
            (((0,), (0,)), ((), ())),
            preferred_element_type=jnp.float32,
        )
        if len(rest) > 1:
            p = p + rest[0][at : at + tile, :].astype(jnp.float32)
        rest[-1][at : at + tile, :] = p


def part_sum(core, features, grads, first, count, *error):
    tokens = features.shape[0]
    width = grads.shape[1]
    part = jax.ShapeDtypeStruct((count, width), jnp.float32)
    return pl.pallas_call(
        functools.partial(part_kernel, first),
        in_specs=[SMEM, VMEM, VMEM] + [VMEM] * len(error),
        out_specs=VMEM,
        out_shape=part,
        compiler_params=params(features, grads, part, *error),
        cost_estimate=cost(2 * tokens * count * width, 2 * tokens * count + 4 * count * width),
    )(core, features, grads, *error)


def collect_kernel(n_chunks, owners, bins, sel, edges, own_ref, *refs):
    parts, (sum_ref, out_ref, count_ref) = refs[:-3], refs[-3:]
    rows, width = sum_ref.shape
    region = rows // owners
    lo, hi = bounds(edges)
    count = rows // n_chunks
    tile = min(1024, count)
    acc = jnp.zeros((8, LANES), jnp.float32)
    for first in range(0, rows, tile):
        s = own_ref[first : first + tile, :]
        for ref in parts[first // count :: n_chunks]:
            s = s + ref[first % count : first % count + tile, :]
        sum_ref[first : first + tile, :] = s
        q = jnp.sum(s * s, axis=1, keepdims=True)
        ids = first + lax.broadcasted_iota(jnp.int32, (tile, LANES), 0)
        hit = (ids >= lo) & (ids < hi)
        acc = acc + jnp.sum(jnp.where(hit, q, 0.0).reshape(tile // 8, 8, LANES), axis=0)
    energy = jnp.sum(acc, axis=0, keepdims=True)
    lane = lax.broadcasted_iota(jnp.int32, (1, LANES), 1)
    out_ref[...] = jnp.zeros_like(out_ref)
    note = jnp.where((lane >= bins) & (lane < bins + CAP), -1.0, energy)
    for o in range(owners):
        out_ref[o * SLOTS + CAP : o * SLOTS + CAP + 1, :] = note
        count_ref[o] = 0

    def take(i, carry):
        r = sel[i]
        o = lax.div(r, region)
        k = count_ref[o]
        count_ref[o] = k + 1
        out_ref[pl.ds(o * SLOTS + k, 1), :] = sum_ref[pl.ds(r, 1), :]
        sum_ref[pl.ds(r, 1), :] = jnp.zeros((1, width), jnp.float32)
        at = pl.ds(o * SLOTS + CAP, 1)
        out_ref[at, :] = jnp.where(
            lane == bins + k, (r - o * region).astype(jnp.float32), out_ref[at, :]
        )
        return carry

    lax.fori_loop(0, sel.shape[0], take, 0, unroll=8)


def collect(selected, edges, own, parts, n_chunks, owners, bins):
    rows, width = own.shape
    return pl.pallas_call(
        functools.partial(collect_kernel, n_chunks, owners, bins),
        in_specs=[SMEM, SMEM, VMEM] + [VMEM] * len(parts),
        out_specs=[VMEM, VMEM],
        out_shape=[
            jax.ShapeDtypeStruct((rows, width), jnp.float32),
            jax.ShapeDtypeStruct((owners * SLOTS, width), jnp.float32),
        ],
        scratch_shapes=[pltpu.SMEM((owners,), jnp.int32)],
        compiler_params=params(own, own, own, *parts),
        cost_estimate=cost(8 * rows * width, 4 * rows * width * 3),
    )(selected, edges, own, *parts)


def grad_kernel(bins, me, least, edges, arr_ref, m_ref, v_ref, w_ref, g_ref, b_ref):
    owners, slots, width = arr_ref.shape
    region = g_ref.shape[0]
    lo, hi = bounds(edges)
    lane = lax.broadcasted_iota(jnp.int32, (1, LANES), 1)
    arr = arr_ref[...]
    notes = arr[:, CAP : CAP + 1, :]
    energy = jnp.sum(notes, axis=0)
    widths = jnp.maximum(hi - lo, 1).astype(jnp.float32)
    normal = 1.0 / jnp.sqrt(energy / (owners * width * widths) + epsilon)
    scale = jnp.where((lane >= least[0]) & (lane < bins), normal, 1.0)
    ids = me[0] * region + lax.broadcasted_iota(jnp.int32, (region, LANES), 0)
    row_scale = jnp.sum(
        jnp.where((ids >= lo) & (ids < hi), scale, 0.0), axis=1, keepdims=True
    )
    slot = lax.broadcasted_iota(jnp.int32, (owners, slots, LANES), 1)
    lane3 = lax.broadcasted_iota(jnp.int32, (owners, slots, LANES), 2)
    offset = jnp.sum(
        jnp.where((lane3 == bins + slot) & (slot < CAP), notes, 0.0), axis=2, keepdims=True
    )
    slot1 = lax.broadcasted_iota(jnp.int32, (owners, slots, 1), 1)
    offset = jnp.where(slot1 < CAP, offset, -1.0).reshape(owners * slots, 1)
    row = lax.broadcasted_iota(jnp.int32, (owners * slots, region), 1).astype(jnp.float32)
    place = jnp.where(row == offset, 1.0, 0.0)
    grad = lax.dot_general(
        place,
        arr.reshape(owners * slots, width),
        (((0,), (0,)), ((), ())),
        precision=lax.Precision.HIGHEST,
        preferred_element_type=jnp.float32,
    )
    grad = grad * row_scale
    g_ref[...] = grad
    b_ref[...] = adam_step(m_ref[...], v_ref[...], w_ref[...], grad)[2].astype(b_ref.dtype)


def adam_step(moment, second, master, grad):
    moment_new = beta_first * moment + (1.0 - beta_first) * grad
    second_new = beta_second * second + (1.0 - beta_second) * grad * grad
    first_hat = moment_new / (1.0 - beta_first**step_count)
    second_hat = second_new / (1.0 - beta_second**step_count)
    master_new = master - learn_rate * (
        first_hat / (jnp.sqrt(second_hat) + adam_epsilon) + decay_rate * master
    )
    return moment_new, second_new, master_new


def weigh(me, least, edges, arrived, moment, second, master):
    f32 = jax.ShapeDtypeStruct(master.shape, jnp.float32)
    return pl.pallas_call(
        functools.partial(grad_kernel, edges.shape[0] - 1),
        in_specs=[SMEM] * 3 + [VMEM] * 4,
        out_specs=[VMEM] * 2,
        out_shape=[f32, jax.ShapeDtypeStruct(master.shape, jnp.bfloat16)],
        compiler_params=params(arrived, arrived, *[f32] * 5),
        cost_estimate=cost(2 * 6 * arrived.size * master.shape[0], 30 * master.size),
    )(me, least, edges, arrived, moment, second, master)


def state_kernel(g_ref, m_ref, v_ref, w_ref, *outs):
    new = adam_step(m_ref[...], v_ref[...], w_ref[...], g_ref[...])
    for out, value in zip(outs, new):
        out[...] = value


def state(grad, moment, second, master):
    return pl.pallas_call(
        state_kernel,
        in_specs=[VMEM] * 4,
        out_specs=[VMEM] * 3,
        out_shape=[jax.ShapeDtypeStruct(grad.shape, jnp.float32)] * 3,
        compiler_params=params(*[grad] * 7),
        cost_estimate=cost(20 * grad.size, 28 * grad.size),
    )(grad, moment, second, master)


def round_kernel(x_ref, o_ref):
    o_ref[...] = x_ref[...].astype(o_ref.dtype)


def rounded(x):
    out = jax.ShapeDtypeStruct(x.shape, jnp.bfloat16)
    return pl.pallas_call(
        round_kernel,
        in_specs=[VMEM],
        out_specs=VMEM,
        out_shape=out,
        compiler_params=params(x, out),
        cost_estimate=cost(x.size, 6 * x.size),
    )(x)


def join_kernel(*refs):
    for i, ref in enumerate(refs[:-1]):
        refs[-1][i] = ref[...]


def join(arrays):
    out = jax.ShapeDtypeStruct((len(arrays), *arrays[0].shape), arrays[0].dtype)
    return pl.pallas_call(
        join_kernel,
        in_specs=[VMEM] * len(arrays),
        out_specs=VMEM,
        out_shape=out,
        compiler_params=params(out, out),
        cost_estimate=cost(out.size, 4 * out.size),
    )(*arrays)


def project_kernel(masks, last, n_f, me, core, *refs):
    feats, w_ref, out_ref = refs[:n_f], refs[n_f], refs[-1]
    tokens = feats[0].shape[0]
    count, region, width = w_ref.shape
    weight = w_ref[...].reshape(count * region, width)
    for i, f_ref in enumerate(feats):
        mine = pl.ds(i * tokens, tokens)
        part = [
            f_ref[:, pl.ds(pl.multiple_of((me[0] ^ m) * region, region), region)] for m in masks
        ]
        total = jnp.dot(
            jnp.concatenate(part, axis=1), weight, preferred_element_type=jnp.float32
        )
        if len(refs) > n_f + 2:
            total = total + refs[n_f + 1][mine, :]
        if last:
            place = lax.rem(core[0] + i, n_f) * tokens
            mine = pl.ds(pl.multiple_of(place, tokens), tokens)
        out_ref[mine, :] = total.astype(out_ref.dtype)


def project(masks, me, core, feats, pieces, total, last):
    region, width = pieces.shape[1:]
    whole = len(feats) * feats[0].shape[0]
    old = [] if total is None else [total]
    out = jax.ShapeDtypeStruct((whole, width), jnp.bfloat16 if last else jnp.float32)
    depth = len(masks) * region
    return pl.pallas_call(
        functools.partial(project_kernel, masks, last, len(feats)),
        in_specs=[SMEM, SMEM] + [VMEM] * (len(feats) + 1 + len(old)),
        out_specs=VMEM,
        out_shape=out,
        compiler_params=params(pieces, out, *feats, *old),
        cost_estimate=cost(2 * whole * depth * width, 2 * whole * depth + 8 * whole * width),
    )(me, core, *feats, pieces, *old)


def spans(mask_bits):
    masks = [0]
    for b in mask_bits:
        masks = masks + [m | b for m in masks]
    return masks


def shards(features, key_grads, error_in, selected, bin_edges, threshold, moment, second, master):
    cores, owners = lax.axis_size("tensor"), lax.axis_size("dp")
    core, me = lax.axis_index("tensor"), lax.axis_index("dp")
    tokens, rows = features.shape
    width = key_grads.shape[1]
    region = rows // owners
    bins = bin_edges.shape[0] - 1
    core1 = core.reshape(1).astype(jnp.int32)
    me1 = me.reshape(1).astype(jnp.int32)

    [held] = load([features])
    n_chunks = 4 if cores == 2 else 1
    count = rows // n_chunks
    made, got = [], []
    for s in range(1, cores):
        theirs = shift(key_grads, "tensor", s)
        for j in range(n_chunks):
            made.append(part_sum(core1, held, theirs, j * count, count))
            got.append(shift(made[-1], "tensor", -s))
    mine, _ = lax.optimization_barrier((key_grads, made[-1]))
    own = part_sum(core1, held, mine, 0, rows, error_in[0])
    later, _ = lax.optimization_barrier((features, [own] + got))
    rest, outgoing = collect(selected[0, 0], bin_edges, own, got, n_chunks, owners, bins)
    error_out = rounded(rest)[None]
    feats = [held] + [shift(later, "tensor", -s) for s in range(1, cores)]

    arrived = lax.all_to_all(
        outgoing.reshape(owners, SLOTS, width), "dp", split_axis=0, concat_axis=0, tiled=True
    )
    arrived, error_out = lax.optimization_barrier((arrived, error_out))
    grad, weight = weigh(me1, threshold, bin_edges, arrived, moment, second, master)
    bits = [1 << i for i in range(owners.bit_length() - 1)]
    if 1 << len(bits) == owners and len(bits) > 2 and region % LANES == 0:
        plane, line = spans(bits[:2]), spans(bits[2:])
        far = [swap(weight, "dp", m) for m in line[1:]]
        others = load(feats[1:])
        far, others = lax.optimization_barrier((far, others))
        feats = [held, *others]
        mine = join([weight] + far)
        groups = [mine if b == 0 else swap(mine, "dp", b) for b in plane]
        keys = None
        for j, b in enumerate(plane):
            masks = tuple(b ^ m for m in line)
            keys = project(masks, me1, core1, feats, groups[j], keys, j == len(plane) - 1)
    else:
        whole = jnp.concatenate(feats, axis=0)
        whole = jnp.roll(whole, core * tokens, axis=0)
        keys = jnp.dot(
            whole,
            lax.all_gather(weight, "dp", axis=0, tiled=True),
            preferred_element_type=jnp.float32,
        ).astype(jnp.bfloat16)
    moment_new, second_new, master_new = state(grad, moment, second, master)
    return (keys, error_out, moment_new, second_new, master_new)


def solution(mesh):
    in_specs = (
        P(("dp", "tensor"), None),
        P("dp", "tensor"),
        P("dp", None, "tensor"),
        P("dp", "tensor", None),
        P(),
        P(),
        P("dp", "tensor"),
        P("dp", "tensor"),
        P("dp", "tensor"),
    )
    out_specs = (
        P("dp", "tensor"),
        P("dp", None, "tensor"),
        P("dp", "tensor"),
        P("dp", "tensor"),
        P("dp", "tensor"),
    )
    return jax.shard_map(shards, mesh=mesh, in_specs=in_specs, out_specs=out_specs, check_vma=False)
```

```python
import functools

import jax
import jax.numpy as jnp
from jax import lax
from jax.experimental import pallas as pl
from jax.experimental.pallas import tpu as pltpu
from jax.sharding import PartitionSpec as P

CAP = 6
SLOTS = 8
LANES = 128

beta_first = 0.9
beta_second = 0.95
learn_rate = 0.001
decay_rate = 0.1
epsilon = 1e-06
adam_epsilon = 1e-08
step_count = 10.0

VMEM = pl.BlockSpec(memory_space=pltpu.VMEM)
SMEM = pl.BlockSpec(memory_space=pltpu.SMEM)
ANY = pl.BlockSpec(memory_space=pl.ANY)


def shift(x, axis, step):
    n = lax.axis_size(axis)
    return lax.ppermute(x, axis, [(i, (i + step) % n) for i in range(n)])


def swap(x, axis, mask):
    return lax.ppermute(x, axis, [(i, i ^ mask) for i in range(lax.axis_size(axis))])


def params(*arrays):
    total = sum(a.size * jnp.dtype(a.dtype).itemsize for a in arrays)
    return pltpu.CompilerParams(vmem_limit_bytes=total + (6 << 20))


def bounds(edges):
    lane = lax.broadcasted_iota(jnp.int32, (1, LANES), 1)
    lo = hi = jnp.zeros((1, LANES), jnp.int32)
    for b in range(edges.shape[0] - 1):
        lo = jnp.where(lane == b, edges[b], lo)
        hi = jnp.where(lane == b, edges[b + 1], hi)
    return lo, hi


def cost(flops, nbytes):
    return pl.CostEstimate(flops=flops, bytes_accessed=nbytes, transcendentals=0)


def load_kernel(pieces, *refs):
    n = len(refs) // 2
    sources, targets, sem = refs[:n], refs[n : 2 * n], refs[2 * n]
    copies = []
    for i in range(n):
        rows = sources[i].shape[0] // pieces
        for j in range(pieces):
            part = pl.ds(j * rows, rows)
            copies.append(
                pltpu.make_async_copy(sources[i].at[part], targets[i].at[part], sem.at[i, j])
            )
            copies[-1].start()
    for copy in copies:
        copy.wait()


def load(arrays):
    pieces = 8
    return pl.pallas_call(
        functools.partial(load_kernel, pieces),
        in_specs=[ANY] * len(arrays),
        out_specs=[VMEM] * len(arrays),
        out_shape=[pltpu.VMEM(a.shape, a.dtype) for a in arrays],
        scratch_shapes=[pltpu.SemaphoreType.DMA((len(arrays), pieces))],
        compiler_params=params(*arrays),
        cost_estimate=cost(0, 4 * sum(a.size for a in arrays)),
    )(*[pltpu.with_memory_space_constraint(a, pltpu.HBM) for a in arrays])


def moves(f_any, first, next_ref, sem):
    rows = next_ref.shape[0] // sem.shape[0]
    return [
        pltpu.make_async_copy(
            f_any.at[j * rows : (j + 1) * rows, first : first + next_ref.shape[1]],
            next_ref.at[j * rows : (j + 1) * rows],
            sem.at[j],
        )
        for j in range(sem.shape[0])
    ]


def part_kernel(following, n_f, core, *refs):
    feats, refs = refs[:n_f], refs[n_f:]
    coming = []
    if following is not None:
        f_any, *refs, next_ref, sem = refs
        coming = moves(f_any, following, next_ref, sem)
        for move in coming:
            move.start()
    if n_f:
        g_ref, *error, out_ref = refs
        tokens, count = feats[0].shape
        g = g_ref[pl.ds(pl.multiple_of(core[0] * tokens, tokens), tokens), :]
        tile = min(1024, count)
        for i, f_ref in enumerate(feats):
            for at in range(0, count, tile):
                p = lax.dot_general(
                    f_ref[:, at : at + tile],
                    g,
                    (((0,), (0,)), ((), ())),
                    preferred_element_type=jnp.float32,
                )
                mine = slice(i * count + at, i * count + at + tile)
                if error:
                    p = p + error[0][mine, :].astype(jnp.float32)
                out_ref[mine, :] = p
    for move in coming:
        move.wait()


def part_sum(core, feats, grads, error, features, following, count):
    tokens = features.shape[0]
    ins, outs, scratch = list(feats), [], []
    specs = [VMEM] * len(feats)
    if following is not None:
        ins.append(pltpu.with_memory_space_constraint(features, pltpu.HBM))
        specs.append(ANY)
        scratch = [pltpu.SemaphoreType.DMA((8,))]
    width = 0
    if feats:
        width = grads.shape[1]
        ins += [grads, *error]
        specs += [VMEM] * (1 + len(error))
        outs.append(jax.ShapeDtypeStruct((len(feats) * count, width), jnp.float32))
    room = [*ins[: len(feats)], *outs, grads, *error]
    if following is not None:
        outs.append(pltpu.VMEM((tokens, count), features.dtype))
        room.append(jax.ShapeDtypeStruct((tokens, count), features.dtype))
    rows = max(1, len(feats)) * count
    return pl.pallas_call(
        functools.partial(part_kernel, following, len(feats)),
        in_specs=[SMEM] + specs,
        out_specs=[VMEM] * len(outs),
        out_shape=outs,
        scratch_shapes=scratch,
        compiler_params=params(*room),
        cost_estimate=cost(2 * tokens * rows * width, 2 * tokens * rows + 4 * rows * width),
    )(core, *ins)


def collect_kernel(n_chunks, owners, bins, sel, edges, own_ref, *refs):
    parts, (sum_ref, out_ref, count_ref) = refs[:-3], refs[-3:]
    rows, width = sum_ref.shape
    region = rows // owners
    lo, hi = bounds(edges)
    count = rows // n_chunks
    tile = min(1024, count)
    acc = jnp.zeros((8, LANES), jnp.float32)
    for first in range(0, rows, tile):
        s = own_ref[first : first + tile, :]
        for ref in parts[first // count :: n_chunks]:
            s = s + ref[first % count : first % count + tile, :]
        sum_ref[first : first + tile, :] = s
        q = jnp.sum(s * s, axis=1, keepdims=True)
        ids = first + lax.broadcasted_iota(jnp.int32, (tile, LANES), 0)
        hit = (ids >= lo) & (ids < hi)
        acc = acc + jnp.sum(jnp.where(hit, q, 0.0).reshape(tile // 8, 8, LANES), axis=0)
    energy = jnp.sum(acc, axis=0, keepdims=True)
    lane = lax.broadcasted_iota(jnp.int32, (1, LANES), 1)
    out_ref[...] = jnp.zeros_like(out_ref)
    note = jnp.where((lane >= bins) & (lane < bins + CAP), -1.0, energy)
    for o in range(owners):
        out_ref[o * SLOTS + CAP : o * SLOTS + CAP + 1, :] = note
        count_ref[o] = 0

    def take(i, carry):
        r = sel[i]
        o = lax.div(r, region)
        k = count_ref[o]
        count_ref[o] = k + 1
        out_ref[pl.ds(o * SLOTS + k, 1), :] = sum_ref[pl.ds(r, 1), :]
        sum_ref[pl.ds(r, 1), :] = jnp.zeros((1, width), jnp.float32)
        at = pl.ds(o * SLOTS + CAP, 1)
        out_ref[at, :] = jnp.where(
            lane == bins + k, (r - o * region).astype(jnp.float32), out_ref[at, :]
        )
        return carry

    lax.fori_loop(0, sel.shape[0], take, 0, unroll=8)


def collect(selected, edges, own, parts, n_chunks, owners, bins):
    rows, width = own.shape
    return pl.pallas_call(
        functools.partial(collect_kernel, n_chunks, owners, bins),
        in_specs=[SMEM, SMEM, VMEM] + [VMEM] * len(parts),
        out_specs=[VMEM, VMEM],
        out_shape=[
            jax.ShapeDtypeStruct((rows, width), jnp.float32),
            jax.ShapeDtypeStruct((owners * SLOTS, width), jnp.float32),
        ],
        scratch_shapes=[pltpu.SMEM((owners,), jnp.int32)],
        compiler_params=params(own, own, own, *parts),
        cost_estimate=cost(8 * rows * width, 4 * rows * width * 3),
    )(selected, edges, own, *parts)


def grad_kernel(bins, me, least, edges, arr_ref, m_ref, v_ref, w_ref, g_ref, b_ref):
    owners, slots, width = arr_ref.shape
    region = g_ref.shape[0]
    lo, hi = bounds(edges)
    lane = lax.broadcasted_iota(jnp.int32, (1, LANES), 1)
    arr = arr_ref[...]
    notes = arr[:, CAP : CAP + 1, :]
    energy = jnp.sum(notes, axis=0)
    widths = jnp.maximum(hi - lo, 1).astype(jnp.float32)
    normal = 1.0 / jnp.sqrt(energy / (owners * width * widths) + epsilon)
    scale = jnp.where((lane >= least[0]) & (lane < bins), normal, 1.0)
    ids = me[0] * region + lax.broadcasted_iota(jnp.int32, (region, LANES), 0)
    row_scale = jnp.sum(
        jnp.where((ids >= lo) & (ids < hi), scale, 0.0), axis=1, keepdims=True
    )
    slot = lax.broadcasted_iota(jnp.int32, (owners, slots, LANES), 1)
    lane3 = lax.broadcasted_iota(jnp.int32, (owners, slots, LANES), 2)
    offset = jnp.sum(
        jnp.where((lane3 == bins + slot) & (slot < CAP), notes, 0.0), axis=2, keepdims=True
    )
    slot1 = lax.broadcasted_iota(jnp.int32, (owners, slots, 1), 1)
    offset = jnp.where(slot1 < CAP, offset, -1.0).reshape(owners * slots, 1)
    row = lax.broadcasted_iota(jnp.int32, (owners * slots, region), 1).astype(jnp.float32)
    place = jnp.where(row == offset, 1.0, 0.0)
    grad = lax.dot_general(
        place,
        arr.reshape(owners * slots, width),
        (((0,), (0,)), ((), ())),
        precision=lax.Precision.HIGHEST,
        preferred_element_type=jnp.float32,
    )
    grad = grad * row_scale
    g_ref[...] = grad
    b_ref[...] = adam_step(m_ref[...], v_ref[...], w_ref[...], grad)[2].astype(b_ref.dtype)


def adam_step(moment, second, master, grad):
    moment_new = beta_first * moment + (1.0 - beta_first) * grad
    second_new = beta_second * second + (1.0 - beta_second) * grad * grad
    first_hat = moment_new / (1.0 - beta_first**step_count)
    second_hat = second_new / (1.0 - beta_second**step_count)
    master_new = master - learn_rate * (
        first_hat / (jnp.sqrt(second_hat) + adam_epsilon) + decay_rate * master
    )
    return moment_new, second_new, master_new


def weigh(me, least, edges, arrived, moment, second, master):
    f32 = jax.ShapeDtypeStruct(master.shape, jnp.float32)
    return pl.pallas_call(
        functools.partial(grad_kernel, edges.shape[0] - 1),
        in_specs=[SMEM] * 3 + [VMEM] * 4,
        out_specs=[VMEM] * 2,
        out_shape=[f32, jax.ShapeDtypeStruct(master.shape, jnp.bfloat16)],
        compiler_params=params(arrived, arrived, *[f32] * 5),
        cost_estimate=cost(2 * 6 * arrived.size * master.shape[0], 30 * master.size),
    )(me, least, edges, arrived, moment, second, master)


def state_kernel(g_ref, m_ref, v_ref, w_ref, *outs):
    new = adam_step(m_ref[...], v_ref[...], w_ref[...], g_ref[...])
    for out, value in zip(outs, new):
        out[...] = value


def state(grad, moment, second, master):
    return pl.pallas_call(
        state_kernel,
        in_specs=[VMEM] * 4,
        out_specs=[VMEM] * 3,
        out_shape=[jax.ShapeDtypeStruct(grad.shape, jnp.float32)] * 3,
        compiler_params=params(*[grad] * 7),
        cost_estimate=cost(20 * grad.size, 28 * grad.size),
    )(grad, moment, second, master)


def round_kernel(x_ref, o_ref):
    o_ref[...] = x_ref[...].astype(o_ref.dtype)


def rounded(x):
    out = jax.ShapeDtypeStruct(x.shape, jnp.bfloat16)
    return pl.pallas_call(
        round_kernel,
        in_specs=[VMEM],
        out_specs=VMEM,
        out_shape=out,
        compiler_params=params(x, out),
        cost_estimate=cost(x.size, 6 * x.size),
    )(x)


def join_kernel(*refs):
    for i, ref in enumerate(refs[:-1]):
        refs[-1][i] = ref[...]


def join(arrays):
    out = jax.ShapeDtypeStruct((len(arrays), *arrays[0].shape), arrays[0].dtype)
    return pl.pallas_call(
        join_kernel,
        in_specs=[VMEM] * len(arrays),
        out_specs=VMEM,
        out_shape=out,
        compiler_params=params(out, out),
        cost_estimate=cost(out.size, 4 * out.size),
    )(*arrays)


def project_kernel(masks, last, n_f, me, core, *refs):
    feats, w_ref, out_ref = refs[:n_f], refs[n_f], refs[-1]
    tokens = feats[0].shape[0]
    count, region, width = w_ref.shape
    weight = w_ref[...].reshape(count * region, width)
    for i, f_ref in enumerate(feats):
        mine = pl.ds(i * tokens, tokens)
        part = [
            f_ref[:, pl.ds(pl.multiple_of((me[0] ^ m) * region, region), region)] for m in masks
        ]
        total = jnp.dot(
            jnp.concatenate(part, axis=1), weight, preferred_element_type=jnp.float32
        )
        if len(refs) > n_f + 2:
            total = total + refs[n_f + 1][mine, :]
        if last:
            place = lax.rem(core[0] + i, n_f) * tokens
            mine = pl.ds(pl.multiple_of(place, tokens), tokens)
        out_ref[mine, :] = total.astype(out_ref.dtype)


def project(masks, me, core, feats, pieces, total, last):
    region, width = pieces.shape[1:]
    whole = len(feats) * feats[0].shape[0]
    old = [] if total is None else [total]
    out = jax.ShapeDtypeStruct((whole, width), jnp.bfloat16 if last else jnp.float32)
    depth = len(masks) * region
    return pl.pallas_call(
        functools.partial(project_kernel, masks, last, len(feats)),
        in_specs=[SMEM, SMEM] + [VMEM] * (len(feats) + 1 + len(old)),
        out_specs=VMEM,
        out_shape=out,
        compiler_params=params(pieces, out, *feats, *old),
        cost_estimate=cost(2 * whole * depth * width, 2 * whole * depth + 8 * whole * width),
    )(me, core, *feats, pieces, *old)


def spans(mask_bits):
    masks = [0]
    for b in mask_bits:
        masks = masks + [m | b for m in masks]
    return masks


def shards(features, key_grads, error_in, selected, bin_edges, threshold, moment, second, master):
    cores, owners = lax.axis_size("tensor"), lax.axis_size("dp")
    core, me = lax.axis_index("tensor"), lax.axis_index("dp")
    tokens, rows = features.shape
    width = key_grads.shape[1]
    region = rows // owners
    bins = bin_edges.shape[0] - 1
    core1 = core.reshape(1).astype(jnp.int32)
    me1 = me.reshape(1).astype(jnp.int32)

    n_chunks = 4 if cores == 2 else 1
    count = rows // n_chunks
    blocks = [*part_sum(core1, [], key_grads, [], features, 0, count)]
    made, got = [], []
    for s in range(1, cores):
        theirs = shift(key_grads, "tensor", s)
        for j in range(n_chunks):
            ahead = (j + 1) * count if len(blocks) == j + 1 < n_chunks else None
            part, *more = part_sum(core1, [blocks[j]], theirs, [], features, ahead, count)
            blocks += more
            made.append(part)
            got.append(shift(part, "tensor", -s))
    mine, _ = lax.optimization_barrier((key_grads, made[-1]))
    [own] = part_sum(core1, blocks, mine, [error_in[0]], features, None, count)
    later, _ = lax.optimization_barrier((features, [own] + got))
    rest, outgoing = collect(selected[0, 0], bin_edges, own, got, n_chunks, owners, bins)
    error_out = rounded(rest)[None]
    feats = [features] + [shift(later, "tensor", -s) for s in range(1, cores)]

    arrived = lax.all_to_all(
        outgoing.reshape(owners, SLOTS, width), "dp", split_axis=0, concat_axis=0, tiled=True
    )
    arrived, error_out = lax.optimization_barrier((arrived, error_out))
    grad, weight = weigh(me1, threshold, bin_edges, arrived, moment, second, master)
    bits = [1 << i for i in range(owners.bit_length() - 1)]
    if 1 << len(bits) == owners and len(bits) > 2 and region % LANES == 0:
        plane, line = spans(bits[:2]), spans(bits[2:])
        far = [swap(weight, "dp", m) for m in line[1:]]
        others = load(feats[1:])
        far, others = lax.optimization_barrier((far, others))
        feats = [*load(feats[:1]), *others]
        mine = join([weight] + far)
        groups = [mine if b == 0 else swap(mine, "dp", b) for b in plane]
        keys = None
        for j, b in enumerate(plane):
            masks = tuple(b ^ m for m in line)
            keys = project(masks, me1, core1, feats, groups[j], keys, j == len(plane) - 1)
    else:
        whole = jnp.concatenate(feats, axis=0)
        whole = jnp.roll(whole, core * tokens, axis=0)
        keys = jnp.dot(
            whole,
            lax.all_gather(weight, "dp", axis=0, tiled=True),
            preferred_element_type=jnp.float32,
        ).astype(jnp.bfloat16)
    moment_new, second_new, master_new = state(grad, moment, second, master)
    return (keys, error_out, moment_new, second_new, master_new)


def solution(mesh):
    in_specs = (
        P(("dp", "tensor"), None),
        P("dp", "tensor"),
        P("dp", None, "tensor"),
        P("dp", "tensor", None),
        P(),
        P(),
        P("dp", "tensor"),
        P("dp", "tensor"),
        P("dp", "tensor"),
    )
    out_specs = (
        P("dp", "tensor"),
        P("dp", None, "tensor"),
        P("dp", "tensor"),
        P("dp", "tensor"),
        P("dp", "tensor"),
    )
    return jax.shard_map(shards, mesh=mesh, in_specs=in_specs, out_specs=out_specs, check_vma=False)
```

```python
import functools

import jax
import jax.numpy as jnp
from jax import lax
from jax.experimental import pallas as pl
from jax.experimental.pallas import tpu as pltpu
from jax.sharding import PartitionSpec as P

CAP = 6
SLOTS = 8
LANES = 128

beta_first = 0.9
beta_second = 0.95
learn_rate = 0.001
decay_rate = 0.1
epsilon = 1e-06
adam_epsilon = 1e-08
step_count = 10.0

VMEM = pl.BlockSpec(memory_space=pltpu.VMEM)
SMEM = pl.BlockSpec(memory_space=pltpu.SMEM)
ANY = pl.BlockSpec(memory_space=pl.ANY)


def shift(x, axis, step):
    n = lax.axis_size(axis)
    return lax.ppermute(x, axis, [(i, (i + step) % n) for i in range(n)])


def swap(x, masks):
    n, cores = lax.axis_size("dp"), lax.axis_size("tensor")
    pairs = [
        (i * cores + c, (i ^ masks[c % len(masks)]) * cores + c)
        for i in range(n)
        for c in range(cores)
    ]
    return lax.ppermute(x, ("dp", "tensor"), pairs)


def params(*arrays):
    total = sum(a.size * jnp.dtype(a.dtype).itemsize for a in arrays)
    return pltpu.CompilerParams(vmem_limit_bytes=total + (6 << 20))


def bounds(edges):
    lane = lax.broadcasted_iota(jnp.int32, (1, LANES), 1)
    lo = hi = jnp.zeros((1, LANES), jnp.int32)
    for b in range(edges.shape[0] - 1):
        lo = jnp.where(lane == b, edges[b], lo)
        hi = jnp.where(lane == b, edges[b + 1], hi)
    return lo, hi


def cost(flops, nbytes):
    return pl.CostEstimate(flops=flops, bytes_accessed=nbytes, transcendentals=0)


def load_kernel(pieces, *refs):
    n = len(refs) // 2
    sources, targets, sem = refs[:n], refs[n : 2 * n], refs[2 * n]
    copies = []
    for i in range(n):
        rows = sources[i].shape[0] // pieces
        for j in range(pieces):
            part = pl.ds(j * rows, rows)
            copies.append(
                pltpu.make_async_copy(sources[i].at[part], targets[i].at[part], sem.at[i, j])
            )
            copies[-1].start()
    for copy in copies:
        copy.wait()


def load(arrays):
    pieces = 8
    return pl.pallas_call(
        functools.partial(load_kernel, pieces),
        in_specs=[ANY] * len(arrays),
        out_specs=[VMEM] * len(arrays),
        out_shape=[pltpu.VMEM(a.shape, a.dtype) for a in arrays],
        scratch_shapes=[pltpu.SemaphoreType.DMA((len(arrays), pieces))],
        compiler_params=params(*arrays),
        cost_estimate=cost(0, 4 * sum(a.size for a in arrays)),
    )(*[pltpu.with_memory_space_constraint(a, pltpu.HBM) for a in arrays])


def part_kernel(first, core, f_ref, g_ref, *rest):
    tokens = f_ref.shape[0]
    count = rest[-1].shape[0]
    tile = min(1024, count)
    g = g_ref[pl.ds(pl.multiple_of(core[0] * tokens, tokens), tokens), :]
    for at in range(0, count, tile):
        p = lax.dot_general(
            f_ref[:, first + at : first + at + tile],
            g,
            (((0,), (0,)), ((), ())),
            preferred_element_type=jnp.float32,
        )
        if len(rest) > 1:
            p = p + rest[0][at : at + tile, :].astype(jnp.float32)
        rest[-1][at : at + tile, :] = p


def part_sum(core, features, grads, first, count, *error):
    tokens = features.shape[0]
    width = grads.shape[1]
    part = jax.ShapeDtypeStruct((count, width), jnp.float32)
    return pl.pallas_call(
        functools.partial(part_kernel, first),
        in_specs=[SMEM, VMEM, VMEM] + [VMEM] * len(error),
        out_specs=VMEM,
        out_shape=part,
        compiler_params=params(features, grads, part, *error),
        cost_estimate=cost(2 * tokens * count * width, 2 * tokens * count + 4 * count * width),
    )(core, features, grads, *error)


def collect_kernel(n_chunks, owners, bins, sel, edges, own_ref, *refs):
    parts, (sum_ref, out_ref, count_ref) = refs[:-3], refs[-3:]
    rows, width = sum_ref.shape
    region = rows // owners
    lo, hi = bounds(edges)
    count = rows // n_chunks
    tile = min(1024, count)
    acc = jnp.zeros((8, LANES), jnp.float32)
    for first in range(0, rows, tile):
        s = own_ref[first : first + tile, :]
        for ref in parts[first // count :: n_chunks]:
            s = s + ref[first % count : first % count + tile, :]
        sum_ref[first : first + tile, :] = s
        q = jnp.sum(s * s, axis=1, keepdims=True)
        ids = first + lax.broadcasted_iota(jnp.int32, (tile, LANES), 0)
        hit = (ids >= lo) & (ids < hi)
        acc = acc + jnp.sum(jnp.where(hit, q, 0.0).reshape(tile // 8, 8, LANES), axis=0)
    energy = jnp.sum(acc, axis=0, keepdims=True)
    lane = lax.broadcasted_iota(jnp.int32, (1, LANES), 1)
    out_ref[...] = jnp.zeros_like(out_ref)
    note = jnp.where((lane >= bins) & (lane < bins + CAP), -1.0, energy)
    for o in range(owners):
        out_ref[o * SLOTS + CAP : o * SLOTS + CAP + 1, :] = note
        count_ref[o] = 0

    def take(i, carry):
        r = sel[i]
        o = lax.div(r, region)
        k = count_ref[o]
        count_ref[o] = k + 1
        out_ref[pl.ds(o * SLOTS + k, 1), :] = sum_ref[pl.ds(r, 1), :]
        sum_ref[pl.ds(r, 1), :] = jnp.zeros((1, width), jnp.float32)
        at = pl.ds(o * SLOTS + CAP, 1)
        out_ref[at, :] = jnp.where(
            lane == bins + k, (r - o * region).astype(jnp.float32), out_ref[at, :]
        )
        return carry

    lax.fori_loop(0, sel.shape[0], take, 0, unroll=8)


def collect(selected, edges, own, parts, n_chunks, owners, bins):
    rows, width = own.shape
    return pl.pallas_call(
        functools.partial(collect_kernel, n_chunks, owners, bins),
        in_specs=[SMEM, SMEM, VMEM] + [VMEM] * len(parts),
        out_specs=[VMEM, VMEM],
        out_shape=[
            jax.ShapeDtypeStruct((rows, width), jnp.float32),
            jax.ShapeDtypeStruct((owners * SLOTS, width), jnp.float32),
        ],
        scratch_shapes=[pltpu.SMEM((owners,), jnp.int32)],
        compiler_params=params(own, own, own, *parts),
        cost_estimate=cost(8 * rows * width, 4 * rows * width * 3),
    )(selected, edges, own, *parts)


def grad_kernel(bins, me, least, edges, arr_ref, m_ref, v_ref, w_ref, g_ref, b_ref):
    owners, slots, width = arr_ref.shape
    region = g_ref.shape[0]
    lo, hi = bounds(edges)
    lane = lax.broadcasted_iota(jnp.int32, (1, LANES), 1)
    arr = arr_ref[...]
    notes = arr[:, CAP : CAP + 1, :]
    energy = jnp.sum(notes, axis=0)
    widths = jnp.maximum(hi - lo, 1).astype(jnp.float32)
    normal = 1.0 / jnp.sqrt(energy / (owners * width * widths) + epsilon)
    scale = jnp.where((lane >= least[0]) & (lane < bins), normal, 1.0)
    ids = me[0] * region + lax.broadcasted_iota(jnp.int32, (region, LANES), 0)
    row_scale = jnp.sum(
        jnp.where((ids >= lo) & (ids < hi), scale, 0.0), axis=1, keepdims=True
    )
    slot = lax.broadcasted_iota(jnp.int32, (owners, slots, LANES), 1)
    lane3 = lax.broadcasted_iota(jnp.int32, (owners, slots, LANES), 2)
    offset = jnp.sum(
        jnp.where((lane3 == bins + slot) & (slot < CAP), notes, 0.0), axis=2, keepdims=True
    )
    slot1 = lax.broadcasted_iota(jnp.int32, (owners, slots, 1), 1)
    offset = jnp.where(slot1 < CAP, offset, -1.0).reshape(owners * slots, 1)
    row = lax.broadcasted_iota(jnp.int32, (owners * slots, region), 1).astype(jnp.float32)
    place = jnp.where(row == offset, 1.0, 0.0)
    grad = lax.dot_general(
        place,
        arr.reshape(owners * slots, width),
        (((0,), (0,)), ((), ())),
        precision=lax.Precision.HIGHEST,
        preferred_element_type=jnp.float32,
    )
    grad = grad * row_scale
    g_ref[...] = grad
    b_ref[...] = adam_step(m_ref[...], v_ref[...], w_ref[...], grad)[2].astype(b_ref.dtype)


def adam_step(moment, second, master, grad):
    moment_new = beta_first * moment + (1.0 - beta_first) * grad
    second_new = beta_second * second + (1.0 - beta_second) * grad * grad
    first_hat = moment_new / (1.0 - beta_first**step_count)
    second_hat = second_new / (1.0 - beta_second**step_count)
    master_new = master - learn_rate * (
        first_hat / (jnp.sqrt(second_hat) + adam_epsilon) + decay_rate * master
    )
    return moment_new, second_new, master_new


def weigh(me, least, edges, arrived, moment, second, master):
    f32 = jax.ShapeDtypeStruct(master.shape, jnp.float32)
    return pl.pallas_call(
        functools.partial(grad_kernel, edges.shape[0] - 1),
        in_specs=[SMEM] * 3 + [VMEM] * 4,
        out_specs=[VMEM] * 2,
        out_shape=[f32, jax.ShapeDtypeStruct(master.shape, jnp.bfloat16)],
        compiler_params=params(arrived, arrived, *[f32] * 5),
        cost_estimate=cost(2 * 6 * arrived.size * master.shape[0], 30 * master.size),
    )(me, least, edges, arrived, moment, second, master)


def state_kernel(g_ref, m_ref, v_ref, w_ref, *outs):
    new = adam_step(m_ref[...], v_ref[...], w_ref[...], g_ref[...])
    for out, value in zip(outs, new):
        out[...] = value


def state(grad, moment, second, master):
    return pl.pallas_call(
        state_kernel,
        in_specs=[VMEM] * 4,
        out_specs=[VMEM] * 3,
        out_shape=[jax.ShapeDtypeStruct(grad.shape, jnp.float32)] * 3,
        compiler_params=params(*[grad] * 7),
        cost_estimate=cost(20 * grad.size, 28 * grad.size),
    )(grad, moment, second, master)


def round_kernel(x_ref, o_ref):
    o_ref[...] = x_ref[...].astype(o_ref.dtype)


def rounded(x):
    out = jax.ShapeDtypeStruct(x.shape, jnp.bfloat16)
    return pl.pallas_call(
        round_kernel,
        in_specs=[VMEM],
        out_specs=VMEM,
        out_shape=out,
        compiler_params=params(x, out),
        cost_estimate=cost(x.size, 6 * x.size),
    )(x)


def join_kernel(*refs):
    for i, ref in enumerate(refs[:-1]):
        refs[-1][i] = ref[...]


def join(arrays):
    out = jax.ShapeDtypeStruct((len(arrays), *arrays[0].shape), arrays[0].dtype)
    return pl.pallas_call(
        join_kernel,
        in_specs=[VMEM] * len(arrays),
        out_specs=VMEM,
        out_shape=out,
        compiler_params=params(out, out),
        cost_estimate=cost(out.size, 4 * out.size),
    )(*arrays)


def project_kernel(masks, last, n_f, me, core, *refs):
    feats, w_ref, out_ref = refs[:n_f], refs[n_f], refs[-1]
    tokens = feats[0].shape[0]
    count, region, width = w_ref.shape
    weight = w_ref[...].reshape(count * region, width)
    odd = lax.rem(core[0], 2) == 1
    mine_of = [jnp.where(odd, m[1], m[0]) for m in masks]
    for i, f_ref in enumerate(feats):
        mine = pl.ds(i * tokens, tokens)
        part = [
            f_ref[:, pl.ds(pl.multiple_of((me[0] ^ m) * region, region), region)] for m in mine_of
        ]
        total = jnp.dot(
            jnp.concatenate(part, axis=1), weight, preferred_element_type=jnp.float32
        )
        if len(refs) > n_f + 2:
            total = total + refs[n_f + 1][mine, :]
        if last:
            place = lax.rem(core[0] + i, n_f) * tokens
            mine = pl.ds(pl.multiple_of(place, tokens), tokens)
        out_ref[mine, :] = total.astype(out_ref.dtype)


def project(masks, me, core, feats, pieces, total, last):
    region, width = pieces.shape[1:]
    whole = len(feats) * feats[0].shape[0]
    old = [] if total is None else [total]
    out = jax.ShapeDtypeStruct((whole, width), jnp.bfloat16 if last else jnp.float32)
    depth = len(masks) * region
    return pl.pallas_call(
        functools.partial(project_kernel, masks, last, len(feats)),
        in_specs=[SMEM, SMEM] + [VMEM] * (len(feats) + 1 + len(old)),
        out_specs=VMEM,
        out_shape=out,
        compiler_params=params(pieces, out, *feats, *old),
        cost_estimate=cost(2 * whole * depth * width, 2 * whole * depth + 8 * whole * width),
    )(me, core, *feats, pieces, *old)


def spans(mask_bits):
    masks = [0]
    for b in mask_bits:
        masks = masks + [m | b for m in masks]
    return masks


def shards(features, key_grads, error_in, selected, bin_edges, threshold, moment, second, master):
    cores, owners = lax.axis_size("tensor"), lax.axis_size("dp")
    core, me = lax.axis_index("tensor"), lax.axis_index("dp")
    tokens, rows = features.shape
    width = key_grads.shape[1]
    region = rows // owners
    bins = bin_edges.shape[0] - 1
    core1 = core.reshape(1).astype(jnp.int32)
    me1 = me.reshape(1).astype(jnp.int32)

    [held] = load([features])
    n_chunks = 4 if cores == 2 else 1
    count = rows // n_chunks
    made, got = [], []
    for s in range(1, cores):
        theirs = shift(key_grads, "tensor", s)
        for j in range(n_chunks):
            made.append(part_sum(core1, held, theirs, j * count, count))
            got.append(shift(made[-1], "tensor", -s))
    mine, _ = lax.optimization_barrier((key_grads, made[-1]))
    own = part_sum(core1, held, mine, 0, rows, error_in[0])
    later, _ = lax.optimization_barrier((features, [own] + got))
    rest, outgoing = collect(selected[0, 0], bin_edges, own, got, n_chunks, owners, bins)
    error_out = rounded(rest)[None]
    feats = [held] + [shift(later, "tensor", -s) for s in range(1, cores)]

    arrived = lax.all_to_all(
        outgoing.reshape(owners, SLOTS, width), "dp", split_axis=0, concat_axis=0, tiled=True
    )
    arrived, error_out = lax.optimization_barrier((arrived, error_out))
    grad, weight = weigh(me1, threshold, bin_edges, arrived, moment, second, master)
    bits = [1 << i for i in range(owners.bit_length() - 1)]
    if 1 << len(bits) == owners and len(bits) > 2 and region % LANES == 0:
        plane, line = spans(bits[:2]), spans(bits[2:])
        plane = list(zip(plane, [plane[0], plane[2], plane[1], *plane[3:]]))
        line = list(zip(line, [line[0], *line[2:], line[1]]))
        far = [swap(weight, m) for m in line[1:]]
        others = load(feats[1:])
        far, others = lax.optimization_barrier((far, others))
        feats = [held, *others]
        mine = join([weight] + far)
        groups = [mine if j == 0 else swap(mine, b) for j, b in enumerate(plane)]
        keys = None
        for j, b in enumerate(plane):
            masks = tuple((b[0] ^ m[0], b[1] ^ m[1]) for m in line)
            keys = project(masks, me1, core1, feats, groups[j], keys, j == len(plane) - 1)
    else:
        whole = jnp.concatenate(feats, axis=0)
        whole = jnp.roll(whole, core * tokens, axis=0)
        keys = jnp.dot(
            whole,
            lax.all_gather(weight, "dp", axis=0, tiled=True),
            preferred_element_type=jnp.float32,
        ).astype(jnp.bfloat16)
    moment_new, second_new, master_new = state(grad, moment, second, master)
    return (keys, error_out, moment_new, second_new, master_new)


def solution(mesh):
    in_specs = (
        P(("dp", "tensor"), None),
        P("dp", "tensor"),
        P("dp", None, "tensor"),
        P("dp", "tensor", None),
        P(),
        P(),
        P("dp", "tensor"),
        P("dp", "tensor"),
        P("dp", "tensor"),
    )
    out_specs = (
        P("dp", "tensor"),
        P("dp", None, "tensor"),
        P("dp", "tensor"),
        P("dp", "tensor"),
        P("dp", "tensor"),
    )
    return jax.shard_map(shards, mesh=mesh, in_specs=in_specs, out_specs=out_specs, check_vma=False)
```

```python
import functools

import jax
import jax.numpy as jnp
from jax import lax
from jax.experimental import pallas as pl
from jax.experimental.pallas import tpu as pltpu
from jax.sharding import PartitionSpec as P

CAP = 6
SLOTS = 8
LANES = 128

beta_first = 0.9
beta_second = 0.95
learn_rate = 0.001
decay_rate = 0.1
epsilon = 1e-06
adam_epsilon = 1e-08
step_count = 10.0

VMEM = pl.BlockSpec(memory_space=pltpu.VMEM)
SMEM = pl.BlockSpec(memory_space=pltpu.SMEM)
ANY = pl.BlockSpec(memory_space=pl.ANY)


def shift(x, axis, step):
    n = lax.axis_size(axis)
    return lax.ppermute(x, axis, [(i, (i + step) % n) for i in range(n)])


def swap(x, axis, mask):
    return lax.ppermute(x, axis, [(i, i ^ mask) for i in range(lax.axis_size(axis))])


def params(*arrays):
    total = sum(a.size * jnp.dtype(a.dtype).itemsize for a in arrays)
    return pltpu.CompilerParams(vmem_limit_bytes=total + (6 << 20))


def bounds(edges):
    lane = lax.broadcasted_iota(jnp.int32, (1, LANES), 1)
    lo = hi = jnp.zeros((1, LANES), jnp.int32)
    for b in range(edges.shape[0] - 1):
        lo = jnp.where(lane == b, edges[b], lo)
        hi = jnp.where(lane == b, edges[b + 1], hi)
    return lo, hi


def cost(flops, nbytes):
    return pl.CostEstimate(flops=flops, bytes_accessed=nbytes, transcendentals=0)


def load_kernel(pieces, *refs):
    n = len(refs) // 2
    sources, targets, sem = refs[:n], refs[n : 2 * n], refs[2 * n]
    copies = []
    for i in range(n):
        rows = sources[i].shape[0] // pieces
        for j in range(pieces):
            part = pl.ds(j * rows, rows)
            copies.append(
                pltpu.make_async_copy(sources[i].at[part], targets[i].at[part], sem.at[i, j])
            )
            copies[-1].start()
    for copy in copies:
        copy.wait()


def load(arrays):
    pieces = 8
    return pl.pallas_call(
        functools.partial(load_kernel, pieces),
        in_specs=[ANY] * len(arrays),
        out_specs=[VMEM] * len(arrays),
        out_shape=[pltpu.VMEM(a.shape, a.dtype) for a in arrays],
        scratch_shapes=[pltpu.SemaphoreType.DMA((len(arrays), pieces))],
        compiler_params=params(*arrays),
        cost_estimate=cost(0, 4 * sum(a.size for a in arrays)),
    )(*[pltpu.with_memory_space_constraint(a, pltpu.HBM) for a in arrays])


def part_kernel(first, core, f_ref, g_ref, *rest):
    tokens = f_ref.shape[0]
    count = rest[-1].shape[0]
    tile = min(1024, count)
    g = g_ref[pl.ds(pl.multiple_of(core[0] * tokens, tokens), tokens), :]
    for at in range(0, count, tile):
        p = lax.dot_general(
            f_ref[:, first + at : first + at + tile],
            g,
            (((0,), (0,)), ((), ())),
            preferred_element_type=jnp.float32,
        )
        if len(rest) > 1:
            p = p + rest[0][at : at + tile, :].astype(jnp.float32)
        rest[-1][at : at + tile, :] = p


def part_sum(core, features, grads, first, count, *error):
    tokens = features.shape[0]
    width = grads.shape[1]
    part = jax.ShapeDtypeStruct((count, width), jnp.float32)
    return pl.pallas_call(
        functools.partial(part_kernel, first),
        in_specs=[SMEM, VMEM, VMEM] + [VMEM] * len(error),
        out_specs=VMEM,
        out_shape=part,
        compiler_params=params(features, grads, part, *error),
        cost_estimate=cost(2 * tokens * count * width, 2 * tokens * count + 4 * count * width),
    )(core, features, grads, *error)


def collect_kernel(n_chunks, owners, bins, sel, edges, own_ref, *refs):
    parts, (sum_ref, out_ref, count_ref) = refs[:-3], refs[-3:]
    rows, width = sum_ref.shape
    region = rows // owners
    lo, hi = bounds(edges)
    count = rows // n_chunks
    tile = min(1024, count)
    acc = jnp.zeros((8, LANES), jnp.float32)
    for first in range(0, rows, tile):
        s = own_ref[first : first + tile, :]
        for ref in parts[first // count :: n_chunks]:
            s = s + ref[first % count : first % count + tile, :]
        sum_ref[first : first + tile, :] = s
        q = jnp.sum(s * s, axis=1, keepdims=True)
        ids = first + lax.broadcasted_iota(jnp.int32, (tile, LANES), 0)
        hit = (ids >= lo) & (ids < hi)
        acc = acc + jnp.sum(jnp.where(hit, q, 0.0).reshape(tile // 8, 8, LANES), axis=0)
    energy = jnp.sum(acc, axis=0, keepdims=True)
    lane = lax.broadcasted_iota(jnp.int32, (1, LANES), 1)
    out_ref[...] = jnp.zeros_like(out_ref)
    note = jnp.where((lane >= bins) & (lane < bins + CAP), -1.0, energy)
    for o in range(owners):
        out_ref[o * SLOTS + CAP : o * SLOTS + CAP + 1, :] = note
        count_ref[o] = 0

    def take(i, carry):
        r = sel[i]
        o = lax.div(r, region)
        k = count_ref[o]
        count_ref[o] = k + 1
        out_ref[pl.ds(o * SLOTS + k, 1), :] = sum_ref[pl.ds(r, 1), :]
        sum_ref[pl.ds(r, 1), :] = jnp.zeros((1, width), jnp.float32)
        at = pl.ds(o * SLOTS + CAP, 1)
        out_ref[at, :] = jnp.where(
            lane == bins + k, (r - o * region).astype(jnp.float32), out_ref[at, :]
        )
        return carry

    lax.fori_loop(0, sel.shape[0], take, 0, unroll=8)


def collect(selected, edges, own, parts, n_chunks, owners, bins):
    rows, width = own.shape
    return pl.pallas_call(
        functools.partial(collect_kernel, n_chunks, owners, bins),
        in_specs=[SMEM, SMEM, VMEM] + [VMEM] * len(parts),
        out_specs=[VMEM, VMEM],
        out_shape=[
            jax.ShapeDtypeStruct((rows, width), jnp.float32),
            jax.ShapeDtypeStruct((owners * SLOTS, width), jnp.float32),
        ],
        scratch_shapes=[pltpu.SMEM((owners,), jnp.int32)],
        compiler_params=params(own, own, own, *parts),
        cost_estimate=cost(8 * rows * width, 4 * rows * width * 3),
    )(selected, edges, own, *parts)


def grad_kernel(bins, me, least, edges, arr_ref, m_ref, v_ref, w_ref, g_ref, b_ref):
    owners, slots, width = arr_ref.shape
    region = g_ref.shape[0]
    lo, hi = bounds(edges)
    lane = lax.broadcasted_iota(jnp.int32, (1, LANES), 1)
    arr = arr_ref[...]
    notes = arr[:, CAP : CAP + 1, :]
    energy = jnp.sum(notes, axis=0)
    widths = jnp.maximum(hi - lo, 1).astype(jnp.float32)
    normal = 1.0 / jnp.sqrt(energy / (owners * width * widths) + epsilon)
    scale = jnp.where((lane >= least[0]) & (lane < bins), normal, 1.0)
    ids = me[0] * region + lax.broadcasted_iota(jnp.int32, (region, LANES), 0)
    row_scale = jnp.sum(
        jnp.where((ids >= lo) & (ids < hi), scale, 0.0), axis=1, keepdims=True
    )
    slot = lax.broadcasted_iota(jnp.int32, (owners, slots, LANES), 1)
    lane3 = lax.broadcasted_iota(jnp.int32, (owners, slots, LANES), 2)
    offset = jnp.sum(
        jnp.where((lane3 == bins + slot) & (slot < CAP), notes, 0.0), axis=2, keepdims=True
    )
    slot1 = lax.broadcasted_iota(jnp.int32, (owners, slots, 1), 1)
    offset = jnp.where(slot1 < CAP, offset, -1.0).reshape(owners * slots, 1)
    row = lax.broadcasted_iota(jnp.int32, (owners * slots, region), 1).astype(jnp.float32)
    place = jnp.where(row == offset, 1.0, 0.0)
    grad = lax.dot_general(
        place,
        arr.reshape(owners * slots, width),
        (((0,), (0,)), ((), ())),
        precision=lax.Precision.HIGHEST,
        preferred_element_type=jnp.float32,
    )
    grad = grad * row_scale
    g_ref[...] = grad
    b_ref[...] = adam_step(m_ref[...], v_ref[...], w_ref[...], grad)[2].astype(b_ref.dtype)


def adam_step(moment, second, master, grad):
    moment_new = beta_first * moment + (1.0 - beta_first) * grad
    second_new = beta_second * second + (1.0 - beta_second) * grad * grad
    first_hat = moment_new / (1.0 - beta_first**step_count)
    second_hat = second_new / (1.0 - beta_second**step_count)
    master_new = master - learn_rate * (
        first_hat / (jnp.sqrt(second_hat) + adam_epsilon) + decay_rate * master
    )
    return moment_new, second_new, master_new


def weigh(me, least, edges, arrived, moment, second, master):
    f32 = jax.ShapeDtypeStruct(master.shape, jnp.float32)
    return pl.pallas_call(
        functools.partial(grad_kernel, edges.shape[0] - 1),
        in_specs=[SMEM] * 3 + [VMEM] * 4,
        out_specs=[VMEM] * 2,
        out_shape=[f32, jax.ShapeDtypeStruct(master.shape, jnp.bfloat16)],
        compiler_params=params(arrived, arrived, *[f32] * 5),
        cost_estimate=cost(2 * 6 * arrived.size * master.shape[0], 30 * master.size),
    )(me, least, edges, arrived, moment, second, master)


def state_kernel(g_ref, m_ref, v_ref, w_ref, *outs):
    new = adam_step(m_ref[...], v_ref[...], w_ref[...], g_ref[...])
    for out, value in zip(outs, new):
        out[...] = value


def state(grad, moment, second, master):
    return pl.pallas_call(
        state_kernel,
        in_specs=[VMEM] * 4,
        out_specs=[VMEM] * 3,
        out_shape=[jax.ShapeDtypeStruct(grad.shape, jnp.float32)] * 3,
        compiler_params=params(*[grad] * 7),
        cost_estimate=cost(20 * grad.size, 28 * grad.size),
    )(grad, moment, second, master)


def round_kernel(x_ref, o_ref):
    o_ref[...] = x_ref[...].astype(o_ref.dtype)


def rounded(x):
    out = jax.ShapeDtypeStruct(x.shape, jnp.bfloat16)
    return pl.pallas_call(
        round_kernel,
        in_specs=[VMEM],
        out_specs=VMEM,
        out_shape=out,
        compiler_params=params(x, out),
        cost_estimate=cost(x.size, 6 * x.size),
    )(x)


def join_kernel(*refs):
    for i, ref in enumerate(refs[:-1]):
        refs[-1][i] = ref[...]


def join(arrays):
    out = jax.ShapeDtypeStruct((len(arrays), *arrays[0].shape), arrays[0].dtype)
    return pl.pallas_call(
        join_kernel,
        in_specs=[VMEM] * len(arrays),
        out_specs=VMEM,
        out_shape=out,
        compiler_params=params(out, out),
        cost_estimate=cost(out.size, 4 * out.size),
    )(*arrays)


def project_kernel(masks, last, n_f, me, core, *refs):
    feats, pieces, out_ref = refs[:n_f], refs[n_f:-1], refs[-1]
    old = [ref for ref in pieces if ref.dtype == jnp.float32]
    pieces = pieces[: len(pieces) - len(old)]
    tokens = feats[0].shape[0]
    region, width = pieces[0].shape[-2:]
    weight = jnp.concatenate([ref[...].reshape(-1, width) for ref in pieces], axis=0)
    for i, f_ref in enumerate(feats):
        mine = pl.ds(i * tokens, tokens)
        part = [
            f_ref[:, pl.ds(pl.multiple_of((me[0] ^ m) * region, region), region)] for m in masks
        ]
        total = jnp.dot(
            jnp.concatenate(part, axis=1), weight, preferred_element_type=jnp.float32
        )
        if old:
            total = total + old[0][mine, :]
        if last:
            place = lax.rem(core[0] + i, n_f) * tokens
            mine = pl.ds(pl.multiple_of(place, tokens), tokens)
        out_ref[mine, :] = total.astype(out_ref.dtype)


def project(masks, me, core, feats, pieces, total, last):
    region, width = pieces[0].shape[-2:]
    whole = len(feats) * feats[0].shape[0]
    old = [] if total is None else [total]
    out = jax.ShapeDtypeStruct((whole, width), jnp.bfloat16 if last else jnp.float32)
    depth = len(masks) * region
    return pl.pallas_call(
        functools.partial(project_kernel, masks, last, len(feats)),
        in_specs=[SMEM, SMEM] + [VMEM] * (len(feats) + len(pieces) + len(old)),
        out_specs=VMEM,
        out_shape=out,
        compiler_params=params(*pieces, out, *feats, *old),
        cost_estimate=cost(2 * whole * depth * width, 2 * whole * depth + 8 * whole * width),
    )(me, core, *feats, *pieces, *old)


def spans(mask_bits):
    masks = [0]
    for b in mask_bits:
        masks = masks + [m | b for m in masks]
    return masks


def shards(features, key_grads, error_in, selected, bin_edges, threshold, moment, second, master):
    cores, owners = lax.axis_size("tensor"), lax.axis_size("dp")
    core, me = lax.axis_index("tensor"), lax.axis_index("dp")
    tokens, rows = features.shape
    width = key_grads.shape[1]
    region = rows // owners
    bins = bin_edges.shape[0] - 1
    core1 = core.reshape(1).astype(jnp.int32)
    me1 = me.reshape(1).astype(jnp.int32)

    [held] = load([features])
    n_chunks = 4 if cores == 2 else 1
    count = rows // n_chunks
    made, got = [], []
    for s in range(1, cores):
        theirs = shift(key_grads, "tensor", s)
        for j in range(n_chunks):
            made.append(part_sum(core1, held, theirs, j * count, count))
            got.append(shift(made[-1], "tensor", -s))
    mine, _ = lax.optimization_barrier((key_grads, made[-1]))
    own = part_sum(core1, held, mine, 0, rows, error_in[0])
    later, _ = lax.optimization_barrier((features, [own] + got))
    rest, outgoing = collect(selected[0, 0], bin_edges, own, got, n_chunks, owners, bins)
    error_out = rounded(rest)[None]
    feats = [held] + [shift(later, "tensor", -s) for s in range(1, cores)]

    arrived = lax.all_to_all(
        outgoing.reshape(owners, SLOTS, width), "dp", split_axis=0, concat_axis=0, tiled=True
    )
    arrived, error_out = lax.optimization_barrier((arrived, error_out))
    grad, weight = weigh(me1, threshold, bin_edges, arrived, moment, second, master)
    bits = [1 << i for i in range(owners.bit_length() - 1)]
    if 1 << len(bits) == owners and len(bits) > 2 and region % LANES == 0:
        plane, line = spans(bits[:2]), spans(bits[2:])
        far = [swap(weight, "dp", m) for m in line[1:]]
        near = [swap(weight, "dp", b) for b in plane[1:]]
        rest = join(far)
        groups = [[weight, rest]]
        groups += [[own, swap(rest, "dp", b)] for own, b in zip(near[:-1], plane[1:-1])]
        final, near = lax.optimization_barrier((rest, near))
        groups.append([near[-1], swap(final, "dp", plane[-1])])
        feats = [held, *load(feats[1:])]
        keys = None
        for j, b in enumerate(plane):
            masks = tuple(b ^ m for m in line)
            keys = project(masks, me1, core1, feats, groups[j], keys, j == len(plane) - 1)
    else:
        whole = jnp.concatenate(feats, axis=0)
        whole = jnp.roll(whole, core * tokens, axis=0)
        keys = jnp.dot(
            whole,
            lax.all_gather(weight, "dp", axis=0, tiled=True),
            preferred_element_type=jnp.float32,
        ).astype(jnp.bfloat16)
    moment_new, second_new, master_new = state(grad, moment, second, master)
    return (keys, error_out, moment_new, second_new, master_new)


def solution(mesh):
    in_specs = (
        P(("dp", "tensor"), None),
        P("dp", "tensor"),
        P("dp", None, "tensor"),
        P("dp", "tensor", None),
        P(),
        P(),
        P("dp", "tensor"),
        P("dp", "tensor"),
        P("dp", "tensor"),
    )
    out_specs = (
        P("dp", "tensor"),
        P("dp", None, "tensor"),
        P("dp", "tensor"),
        P("dp", "tensor"),
        P("dp", "tensor"),
    )
    return jax.shard_map(shards, mesh=mesh, in_specs=in_specs, out_specs=out_specs, check_vma=False)
```

```python
import functools

import jax
import jax.numpy as jnp
from jax import lax
from jax.experimental import pallas as pl
from jax.experimental.pallas import tpu as pltpu
from jax.sharding import PartitionSpec as P

CAP = 6
SLOTS = 8
LANES = 128

beta_first = 0.9
beta_second = 0.95
learn_rate = 0.001
decay_rate = 0.1
epsilon = 1e-06
adam_epsilon = 1e-08
step_count = 10.0

VMEM = pl.BlockSpec(memory_space=pltpu.VMEM)
SMEM = pl.BlockSpec(memory_space=pltpu.SMEM)
ANY = pl.BlockSpec(memory_space=pl.ANY)


def shift(x, axis, step):
    n = lax.axis_size(axis)
    return lax.ppermute(x, axis, [(i, (i + step) % n) for i in range(n)])


def swap(x, axis, mask):
    return lax.ppermute(x, axis, [(i, i ^ mask) for i in range(lax.axis_size(axis))])


def params(*arrays):
    total = sum(a.size * jnp.dtype(a.dtype).itemsize for a in arrays)
    return pltpu.CompilerParams(vmem_limit_bytes=total + (6 << 20))


def bounds(edges):
    lane = lax.broadcasted_iota(jnp.int32, (1, LANES), 1)
    lo = hi = jnp.zeros((1, LANES), jnp.int32)
    for b in range(edges.shape[0] - 1):
        lo = jnp.where(lane == b, edges[b], lo)
        hi = jnp.where(lane == b, edges[b + 1], hi)
    return lo, hi


def cost(flops, nbytes):
    return pl.CostEstimate(flops=flops, bytes_accessed=nbytes, transcendentals=0)


def load_kernel(pieces, *refs):
    n = len(refs) // 2
    sources, targets, sem = refs[:n], refs[n : 2 * n], refs[2 * n]
    copies = []
    for i in range(n):
        rows = sources[i].shape[0] // pieces
        for j in range(pieces):
            part = pl.ds(j * rows, rows)
            copies.append(
                pltpu.make_async_copy(sources[i].at[part], targets[i].at[part], sem.at[i, j])
            )
            copies[-1].start()
    for copy in copies:
        copy.wait()


def load(arrays):
    pieces = 8
    return pl.pallas_call(
        functools.partial(load_kernel, pieces),
        in_specs=[ANY] * len(arrays),
        out_specs=[VMEM] * len(arrays),
        out_shape=[pltpu.VMEM(a.shape, a.dtype) for a in arrays],
        scratch_shapes=[pltpu.SemaphoreType.DMA((len(arrays), pieces))],
        compiler_params=params(*arrays),
        cost_estimate=cost(0, 4 * sum(a.size for a in arrays)),
    )(*[pltpu.with_memory_space_constraint(a, pltpu.HBM) for a in arrays])


def part_kernel(first, core, f_ref, g_ref, *rest):
    tokens = f_ref.shape[0]
    count = rest[-1].shape[0]
    tile = min(1024, count)
    g = g_ref[pl.ds(pl.multiple_of(core[0] * tokens, tokens), tokens), :]
    for at in range(0, count, tile):
        p = lax.dot_general(
            f_ref[:, first + at : first + at + tile],
            g,
            (((0,), (0,)), ((), ())),
            preferred_element_type=jnp.float32,
        )
        if len(rest) > 1:
            p = p + rest[0][at : at + tile, :].astype(jnp.float32)
        rest[-1][at : at + tile, :] = p


def part_sum(core, features, grads, first, count, *error):
    tokens = features.shape[0]
    width = grads.shape[1]
    part = jax.ShapeDtypeStruct((count, width), jnp.float32)
    return pl.pallas_call(
        functools.partial(part_kernel, first),
        in_specs=[SMEM, VMEM, VMEM] + [VMEM] * len(error),
        out_specs=VMEM,
        out_shape=part,
        compiler_params=params(features, grads, part, *error),
        cost_estimate=cost(2 * tokens * count * width, 2 * tokens * count + 4 * count * width),
    )(core, features, grads, *error)


def collect_kernel(n_chunks, owners, bins, sel, edges, own_ref, *refs):
    parts, (sum_ref, out_ref, count_ref) = refs[:-3], refs[-3:]
    rows, width = sum_ref.shape
    region = rows // owners
    lo, hi = bounds(edges)
    count = rows // n_chunks
    tile = min(1024, count)
    acc = jnp.zeros((8, LANES), jnp.float32)
    for first in range(0, rows, tile):
        s = own_ref[first : first + tile, :]
        for ref in parts[first // count :: n_chunks]:
            s = s + ref[first % count : first % count + tile, :]
        sum_ref[first : first + tile, :] = s
        q = jnp.sum(s * s, axis=1, keepdims=True)
        ids = first + lax.broadcasted_iota(jnp.int32, (tile, LANES), 0)
        hit = (ids >= lo) & (ids < hi)
        acc = acc + jnp.sum(jnp.where(hit, q, 0.0).reshape(tile // 8, 8, LANES), axis=0)
    energy = jnp.sum(acc, axis=0, keepdims=True)
    lane = lax.broadcasted_iota(jnp.int32, (1, LANES), 1)
    out_ref[...] = jnp.zeros_like(out_ref)
    note = jnp.where((lane >= bins) & (lane < bins + CAP), -1.0, energy)
    for o in range(owners):
        out_ref[o * SLOTS + CAP : o * SLOTS + CAP + 1, :] = note
        count_ref[o] = 0

    def take(i, carry):
        r = sel[i]
        o = lax.div(r, region)
        k = count_ref[o]
        count_ref[o] = k + 1
        out_ref[pl.ds(o * SLOTS + k, 1), :] = sum_ref[pl.ds(r, 1), :]
        sum_ref[pl.ds(r, 1), :] = jnp.zeros((1, width), jnp.float32)
        at = pl.ds(o * SLOTS + CAP, 1)
        out_ref[at, :] = jnp.where(
            lane == bins + k, (r - o * region).astype(jnp.float32), out_ref[at, :]
        )
        return carry

    lax.fori_loop(0, sel.shape[0], take, 0, unroll=8)


def collect(selected, edges, own, parts, n_chunks, owners, bins):
    rows, width = own.shape
    return pl.pallas_call(
        functools.partial(collect_kernel, n_chunks, owners, bins),
        in_specs=[SMEM, SMEM, VMEM] + [VMEM] * len(parts),
        out_specs=[VMEM, VMEM],
        out_shape=[
            jax.ShapeDtypeStruct((rows, width), jnp.float32),
            jax.ShapeDtypeStruct((owners * SLOTS, width), jnp.float32),
        ],
        scratch_shapes=[pltpu.SMEM((owners,), jnp.int32)],
        compiler_params=params(own, own, own, *parts),
        cost_estimate=cost(8 * rows * width, 4 * rows * width * 3),
    )(selected, edges, own, *parts)


def grad_kernel(bins, me, least, edges, arr_ref, m_ref, v_ref, w_ref, g_ref, b_ref):
    owners, slots, width = arr_ref.shape
    region = g_ref.shape[0]
    lo, hi = bounds(edges)
    lane = lax.broadcasted_iota(jnp.int32, (1, LANES), 1)
    arr = arr_ref[...]
    notes = arr[:, CAP : CAP + 1, :]
    energy = jnp.sum(notes, axis=0)
    widths = jnp.maximum(hi - lo, 1).astype(jnp.float32)
    normal = 1.0 / jnp.sqrt(energy / (owners * width * widths) + epsilon)
    scale = jnp.where((lane >= least[0]) & (lane < bins), normal, 1.0)
    ids = me[0] * region + lax.broadcasted_iota(jnp.int32, (region, LANES), 0)
    row_scale = jnp.sum(
        jnp.where((ids >= lo) & (ids < hi), scale, 0.0), axis=1, keepdims=True
    )
    slot = lax.broadcasted_iota(jnp.int32, (owners, slots, LANES), 1)
    lane3 = lax.broadcasted_iota(jnp.int32, (owners, slots, LANES), 2)
    offset = jnp.sum(
        jnp.where((lane3 == bins + slot) & (slot < CAP), notes, 0.0), axis=2, keepdims=True
    )
    slot1 = lax.broadcasted_iota(jnp.int32, (owners, slots, 1), 1)
    offset = jnp.where(slot1 < CAP, offset, -1.0).reshape(owners * slots, 1)
    row = lax.broadcasted_iota(jnp.int32, (owners * slots, region), 1).astype(jnp.float32)
    place = jnp.where(row == offset, 1.0, 0.0)
    grad = lax.dot_general(
        place,
        arr.reshape(owners * slots, width),
        (((0,), (0,)), ((), ())),
        precision=lax.Precision.HIGHEST,
        preferred_element_type=jnp.float32,
    )
    grad = grad * row_scale
    g_ref[...] = grad
    b_ref[...] = adam_step(m_ref[...], v_ref[...], w_ref[...], grad)[2].astype(b_ref.dtype)


def adam_step(moment, second, master, grad):
    moment_new = beta_first * moment + (1.0 - beta_first) * grad
    second_new = beta_second * second + (1.0 - beta_second) * grad * grad
    first_hat = moment_new / (1.0 - beta_first**step_count)
    second_hat = second_new / (1.0 - beta_second**step_count)
    master_new = master - learn_rate * (
        first_hat / (jnp.sqrt(second_hat) + adam_epsilon) + decay_rate * master
    )
    return moment_new, second_new, master_new


def weigh(me, least, edges, arrived, moment, second, master):
    f32 = jax.ShapeDtypeStruct(master.shape, jnp.float32)
    return pl.pallas_call(
        functools.partial(grad_kernel, edges.shape[0] - 1),
        in_specs=[SMEM] * 3 + [VMEM] * 4,
        out_specs=[VMEM] * 2,
        out_shape=[f32, jax.ShapeDtypeStruct(master.shape, jnp.bfloat16)],
        compiler_params=params(arrived, arrived, *[f32] * 5),
        cost_estimate=cost(2 * 6 * arrived.size * master.shape[0], 30 * master.size),
    )(me, least, edges, arrived, moment, second, master)


def state_kernel(g_ref, m_ref, v_ref, w_ref, *outs):
    new = adam_step(m_ref[...], v_ref[...], w_ref[...], g_ref[...])
    for out, value in zip(outs, new):
        out[...] = value


def state(grad, moment, second, master):
    return pl.pallas_call(
        state_kernel,
        in_specs=[VMEM] * 4,
        out_specs=[VMEM] * 3,
        out_shape=[jax.ShapeDtypeStruct(grad.shape, jnp.float32)] * 3,
        compiler_params=params(*[grad] * 7),
        cost_estimate=cost(20 * grad.size, 28 * grad.size),
    )(grad, moment, second, master)


def round_kernel(x_ref, o_ref):
    o_ref[...] = x_ref[...].astype(o_ref.dtype)


def rounded(x):
    out = jax.ShapeDtypeStruct(x.shape, jnp.bfloat16)
    return pl.pallas_call(
        round_kernel,
        in_specs=[VMEM],
        out_specs=VMEM,
        out_shape=out,
        compiler_params=params(x, out),
        cost_estimate=cost(x.size, 6 * x.size),
    )(x)


def join_kernel(*refs):
    for i, ref in enumerate(refs[:-1]):
        refs[-1][i] = ref[...]


def join(arrays):
    out = jax.ShapeDtypeStruct((len(arrays), *arrays[0].shape), arrays[0].dtype)
    return pl.pallas_call(
        join_kernel,
        in_specs=[VMEM] * len(arrays),
        out_specs=VMEM,
        out_shape=out,
        compiler_params=params(out, out),
        cost_estimate=cost(out.size, 4 * out.size),
    )(*arrays)


def project_kernel(masks, last, n_f, me, core, *refs):
    feats, pieces, out_ref = refs[:n_f], refs[n_f:-1], refs[-1]
    old = [ref for ref in pieces if ref.dtype == jnp.float32]
    pieces = pieces[: len(pieces) - len(old)]
    tokens = feats[0].shape[0]
    region, width = pieces[0].shape[-2:]
    weight = jnp.concatenate([ref[...].reshape(-1, width) for ref in pieces], axis=0)
    for i, f_ref in enumerate(feats):
        mine = pl.ds(i * tokens, tokens)
        part = [
            f_ref[:, pl.ds(pl.multiple_of((me[0] ^ m) * region, region), region)] for m in masks
        ]
        total = jnp.dot(
            jnp.concatenate(part, axis=1), weight, preferred_element_type=jnp.float32
        )
        if old:
            total = total + old[0][mine, :]
        if last:
            place = lax.rem(core[0] + i, n_f) * tokens
            mine = pl.ds(pl.multiple_of(place, tokens), tokens)
        out_ref[mine, :] = total.astype(out_ref.dtype)


def project(masks, me, core, feats, pieces, total, last):
    region, width = pieces[0].shape[-2:]
    whole = len(feats) * feats[0].shape[0]
    old = [] if total is None else [total]
    out = jax.ShapeDtypeStruct((whole, width), jnp.bfloat16 if last else jnp.float32)
    depth = len(masks) * region
    return pl.pallas_call(
        functools.partial(project_kernel, masks, last, len(feats)),
        in_specs=[SMEM, SMEM] + [VMEM] * (len(feats) + len(pieces) + len(old)),
        out_specs=VMEM,
        out_shape=out,
        compiler_params=params(*pieces, out, *feats, *old),
        cost_estimate=cost(2 * whole * depth * width, 2 * whole * depth + 8 * whole * width),
    )(me, core, *feats, *pieces, *old)


def spans(mask_bits):
    masks = [0]
    for b in mask_bits:
        masks = masks + [m | b for m in masks]
    return masks


def shards(features, key_grads, error_in, selected, bin_edges, threshold, moment, second, master):
    cores, owners = lax.axis_size("tensor"), lax.axis_size("dp")
    core, me = lax.axis_index("tensor"), lax.axis_index("dp")
    tokens, rows = features.shape
    width = key_grads.shape[1]
    region = rows // owners
    bins = bin_edges.shape[0] - 1
    core1 = core.reshape(1).astype(jnp.int32)
    me1 = me.reshape(1).astype(jnp.int32)

    [held] = load([features])
    n_chunks = 4 if cores == 2 else 1
    count = rows // n_chunks
    made, got = [], []
    for s in range(1, cores):
        theirs = shift(key_grads, "tensor", s)
        for j in range(n_chunks):
            made.append(part_sum(core1, held, theirs, j * count, count))
            got.append(shift(made[-1], "tensor", -s))
    mine, _ = lax.optimization_barrier((key_grads, made[-1]))
    own = part_sum(core1, held, mine, 0, rows, error_in[0])
    later, _ = lax.optimization_barrier((features, [own] + got))
    rest, outgoing = collect(selected[0, 0], bin_edges, own, got, n_chunks, owners, bins)
    error_out = rounded(rest)[None]
    feats = [held] + [shift(later, "tensor", -s) for s in range(1, cores)]

    arrived = lax.all_to_all(
        outgoing.reshape(owners, SLOTS, width), "dp", split_axis=0, concat_axis=0, tiled=True
    )
    arrived, error_out = lax.optimization_barrier((arrived, error_out))
    grad, weight = weigh(me1, threshold, bin_edges, arrived, moment, second, master)
    bits = [1 << i for i in range(owners.bit_length() - 1)]
    if 1 << len(bits) == owners and len(bits) > 2 and region % LANES == 0:
        plane, line = spans(bits[:2]), spans(bits[2:])
        far = [swap(weight, "dp", m) for m in line[1:]]
        near = [swap(weight, "dp", b) for b in plane[1:]]
        rest = join(far)
        groups = [[weight, rest]]
        groups += [[own, swap(rest, "dp", b)] for own, b in zip(near[:-1], plane[1:-1])]
        final, near, others = lax.optimization_barrier((rest, near, load(feats[1:])))
        groups.append([near[-1], swap(final, "dp", plane[-1])])
        feats = [held, *others]
        keys = None
        for j, b in enumerate(plane):
            masks = tuple(b ^ m for m in line)
            keys = project(masks, me1, core1, feats, groups[j], keys, j == len(plane) - 1)
    else:
        whole = jnp.concatenate(feats, axis=0)
        whole = jnp.roll(whole, core * tokens, axis=0)
        keys = jnp.dot(
            whole,
            lax.all_gather(weight, "dp", axis=0, tiled=True),
            preferred_element_type=jnp.float32,
        ).astype(jnp.bfloat16)
    moment_new, second_new, master_new = state(grad, moment, second, master)
    return (keys, error_out, moment_new, second_new, master_new)


def solution(mesh):
    in_specs = (
        P(("dp", "tensor"), None),
        P("dp", "tensor"),
        P("dp", None, "tensor"),
        P("dp", "tensor", None),
        P(),
        P(),
        P("dp", "tensor"),
        P("dp", "tensor"),
        P("dp", "tensor"),
    )
    out_specs = (
        P("dp", "tensor"),
        P("dp", None, "tensor"),
        P("dp", "tensor"),
        P("dp", "tensor"),
        P("dp", "tensor"),
    )
    return jax.shard_map(shards, mesh=mesh, in_specs=in_specs, out_specs=out_specs, check_vma=False)
```

```python
import functools

import jax
import jax.numpy as jnp
from jax import lax
from jax.experimental import pallas as pl
from jax.experimental.pallas import tpu as pltpu
from jax.sharding import PartitionSpec as P

CAP = 6
SLOTS = 8
LANES = 128

beta_first = 0.9
beta_second = 0.95
learn_rate = 0.001
decay_rate = 0.1
epsilon = 1e-06
adam_epsilon = 1e-08
step_count = 10.0

VMEM = pl.BlockSpec(memory_space=pltpu.VMEM)
SMEM = pl.BlockSpec(memory_space=pltpu.SMEM)
ANY = pl.BlockSpec(memory_space=pl.ANY)


def shift(x, axis, step):
    n = lax.axis_size(axis)
    return lax.ppermute(x, axis, [(i, (i + step) % n) for i in range(n)])


def swap(x, axis, mask):
    return lax.ppermute(x, axis, [(i, i ^ mask) for i in range(lax.axis_size(axis))])


def params(*arrays):
    total = sum(a.size * jnp.dtype(a.dtype).itemsize for a in arrays)
    return pltpu.CompilerParams(vmem_limit_bytes=total + (6 << 20))


def bounds(edges):
    lane = lax.broadcasted_iota(jnp.int32, (1, LANES), 1)
    lo = hi = jnp.zeros((1, LANES), jnp.int32)
    for b in range(edges.shape[0] - 1):
        lo = jnp.where(lane == b, edges[b], lo)
        hi = jnp.where(lane == b, edges[b + 1], hi)
    return lo, hi


def cost(flops, nbytes):
    return pl.CostEstimate(flops=flops, bytes_accessed=nbytes, transcendentals=0)


def load_kernel(pieces, *refs):
    n = len(refs) // 2
    sources, targets, sem = refs[:n], refs[n : 2 * n], refs[2 * n]
    copies = []
    for i in range(n):
        rows = sources[i].shape[0] // pieces
        for j in range(pieces):
            part = pl.ds(j * rows, rows)
            copies.append(
                pltpu.make_async_copy(sources[i].at[part], targets[i].at[part], sem.at[i, j])
            )
            copies[-1].start()
    for copy in copies:
        copy.wait()


def load(arrays):
    pieces = 8
    return pl.pallas_call(
        functools.partial(load_kernel, pieces),
        in_specs=[ANY] * len(arrays),
        out_specs=[VMEM] * len(arrays),
        out_shape=[pltpu.VMEM(a.shape, a.dtype) for a in arrays],
        scratch_shapes=[pltpu.SemaphoreType.DMA((len(arrays), pieces))],
        compiler_params=params(*arrays),
        cost_estimate=cost(0, 4 * sum(a.size for a in arrays)),
    )(*[pltpu.with_memory_space_constraint(a, pltpu.HBM) for a in arrays])


def part_kernel(first, core, f_ref, g_ref, *rest):
    tokens = f_ref.shape[0]
    count = rest[-1].shape[0]
    tile = min(1024, count)
    g = g_ref[pl.ds(pl.multiple_of(core[0] * tokens, tokens), tokens), :]
    for at in range(0, count, tile):
        p = lax.dot_general(
            f_ref[:, first + at : first + at + tile],
            g,
            (((0,), (0,)), ((), ())),
            preferred_element_type=jnp.float32,
        )
        if len(rest) > 1:
            p = p + rest[0][at : at + tile, :].astype(jnp.float32)
        rest[-1][at : at + tile, :] = p


def part_sum(core, features, grads, first, count, *error):
    tokens = features.shape[0]
    width = grads.shape[1]
    part = jax.ShapeDtypeStruct((count, width), jnp.float32)
    return pl.pallas_call(
        functools.partial(part_kernel, first),
        in_specs=[SMEM, VMEM, VMEM] + [VMEM] * len(error),
        out_specs=VMEM,
        out_shape=part,
        compiler_params=params(features, grads, part, *error),
        cost_estimate=cost(2 * tokens * count * width, 2 * tokens * count + 4 * count * width),
    )(core, features, grads, *error)


def collect_kernel(n_chunks, owners, bins, sel, edges, own_ref, *refs):
    parts, (sum_ref, out_ref, count_ref) = refs[:-3], refs[-3:]
    rows, width = sum_ref.shape
    region = rows // owners
    lo, hi = bounds(edges)
    count = rows // n_chunks
    tile = min(1024, count)
    acc = jnp.zeros((8, LANES), jnp.float32)
    for first in range(0, rows, tile):
        s = own_ref[first : first + tile, :]
        for ref in parts[first // count :: n_chunks]:
            s = s + ref[first % count : first % count + tile, :]
        sum_ref[first : first + tile, :] = s
        q = jnp.sum(s * s, axis=1, keepdims=True)
        ids = first + lax.broadcasted_iota(jnp.int32, (tile, LANES), 0)
        hit = (ids >= lo) & (ids < hi)
        acc = acc + jnp.sum(jnp.where(hit, q, 0.0).reshape(tile // 8, 8, LANES), axis=0)
    energy = jnp.sum(acc, axis=0, keepdims=True)
    lane = lax.broadcasted_iota(jnp.int32, (1, LANES), 1)
    out_ref[...] = jnp.zeros_like(out_ref)
    note = jnp.where((lane >= bins) & (lane < bins + CAP), -1.0, energy)
    for o in range(owners):
        out_ref[o * SLOTS + CAP : o * SLOTS + CAP + 1, :] = note
        count_ref[o] = 0

    def take(i, carry):
        r = sel[i]
        o = lax.div(r, region)
        k = count_ref[o]
        count_ref[o] = k + 1
        out_ref[pl.ds(o * SLOTS + k, 1), :] = sum_ref[pl.ds(r, 1), :]
        sum_ref[pl.ds(r, 1), :] = jnp.zeros((1, width), jnp.float32)
        at = pl.ds(o * SLOTS + CAP, 1)
        out_ref[at, :] = jnp.where(
            lane == bins + k, (r - o * region).astype(jnp.float32), out_ref[at, :]
        )
        return carry

    lax.fori_loop(0, sel.shape[0], take, 0, unroll=8)


def collect(selected, edges, own, parts, n_chunks, owners, bins):
    rows, width = own.shape
    return pl.pallas_call(
        functools.partial(collect_kernel, n_chunks, owners, bins),
        in_specs=[SMEM, SMEM, VMEM] + [VMEM] * len(parts),
        out_specs=[VMEM, VMEM],
        out_shape=[
            jax.ShapeDtypeStruct((rows, width), jnp.float32),
            jax.ShapeDtypeStruct((owners * SLOTS, width), jnp.float32),
        ],
        scratch_shapes=[pltpu.SMEM((owners,), jnp.int32)],
        compiler_params=params(own, own, own, *parts),
        cost_estimate=cost(8 * rows * width, 4 * rows * width * 3),
    )(selected, edges, own, *parts)


def grad_kernel(bins, me, least, edges, arr_ref, m_ref, v_ref, w_ref, g_ref, b_ref):
    owners, slots, width = arr_ref.shape
    region = g_ref.shape[0]
    lo, hi = bounds(edges)
    lane = lax.broadcasted_iota(jnp.int32, (1, LANES), 1)
    arr = arr_ref[...]
    notes = arr[:, CAP : CAP + 1, :]
    energy = jnp.sum(notes, axis=0)
    widths = jnp.maximum(hi - lo, 1).astype(jnp.float32)
    normal = 1.0 / jnp.sqrt(energy / (owners * width * widths) + epsilon)
    scale = jnp.where((lane >= least[0]) & (lane < bins), normal, 1.0)
    ids = me[0] * region + lax.broadcasted_iota(jnp.int32, (region, LANES), 0)
    row_scale = jnp.sum(
        jnp.where((ids >= lo) & (ids < hi), scale, 0.0), axis=1, keepdims=True
    )
    slot = lax.broadcasted_iota(jnp.int32, (owners, slots, LANES), 1)
    lane3 = lax.broadcasted_iota(jnp.int32, (owners, slots, LANES), 2)
    offset = jnp.sum(
        jnp.where((lane3 == bins + slot) & (slot < CAP), notes, 0.0), axis=2, keepdims=True
    )
    slot1 = lax.broadcasted_iota(jnp.int32, (owners, slots, 1), 1)
    offset = jnp.where(slot1 < CAP, offset, -1.0).reshape(owners * slots, 1)
    row = lax.broadcasted_iota(jnp.int32, (owners * slots, region), 1).astype(jnp.float32)
    place = jnp.where(row == offset, 1.0, 0.0)
    grad = lax.dot_general(
        place,
        arr.reshape(owners * slots, width),
        (((0,), (0,)), ((), ())),
        precision=lax.Precision.HIGHEST,
        preferred_element_type=jnp.float32,
    )
    grad = grad * row_scale
    g_ref[...] = grad
    b_ref[...] = adam_step(m_ref[...], v_ref[...], w_ref[...], grad)[2].astype(b_ref.dtype)


def adam_step(moment, second, master, grad):
    moment_new = beta_first * moment + (1.0 - beta_first) * grad
    second_new = beta_second * second + (1.0 - beta_second) * grad * grad
    first_hat = moment_new / (1.0 - beta_first**step_count)
    second_hat = second_new / (1.0 - beta_second**step_count)
    master_new = master - learn_rate * (
        first_hat / (jnp.sqrt(second_hat) + adam_epsilon) + decay_rate * master
    )
    return moment_new, second_new, master_new


def weigh(me, least, edges, arrived, moment, second, master):
    f32 = jax.ShapeDtypeStruct(master.shape, jnp.float32)
    return pl.pallas_call(
        functools.partial(grad_kernel, edges.shape[0] - 1),
        in_specs=[SMEM] * 3 + [VMEM] * 4,
        out_specs=[VMEM] * 2,
        out_shape=[f32, jax.ShapeDtypeStruct(master.shape, jnp.bfloat16)],
        compiler_params=params(arrived, arrived, *[f32] * 5),
        cost_estimate=cost(2 * 6 * arrived.size * master.shape[0], 30 * master.size),
    )(me, least, edges, arrived, moment, second, master)


def state_kernel(g_ref, m_ref, v_ref, w_ref, *outs):
    new = adam_step(m_ref[...], v_ref[...], w_ref[...], g_ref[...])
    for out, value in zip(outs, new):
        out[...] = value


def state(grad, moment, second, master):
    return pl.pallas_call(
        state_kernel,
        in_specs=[VMEM] * 4,
        out_specs=[VMEM] * 3,
        out_shape=[jax.ShapeDtypeStruct(grad.shape, jnp.float32)] * 3,
        compiler_params=params(*[grad] * 7),
        cost_estimate=cost(20 * grad.size, 28 * grad.size),
    )(grad, moment, second, master)


def round_kernel(x_ref, o_ref):
    o_ref[...] = x_ref[...].astype(o_ref.dtype)


def rounded(x):
    out = jax.ShapeDtypeStruct(x.shape, jnp.bfloat16)
    return pl.pallas_call(
        round_kernel,
        in_specs=[VMEM],
        out_specs=VMEM,
        out_shape=out,
        compiler_params=params(x, out),
        cost_estimate=cost(x.size, 6 * x.size),
    )(x)


def join_kernel(*refs):
    for i, ref in enumerate(refs[:-1]):
        refs[-1][i] = ref[...]


def join(arrays):
    out = jax.ShapeDtypeStruct((len(arrays), *arrays[0].shape), arrays[0].dtype)
    return pl.pallas_call(
        join_kernel,
        in_specs=[VMEM] * len(arrays),
        out_specs=VMEM,
        out_shape=out,
        compiler_params=params(out, out),
        cost_estimate=cost(out.size, 4 * out.size),
    )(*arrays)


def project_kernel(masks, last, n_f, me, core, *refs):
    feats, pieces, out_ref = refs[:n_f], refs[n_f:-1], refs[-1]
    old = [ref for ref in pieces if ref.dtype == jnp.float32]
    pieces = pieces[: len(pieces) - len(old)]
    tokens = feats[0].shape[0]
    region, width = pieces[0].shape[-2:]
    weight = jnp.concatenate([ref[...].reshape(-1, width) for ref in pieces], axis=0)
    for i, f_ref in enumerate(feats):
        mine = pl.ds(i * tokens, tokens)
        part = [
            f_ref[:, pl.ds(pl.multiple_of((me[0] ^ m) * region, region), region)] for m in masks
        ]
        total = jnp.dot(
            jnp.concatenate(part, axis=1), weight, preferred_element_type=jnp.float32
        )
        if old:
            total = total + old[0][mine, :]
        if last:
            place = lax.rem(core[0] + i, n_f) * tokens
            mine = pl.ds(pl.multiple_of(place, tokens), tokens)
        out_ref[mine, :] = total.astype(out_ref.dtype)


def project(masks, me, core, feats, pieces, total, last):
    region, width = pieces[0].shape[-2:]
    whole = len(feats) * feats[0].shape[0]
    old = [] if total is None else [total]
    out = jax.ShapeDtypeStruct((whole, width), jnp.bfloat16 if last else jnp.float32)
    depth = len(masks) * region
    return pl.pallas_call(
        functools.partial(project_kernel, masks, last, len(feats)),
        in_specs=[SMEM, SMEM] + [VMEM] * (len(feats) + len(pieces) + len(old)),
        out_specs=VMEM,
        out_shape=out,
        compiler_params=params(*pieces, out, *feats, *old),
        cost_estimate=cost(2 * whole * depth * width, 2 * whole * depth + 8 * whole * width),
    )(me, core, *feats, *pieces, *old)


def spans(mask_bits):
    masks = [0]
    for b in mask_bits:
        masks = masks + [m | b for m in masks]
    return masks


def shards(features, key_grads, error_in, selected, bin_edges, threshold, moment, second, master):
    cores, owners = lax.axis_size("tensor"), lax.axis_size("dp")
    core, me = lax.axis_index("tensor"), lax.axis_index("dp")
    tokens, rows = features.shape
    width = key_grads.shape[1]
    region = rows // owners
    bins = bin_edges.shape[0] - 1
    core1 = core.reshape(1).astype(jnp.int32)
    me1 = me.reshape(1).astype(jnp.int32)

    [held] = load([features])
    n_chunks = 4 if cores == 2 else 1
    count = rows // n_chunks
    made, got = [], []
    for s in range(1, cores):
        theirs = shift(key_grads, "tensor", s)
        for j in range(n_chunks):
            made.append(part_sum(core1, held, theirs, j * count, count))
            got.append(shift(made[-1], "tensor", -s))
    mine, _ = lax.optimization_barrier((key_grads, made[-1]))
    own = part_sum(core1, held, mine, 0, rows, error_in[0])
    later, _ = lax.optimization_barrier((features, [own] + got))
    rest, outgoing = collect(selected[0, 0], bin_edges, own, got, n_chunks, owners, bins)
    error_out = rounded(rest)[None]
    feats = [held] + [shift(later, "tensor", -s) for s in range(1, cores)]

    arrived = lax.all_to_all(
        outgoing.reshape(owners, SLOTS, width), "dp", split_axis=0, concat_axis=0, tiled=True
    )
    arrived, error_out = lax.optimization_barrier((arrived, error_out))
    grad, weight = weigh(me1, threshold, bin_edges, arrived, moment, second, master)
    states = state(grad, moment, second, master)

    bits = [1 << i for i in range(owners.bit_length() - 1)]
    if 1 << len(bits) == owners and len(bits) > 2 and region % LANES == 0:
        plane, line = spans(bits[:2]), spans(bits[2:])
        far = [swap(weight, "dp", m) for m in line[1:]]
        near = [swap(weight, "dp", b) for b in plane[1:]]
        rest = join(far)
        groups = [[weight, rest]]
        groups += [[own, swap(rest, "dp", b)] for own, b in zip(near[:-1], plane[1:-1])]
        final, near, states = lax.optimization_barrier((rest, near, states))
        others = load(feats[1:])
        groups.append([near[-1], swap(final, "dp", plane[-1])])
        feats = [held, *others]
        keys = None
        for j, b in enumerate(plane):
            masks = tuple(b ^ m for m in line)
            keys = project(masks, me1, core1, feats, groups[j], keys, j == len(plane) - 1)
    else:
        whole = jnp.concatenate(feats, axis=0)
        whole = jnp.roll(whole, core * tokens, axis=0)
        keys = jnp.dot(
            whole,
            lax.all_gather(weight, "dp", axis=0, tiled=True),
            preferred_element_type=jnp.float32,
        ).astype(jnp.bfloat16)
    moment_new, second_new, master_new = states
    return (keys, error_out, moment_new, second_new, master_new)


def solution(mesh):
    in_specs = (
        P(("dp", "tensor"), None),
        P("dp", "tensor"),
        P("dp", None, "tensor"),
        P("dp", "tensor", None),
        P(),
        P(),
        P("dp", "tensor"),
        P("dp", "tensor"),
        P("dp", "tensor"),
    )
    out_specs = (
        P("dp", "tensor"),
        P("dp", None, "tensor"),
        P("dp", "tensor"),
        P("dp", "tensor"),
        P("dp", "tensor"),
    )
    return jax.shard_map(shards, mesh=mesh, in_specs=in_specs, out_specs=out_specs, check_vma=False)
```

```python
import functools

import jax
import jax.numpy as jnp
from jax import lax
from jax.experimental import pallas as pl
from jax.experimental.pallas import tpu as pltpu
from jax.sharding import PartitionSpec as P

CAP = 6
SLOTS = 8
LANES = 128

beta_first = 0.9
beta_second = 0.95
learn_rate = 0.001
decay_rate = 0.1
epsilon = 1e-06
adam_epsilon = 1e-08
step_count = 10.0

VMEM = pl.BlockSpec(memory_space=pltpu.VMEM)
SMEM = pl.BlockSpec(memory_space=pltpu.SMEM)
ANY = pl.BlockSpec(memory_space=pl.ANY)


def shift(x, axis, step):
    n = lax.axis_size(axis)
    return lax.ppermute(x, axis, [(i, (i + step) % n) for i in range(n)])


def swap(x, axis, mask):
    return lax.ppermute(x, axis, [(i, i ^ mask) for i in range(lax.axis_size(axis))])


def params(*arrays):
    total = sum(a.size * jnp.dtype(a.dtype).itemsize for a in arrays)
    return pltpu.CompilerParams(vmem_limit_bytes=total + (6 << 20))


def bounds(edges):
    lane = lax.broadcasted_iota(jnp.int32, (1, LANES), 1)
    lo = hi = jnp.zeros((1, LANES), jnp.int32)
    for b in range(edges.shape[0] - 1):
        lo = jnp.where(lane == b, edges[b], lo)
        hi = jnp.where(lane == b, edges[b + 1], hi)
    return lo, hi


def cost(flops, nbytes):
    return pl.CostEstimate(flops=flops, bytes_accessed=nbytes, transcendentals=0)


def load_kernel(pieces, *refs):
    n = len(refs) // 2
    sources, targets, sem = refs[:n], refs[n : 2 * n], refs[2 * n]
    copies = []
    for i in range(n):
        rows = sources[i].shape[0] // pieces
        for j in range(pieces):
            part = pl.ds(j * rows, rows)
            copies.append(
                pltpu.make_async_copy(sources[i].at[part], targets[i].at[part], sem.at[i, j])
            )
            copies[-1].start()
    for copy in copies:
        copy.wait()


def load(arrays):
    pieces = 8
    return pl.pallas_call(
        functools.partial(load_kernel, pieces),
        in_specs=[ANY] * len(arrays),
        out_specs=[VMEM] * len(arrays),
        out_shape=[pltpu.VMEM(a.shape, a.dtype) for a in arrays],
        scratch_shapes=[pltpu.SemaphoreType.DMA((len(arrays), pieces))],
        compiler_params=params(*arrays),
        cost_estimate=cost(0, 4 * sum(a.size for a in arrays)),
    )(*[pltpu.with_memory_space_constraint(a, pltpu.HBM) for a in arrays])


def part_kernel(first, core, f_ref, g_ref, *rest):
    tokens = f_ref.shape[0]
    count = rest[-1].shape[0]
    tile = min(1024, count)
    g = g_ref[pl.ds(pl.multiple_of(core[0] * tokens, tokens), tokens), :]
    for at in range(0, count, tile):
        p = lax.dot_general(
            f_ref[:, first + at : first + at + tile],
            g,
            (((0,), (0,)), ((), ())),
            preferred_element_type=jnp.float32,
        )
        if len(rest) > 1:
            p = p + rest[0][at : at + tile, :].astype(jnp.float32)
        rest[-1][at : at + tile, :] = p


def part_sum(core, features, grads, first, count, *error):
    tokens = features.shape[0]
    width = grads.shape[1]
    part = jax.ShapeDtypeStruct((count, width), jnp.float32)
    return pl.pallas_call(
        functools.partial(part_kernel, first),
        in_specs=[SMEM, VMEM, VMEM] + [VMEM] * len(error),
        out_specs=VMEM,
        out_shape=part,
        compiler_params=params(features, grads, part, *error),
        cost_estimate=cost(2 * tokens * count * width, 2 * tokens * count + 4 * count * width),
    )(core, features, grads, *error)


def collect_kernel(n_chunks, owners, bins, sel, edges, own_ref, *refs):
    parts, (sum_ref, out_ref, count_ref) = refs[:-3], refs[-3:]
    rows, width = sum_ref.shape
    region = rows // owners
    lo, hi = bounds(edges)
    count = rows // n_chunks
    tile = min(1024, count)
    acc = jnp.zeros((8, LANES), jnp.float32)
    for first in range(0, rows, tile):
        s = own_ref[first : first + tile, :]
        for ref in parts[first // count :: n_chunks]:
            s = s + ref[first % count : first % count + tile, :]
        sum_ref[first : first + tile, :] = s
        q = jnp.sum(s * s, axis=1, keepdims=True)
        ids = first + lax.broadcasted_iota(jnp.int32, (tile, LANES), 0)
        hit = (ids >= lo) & (ids < hi)
        acc = acc + jnp.sum(jnp.where(hit, q, 0.0).reshape(tile // 8, 8, LANES), axis=0)
    energy = jnp.sum(acc, axis=0, keepdims=True)
    lane = lax.broadcasted_iota(jnp.int32, (1, LANES), 1)
    out_ref[...] = jnp.zeros_like(out_ref)
    note = jnp.where((lane >= bins) & (lane < bins + CAP), -1.0, energy)
    for o in range(owners):
        out_ref[o * SLOTS + CAP : o * SLOTS + CAP + 1, :] = note
        count_ref[o] = 0

    def take(i, carry):
        r = sel[i]
        o = lax.div(r, region)
        k = count_ref[o]
        count_ref[o] = k + 1
        out_ref[pl.ds(o * SLOTS + k, 1), :] = sum_ref[pl.ds(r, 1), :]
        sum_ref[pl.ds(r, 1), :] = jnp.zeros((1, width), jnp.float32)
        at = pl.ds(o * SLOTS + CAP, 1)
        out_ref[at, :] = jnp.where(
            lane == bins + k, (r - o * region).astype(jnp.float32), out_ref[at, :]
        )
        return carry

    lax.fori_loop(0, sel.shape[0], take, 0, unroll=8)


def collect(selected, edges, own, parts, n_chunks, owners, bins):
    rows, width = own.shape
    return pl.pallas_call(
        functools.partial(collect_kernel, n_chunks, owners, bins),
        in_specs=[SMEM, SMEM, VMEM] + [VMEM] * len(parts),
        out_specs=[VMEM, VMEM],
        out_shape=[
            jax.ShapeDtypeStruct((rows, width), jnp.float32),
            jax.ShapeDtypeStruct((owners * SLOTS, width), jnp.float32),
        ],
        scratch_shapes=[pltpu.SMEM((owners,), jnp.int32)],
        compiler_params=params(own, own, own, *parts),
        cost_estimate=cost(8 * rows * width, 4 * rows * width * 3),
    )(selected, edges, own, *parts)


def grad_kernel(bins, me, least, edges, arr_ref, m_ref, v_ref, w_ref, g_ref, b_ref):
    owners, slots, width = arr_ref.shape
    region = g_ref.shape[0]
    lo, hi = bounds(edges)
    lane = lax.broadcasted_iota(jnp.int32, (1, LANES), 1)
    arr = arr_ref[...]
    notes = arr[:, CAP : CAP + 1, :]
    energy = jnp.sum(notes, axis=0)
    widths = jnp.maximum(hi - lo, 1).astype(jnp.float32)
    normal = 1.0 / jnp.sqrt(energy / (owners * width * widths) + epsilon)
    scale = jnp.where((lane >= least[0]) & (lane < bins), normal, 1.0)
    ids = me[0] * region + lax.broadcasted_iota(jnp.int32, (region, LANES), 0)
    row_scale = jnp.sum(
        jnp.where((ids >= lo) & (ids < hi), scale, 0.0), axis=1, keepdims=True
    )
    slot = lax.broadcasted_iota(jnp.int32, (owners, slots, LANES), 1)
    lane3 = lax.broadcasted_iota(jnp.int32, (owners, slots, LANES), 2)
    offset = jnp.sum(
        jnp.where((lane3 == bins + slot) & (slot < CAP), notes, 0.0), axis=2, keepdims=True
    )
    slot1 = lax.broadcasted_iota(jnp.int32, (owners, slots, 1), 1)
    offset = jnp.where(slot1 < CAP, offset, -1.0).reshape(owners * slots, 1)
    row = lax.broadcasted_iota(jnp.int32, (owners * slots, region), 1).astype(jnp.float32)
    place = jnp.where(row == offset, 1.0, 0.0)
    grad = lax.dot_general(
        place,
        arr.reshape(owners * slots, width),
        (((0,), (0,)), ((), ())),
        precision=lax.Precision.HIGHEST,
        preferred_element_type=jnp.float32,
    )
    grad = grad * row_scale
    g_ref[...] = grad
    b_ref[...] = adam_step(m_ref[...], v_ref[...], w_ref[...], grad)[2].astype(b_ref.dtype)


def adam_step(moment, second, master, grad):
    moment_new = beta_first * moment + (1.0 - beta_first) * grad
    second_new = beta_second * second + (1.0 - beta_second) * grad * grad
    first_hat = moment_new / (1.0 - beta_first**step_count)
    second_hat = second_new / (1.0 - beta_second**step_count)
    master_new = master - learn_rate * (
        first_hat / (jnp.sqrt(second_hat) + adam_epsilon) + decay_rate * master
    )
    return moment_new, second_new, master_new


def weigh(me, least, edges, arrived, moment, second, master):
    f32 = jax.ShapeDtypeStruct(master.shape, jnp.float32)
    return pl.pallas_call(
        functools.partial(grad_kernel, edges.shape[0] - 1),
        in_specs=[SMEM] * 3 + [VMEM] * 4,
        out_specs=[VMEM] * 2,
        out_shape=[f32, jax.ShapeDtypeStruct(master.shape, jnp.bfloat16)],
        compiler_params=params(arrived, arrived, *[f32] * 5),
        cost_estimate=cost(2 * 6 * arrived.size * master.shape[0], 30 * master.size),
    )(me, least, edges, arrived, moment, second, master)


def state_kernel(g_ref, m_ref, v_ref, w_ref, *outs):
    new = adam_step(m_ref[...], v_ref[...], w_ref[...], g_ref[...])
    for out, value in zip(outs, new):
        out[...] = value


def state(grad, moment, second, master):
    return pl.pallas_call(
        state_kernel,
        in_specs=[VMEM] * 4,
        out_specs=[VMEM] * 3,
        out_shape=[jax.ShapeDtypeStruct(grad.shape, jnp.float32)] * 3,
        compiler_params=params(*[grad] * 7),
        cost_estimate=cost(20 * grad.size, 28 * grad.size),
    )(grad, moment, second, master)


def round_kernel(x_ref, o_ref):
    o_ref[...] = x_ref[...].astype(o_ref.dtype)


def rounded(x):
    out = jax.ShapeDtypeStruct(x.shape, jnp.bfloat16)
    return pl.pallas_call(
        round_kernel,
        in_specs=[VMEM],
        out_specs=VMEM,
        out_shape=out,
        compiler_params=params(x, out),
        cost_estimate=cost(x.size, 6 * x.size),
    )(x)


def join_kernel(*refs):
    for i, ref in enumerate(refs[:-1]):
        refs[-1][i] = ref[...]


def join(arrays):
    out = jax.ShapeDtypeStruct((len(arrays), *arrays[0].shape), arrays[0].dtype)
    return pl.pallas_call(
        join_kernel,
        in_specs=[VMEM] * len(arrays),
        out_specs=VMEM,
        out_shape=out,
        compiler_params=params(out, out),
        cost_estimate=cost(out.size, 4 * out.size),
    )(*arrays)


def project_kernel(masks, last, n_f, me, core, *refs):
    feats, pieces, out_ref = refs[:n_f], refs[n_f:-1], refs[-1]
    old = [ref for ref in pieces if ref.dtype == jnp.float32]
    pieces = pieces[: len(pieces) - len(old)]
    tokens = feats[0].shape[0]
    region, width = pieces[0].shape[-2:]
    weight = jnp.concatenate([ref[...].reshape(-1, width) for ref in pieces], axis=0)
    for i, f_ref in enumerate(feats):
        mine = pl.ds(i * tokens, tokens)
        part = [
            f_ref[:, pl.ds(pl.multiple_of((me[0] ^ m) * region, region), region)] for m in masks
        ]
        total = jnp.dot(
            jnp.concatenate(part, axis=1), weight, preferred_element_type=jnp.float32
        )
        if old:
            total = total + old[0][mine, :]
        if last:
            place = lax.rem(core[0] + i, n_f) * tokens
            mine = pl.ds(pl.multiple_of(place, tokens), tokens)
        out_ref[mine, :] = total.astype(out_ref.dtype)


def project(masks, me, core, feats, pieces, total, last):
    region, width = pieces[0].shape[-2:]
    whole = len(feats) * feats[0].shape[0]
    old = [] if total is None else [total]
    out = jax.ShapeDtypeStruct((whole, width), jnp.bfloat16 if last else jnp.float32)
    depth = len(masks) * region
    return pl.pallas_call(
        functools.partial(project_kernel, masks, last, len(feats)),
        in_specs=[SMEM, SMEM] + [VMEM] * (len(feats) + len(pieces) + len(old)),
        out_specs=VMEM,
        out_shape=out,
        compiler_params=params(*pieces, out, *feats, *old),
        cost_estimate=cost(2 * whole * depth * width, 2 * whole * depth + 8 * whole * width),
    )(me, core, *feats, *pieces, *old)


def spans(mask_bits):
    masks = [0]
    for b in mask_bits:
        masks = masks + [m | b for m in masks]
    return masks


def shards(features, key_grads, error_in, selected, bin_edges, threshold, moment, second, master):
    cores, owners = lax.axis_size("tensor"), lax.axis_size("dp")
    core, me = lax.axis_index("tensor"), lax.axis_index("dp")
    tokens, rows = features.shape
    width = key_grads.shape[1]
    region = rows // owners
    bins = bin_edges.shape[0] - 1
    core1 = core.reshape(1).astype(jnp.int32)
    me1 = me.reshape(1).astype(jnp.int32)

    [held] = load([features])
    n_chunks = 4 if cores == 2 else 1
    count = rows // n_chunks
    made, got = [], []
    for s in range(1, cores):
        theirs = shift(key_grads, "tensor", s)
        for j in range(n_chunks):
            made.append(part_sum(core1, held, theirs, j * count, count))
            got.append(shift(made[-1], "tensor", -s))
    mine, _ = lax.optimization_barrier((key_grads, made[-1]))
    own = part_sum(core1, held, mine, 0, rows, error_in[0])
    later, _ = lax.optimization_barrier((features, [own] + got))
    rest, outgoing = collect(selected[0, 0], bin_edges, own, got, n_chunks, owners, bins)
    error_out = rounded(rest)[None]
    feats = [held] + [shift(later, "tensor", -s) for s in range(1, cores)]

    arrived = lax.all_to_all(
        outgoing.reshape(owners, SLOTS, width), "dp", split_axis=0, concat_axis=0, tiled=True
    )
    arrived, error_out = lax.optimization_barrier((arrived, error_out))
    grad, weight = weigh(me1, threshold, bin_edges, arrived, moment, second, master)
    bits = [1 << i for i in range(owners.bit_length() - 1)]
    if 1 << len(bits) == owners and len(bits) > 2 and region % LANES == 0:
        plane, line = spans(bits[:2]), spans(bits[2:])
        plane = [plane[0], *plane[:0:-1]]
        far = [swap(weight, "dp", m) for m in line[1:]]
        near = [swap(weight, "dp", b) for b in plane[1:]]
        rest = join(far)
        groups = [[weight, rest]]
        groups += [[own, swap(rest, "dp", b)] for own, b in zip(near[:-1], plane[1:-1])]
        final, near, others = lax.optimization_barrier((rest, near, load(feats[1:])))
        groups.append([near[-1], swap(final, "dp", plane[-1])])
        feats = [held, *others]
        keys = None
        for j, b in enumerate(plane):
            masks = tuple(b ^ m for m in line)
            keys = project(masks, me1, core1, feats, groups[j], keys, j == len(plane) - 1)
    else:
        whole = jnp.concatenate(feats, axis=0)
        whole = jnp.roll(whole, core * tokens, axis=0)
        keys = jnp.dot(
            whole,
            lax.all_gather(weight, "dp", axis=0, tiled=True),
            preferred_element_type=jnp.float32,
        ).astype(jnp.bfloat16)
    moment_new, second_new, master_new = state(grad, moment, second, master)
    return (keys, error_out, moment_new, second_new, master_new)


def solution(mesh):
    in_specs = (
        P(("dp", "tensor"), None),
        P("dp", "tensor"),
        P("dp", None, "tensor"),
        P("dp", "tensor", None),
        P(),
        P(),
        P("dp", "tensor"),
        P("dp", "tensor"),
        P("dp", "tensor"),
    )
    out_specs = (
        P("dp", "tensor"),
        P("dp", None, "tensor"),
        P("dp", "tensor"),
        P("dp", "tensor"),
        P("dp", "tensor"),
    )
    return jax.shard_map(shards, mesh=mesh, in_specs=in_specs, out_specs=out_specs, check_vma=False)
```
